32 devices in a mesh: page: 4 (over z), blk: 8 (over y, x, core).
Axes of the slice: x: 2, y: 2, z: 4, core: 2. Of those that a mesh axis runs over, the one named last changes fastest.
Arguments:
- tokens: bfloat16 [8, 4096, 1024], P('page', 'blk'), may hold values from -6 to 6
- memory: bfloat16 [8, 588, 1024], P('page', None, 'blk'), may hold values from -6 to 6
- end_only: int32 [8], P('page'), may hold values from 0 to 1, as said below
- lengths: int32 [8], P('page'), may hold values from 1 to 4096, as said below
- norm_gain: float32 [3, 1024], replicated, may hold values from 0.5 to 1.5
- norm_bias: float32 [3, 1024], replicated, may hold values from -3 to 3
- self_qkv: bfloat16 [1024, 3072], replicated, may hold values from -0.1875 to 0.1875
- self_out: bfloat16 [1024, 1024], replicated, may hold values from -1.5 to 1.5
- cross_q: bfloat16 [1024, 1024], replicated, may hold values from -0.1875 to 0.1875
- cross_kv: bfloat16 [1024, 2048], replicated, may hold values from -0.1875 to 0.1875
- cross_out: bfloat16 [1024, 1024], replicated, may hold values from -1.5 to 1.5
- fc_in: bfloat16 [1024, 4096], replicated, may hold values from -0.1875 to 0.1875
- fc_out: bfloat16 [4096, 1024], replicated, may hold values from -0.09375 to 0.09375
- fc_in_bias: float32 [4096], replicated, may hold values from -3 to 3
- proj_bias: float32 [7, 1024], replicated, may hold values from -3 to 3
- cotangent: bfloat16 [8, 4096, 1024], P('page', 'blk'), may hold values from -6 to 6
Outputs:
- out: bfloat16 [8, 4096, 1024], P('page', 'blk')
- grad_tokens: float32 [8, 4096, 1024], P('page', 'blk')
- grad_memory: float32 [8, 588, 1024], P('page', None, 'blk')
- grad_norm_gain: float32 [3, 1024], P(None, 'blk')
- grad_norm_bias: float32 [3, 1024], P(None, 'blk')
- grad_self_qkv: float32 [1024, 3072], P('blk')
- grad_self_out: float32 [1024, 1024], P('blk')
- grad_cross_q: float32 [1024, 1024], P('blk')
- grad_cross_kv: float32 [1024, 2048], P('blk')
- grad_cross_out: float32 [1024, 1024], P('blk')
- grad_fc_in: float32 [1024, 4096], P('blk')
- grad_fc_out: float32 [4096, 1024], P('blk')
- grad_fc_in_bias: float32 [4096], P('blk')
- grad_proj_bias: float32 [7, 1024], P(None, 'blk')
The draws below stay inside these ranges and needn't reach their ends.
Inputs may be any that keep to these rules, and one draw needn't show every extreme that they name: `lengths`: in each group of 2 consecutive sequences one has length 4096 and end_only 0. At least one sequence of the whole batch has end_only 1.
All inputs are finite; a program needn't handle non-finite values.
Results may differ from the reference program's by a relative error of at most 0.02.
Values may be sent and summed in bfloat16 or wider, within the bound.
No kernel may reach another device: no remote copies, remote signals or barrier semaphores. Data moves between devices by JAX's collectives and lax.ppermute only.
A program may use at most 576 MiB of HBM per device.

```python
import jax
import jax.numpy as jnp
from jax import lax

D = 1024
HEADS = 16
FF = 4096
MEM = 588
SEQS = 2
LEN = 4096
SEQ_ALL = 8


def page_spans(key):
    groups = SEQ_ALL // SEQS
    raw_lengths = jax.random.randint(jax.random.fold_in(key, 11), (SEQ_ALL,), 1, LEN + 1)
    raw_flags = (jax.random.randint(jax.random.fold_in(key, 12), (SEQ_ALL,), 0, 4) == 0).astype(jnp.int32)
    chosen = jax.random.randint(jax.random.fold_in(key, 13), (groups, 1), 0, SEQS)
    offsets = jax.random.randint(jax.random.fold_in(key, 14), (groups, 1), 1, SEQS)
    marked_group = jax.random.randint(jax.random.fold_in(key, 15), (), 0, groups)
    slots = jnp.arange(SEQS, dtype=jnp.int32)[None, :]
    group_ids = jnp.arange(groups, dtype=jnp.int32)[:, None]
    full_seq = (slots == chosen).reshape(SEQ_ALL)
    flagged = ((slots == (chosen + offsets) % SEQS) & (group_ids == marked_group)).reshape(SEQ_ALL)
    lengths = jnp.where(full_seq, LEN, raw_lengths).astype(jnp.int32)
    flags = jnp.where(full_seq, 0, jnp.where(flagged, 1, raw_flags)).astype(jnp.int32)
    return (lengths, flags)


def draw_lengths(key, part):
    return page_spans(key)[0]


def draw_end_only(key, part):
    return page_spans(key)[1]


def block_levels(stream_key, shape, split, smallest, top_value):
    factor_of = 1.0
    for dim, shards_of in split:
        draws = jax.random.uniform(jax.random.fold_in(jax.random.fold_in(stream_key, 6), dim), (shards_of,), jnp.float32, smallest / len(split), top_value / len(split))
        factor_of = factor_of * jnp.repeat(jnp.exp(draws), shape[dim] // shards_of).reshape((-1,) + (1,) * (len(shape) - 1 - dim))
    return factor_of


def scatter_about(stream_key, dims, scale, reach, split=(), kind=jnp.bfloat16):
    factor_of = block_levels(stream_key, dims, split, -0.22, 0.18) if split else 1.0
    array = jax.random.normal(stream_key, dims, jnp.float32) * scale * factor_of
    return jnp.minimum(jnp.maximum(array, -reach), reach).astype(kind)


def setup_inputs(seed: int = 0) -> dict:
    seeds = jax.random.split(jax.random.key(seed), 17)
    return {
        "tokens": scatter_about(seeds[0], (SEQ_ALL, LEN, D), 1.0, 6.0, ((0, 4), (1, 8))),
        "memory": scatter_about(seeds[1], (SEQ_ALL, MEM, D), 1.0, 6.0, ((0, 4), (2, 8))),
        "end_only": draw_end_only(jax.random.fold_in(seeds[16], 71), 0),
        "lengths": draw_lengths(jax.random.fold_in(seeds[16], 71), 0),
        "norm_gain": jnp.clip(1.0 + 0.1 * jax.random.normal(seeds[4], (3, D), jnp.float32), 0.5, 1.5),
        "norm_bias": scatter_about(seeds[5], (3, D), 0.5, 3.0, (), jnp.float32),
        "self_qkv": scatter_about(seeds[6], (D, 3 * D), D ** -0.5, 0.1875),
        "self_out": scatter_about(seeds[7], (D, D), (max(D // 64, 1)) ** -0.5, 1.5),
        "cross_q": scatter_about(seeds[8], (D, D), D ** -0.5, 0.1875),
        "cross_kv": scatter_about(seeds[9], (D, 2 * D), D ** -0.5, 0.1875),
        "cross_out": scatter_about(seeds[10], (D, D), (max(D // 64, 1)) ** -0.5, 1.5),
        "fc_in": scatter_about(seeds[11], (D, FF), D ** -0.5, 0.1875),
        "fc_out": scatter_about(seeds[12], (FF, D), FF ** -0.5, 0.09375),
        "fc_in_bias": scatter_about(seeds[13], (FF,), 0.5, 3.0, (), jnp.float32),
        "proj_bias": scatter_about(seeds[14], (7, D), 0.5, 3.0, (), jnp.float32),
        "cotangent": scatter_about(seeds[15], (SEQ_ALL, LEN, D), 1.0, 6.0, ((0, 4), (1, 8))),
    }


EPSILON = 1e-05
NEG_LARGE = -1e+30
HIGHEST = lax.Precision.HIGHEST

@jax.custom_vjp
def low(v):
    return lax.optimization_barrier(v.astype(jnp.bfloat16)).astype(jnp.float32)

@jax.custom_vjp
def low_back(v):
    return v

def low_keep(v):
    return (low(v), None)

def low_pass(kept, grad):
    return (grad,)

def back_keep(v):
    return (v, None)

def back_low(kept, grad):
    return (low(grad),)
low.defvjp(low_keep, low_pass)
low_back.defvjp(back_keep, back_low)

def precise(left_op, right_op):
    return jnp.dot(left_op, right_op, precision=HIGHEST, preferred_element_type=jnp.float32)

def layer_norm(vector, gain_vec, shift_vec):
    centre = vector - lax.optimization_barrier(jnp.mean(vector, axis=-1, keepdims=True))
    spread = lax.optimization_barrier(jnp.mean(centre * centre, axis=-1, keepdims=True))
    return centre * lax.rsqrt(spread + EPSILON) * gain_vec + shift_vec

def to_heads(tensor):
    return tensor.reshape(tensor.shape[0], HEADS, tensor.shape[1] // HEADS).transpose(1, 0, 2)

def attend(queries, key_rows, values, allowed):

    def single_head(inputs):
        head_q, head_k, head_v = inputs
        scores = low_back(precise(head_q, head_k.T) * 0.125)
        scores = jnp.where(allowed, scores, NEG_LARGE)
        row_max = lax.optimization_barrier(jnp.max(scores, axis=-1, keepdims=True))
        exp_scores = jnp.exp(scores - row_max)
        attn_probs = exp_scores / lax.optimization_barrier(jnp.sum(exp_scores, axis=-1, keepdims=True))
        return precise(low(attn_probs), head_v)
    stacked = lax.map(jax.checkpoint(single_head), (to_heads(queries), to_heads(key_rows), to_heads(values)))
    return stacked.transpose(1, 0, 2).reshape(queries.shape[0], queries.shape[1])

def sequence(stream_in, mem_rows, row_valid, params):
    norm_gain, norm_bias, self_qkv, self_out, cross_q, cross_kv, cross_out, fc_in, fc_out, fc_in_bias, proj_bias = params
    model_width = stream_in.shape[1]
    length = stream_in.shape[0]
    causal = jnp.arange(length, dtype=jnp.int32)[None, :] <= jnp.arange(length, dtype=jnp.int32)[:, None]
    everywhere = jnp.ones((length, mem_rows.shape[0]), dtype=jnp.bool_)
    normed_self = low(layer_norm(stream_in, norm_gain[0], norm_bias[0]))
    projected = precise(normed_self, self_qkv)
    queries = low(low_back(projected[:, :model_width] + proj_bias[0]))
    key_rows = low(low_back(projected[:, model_width:2 * model_width]))
    values = low(low_back(projected[:, 2 * model_width:] + proj_bias[1]))
    attended = low(low_back(attend(queries, key_rows, values, causal)))
    stream_mid = stream_in + low_back(precise(attended, self_out) + proj_bias[2])
    normed_cross = low(layer_norm(stream_mid, norm_gain[1], norm_bias[1]))
    cross_queries = low(low_back(precise(normed_cross, cross_q) + proj_bias[3]))
    mem_proj = precise(mem_rows, cross_kv)
    cross_keys = low(low_back(mem_proj[:, :model_width]))
    cross_values = low(low_back(mem_proj[:, model_width:] + proj_bias[4]))
    crossed = low(low_back(attend(cross_queries, cross_keys, cross_values, everywhere)))
    stream_late = stream_mid + low_back(precise(crossed, cross_out) + proj_bias[5])
    normed_mlp = low(layer_norm(stream_late, norm_gain[2], norm_bias[2]))
    hidden_pre = low_back(precise(normed_mlp, fc_in) + fc_in_bias)
    hidden_act = low(jax.nn.gelu(hidden_pre, approximate=False))
    stream_out = stream_late + low_back(precise(hidden_act, fc_out) + proj_bias[6])
    return stream_out * row_valid[:, None]

def reference(tokens, memory, end_only, lengths, norm_gain, norm_bias, self_qkv, self_out, cross_q, cross_kv, cross_out, fc_in, fc_out, fc_in_bias, proj_bias, cotangent):
    weights = tuple((weight.astype(jnp.float32) for weight in (norm_gain, norm_bias, self_qkv, self_out, cross_q, cross_kv, cross_out, fc_in, fc_out, fc_in_bias, proj_bias)))
    live_span = jnp.where(end_only == 1, 1, lengths).astype(jnp.int32)
    row_valid = (jnp.arange(LEN, dtype=jnp.int32)[None, :] < live_span[:, None]).astype(jnp.float32)

    def forward(tok_in, mem_in, *params):

        def single(inputs):
            return sequence(inputs[0], inputs[1], inputs[2], params)
        return lax.map(jax.checkpoint(single), (tok_in, mem_in, row_valid))
    result, pullback = jax.vjp(forward, tokens.astype(jnp.float32), memory.astype(jnp.float32), *weights)
    gradients = pullback(cotangent.astype(jnp.float32))
    return (result.astype(jnp.bfloat16), gradients[0], gradients[1], gradients[2], gradients[3], gradients[4], gradients[5], gradients[6], gradients[7], gradients[8], gradients[9], gradients[10], gradients[11], gradients[12])
```

```python
from functools import partial

import jax
import jax.numpy as jnp
from jax import lax
from jax.experimental import pallas as pl
from jax.experimental.pallas import tpu as pltpu
from jax.sharding import PartitionSpec as P

HEADS = 16
EPSILON = 1e-05
NEG_LARGE = -1e30
HALF = jnp.bfloat16
F32 = jnp.float32
LOG2E = 1.4426950408889634
LN2 = 0.6931471805599453
NT = (((1,), (1,)), ((), ()))
NN = (((1,), (0,)), ((), ()))
TN = (((0,), (0,)), ((), ()))
VMEM_LIMIT = 56 * 2**20


def mxu(left_op, right_op, dims=NN):
    return lax.dot_general(left_op, right_op, dims, preferred_element_type=F32)


def head_lanes(width, head, head_dim):
    lane = lax.broadcasted_iota(jnp.int32, (1, width), 1)
    return (lane >= head * head_dim) & (lane < (head + 1) * head_dim)


def one_head(tensor, head, n_heads, head_dim):
    if n_heads == 1:
        return tensor
    return jnp.where(
        head_lanes(tensor.shape[-1], head, head_dim), tensor, jnp.zeros_like(tensor)
    )


def causal(scores, key_start, query_start):
    key_pos = key_start + lax.broadcasted_iota(jnp.int32, scores.shape, 0)
    query_pos = query_start + lax.broadcasted_iota(jnp.int32, scores.shape, 1)
    return jnp.where(key_pos <= query_pos, scores, NEG_LARGE)


def load_pieces(scalars, pieces, whole, sem):
    rows = pieces[0].shape[0]
    me = scalars[1]
    copies = []
    for step, piece in enumerate(pieces):
        start = pl.multiple_of(lax.bitwise_xor(me, step) * rows, rows)
        copies.append(pltpu.make_async_copy(piece, whole.at[pl.ds(start, rows)], sem.at[step]))
    for copy in copies:
        copy.start()
    return copies


def store_pieces(scalars, pieces, whole, sem):
    rows = pieces[0].shape[0]
    me = scalars[1]
    copies = []
    for step, piece in enumerate(pieces):
        start = pl.multiple_of(lax.bitwise_xor(me, step) * rows, rows)
        copies.append(pltpu.make_async_copy(whole.at[pl.ds(start, rows)], piece, sem.at[step]))
    for copy in copies:
        copy.start()
    for copy in copies:
        copy.wait()


def self_forward_kernel(scalars, *refs, n, n_heads, head_dim, q_block, k_block, stat_block):
    pieces, refs = refs[:n], refs[n:]
    out_pieces, refs = refs[:n], refs[n:]
    kept_out, log_sums, whole, values_t, sem = refs
    width = n_heads * head_dim
    index = pl.program_id(0)
    k_blocks = values_t.shape[0]

    @pl.when(index == 0)
    def _():
        for copy in load_pieces(scalars, pieces, whole, sem):
            copy.wait()
        for b in range(k_blocks):
            values_t[b] = whole[b * k_block : (b + 1) * k_block, 2 * width :].T

    start = pl.multiple_of(index * q_block, q_block)
    q_rows = pl.ds(start, q_block)
    live = start < scalars[0]

    @pl.when(jnp.logical_not(live))
    def _():
        kept_out[q_rows, :] = jnp.zeros((q_block, width), HALF)
        log_sums[...] = jnp.zeros_like(log_sums)

    @pl.when(live)
    def _():
        query = whole[q_rows, :width]
        queries = [one_head(query, h, n_heads, head_dim) for h in range(n_heads)]

        def step(kb, carry, masked):
            keys = whole[pl.ds(pl.multiple_of(kb * k_block, k_block), k_block), width : 2 * width]
            value_t = values_t[kb]
            out = []
            for h in range(n_heads):
                top, total, acc = carry[h]
                scores = mxu(keys, queries[h], NT)
                if masked:
                    scores = causal(scores, kb * k_block, start)
                new_top = jnp.maximum(top, jnp.max(scores, axis=0, keepdims=True))
                probs = jnp.exp2(scores - new_top)
                scale = jnp.exp2(top - new_top)
                total = total * scale + jnp.sum(probs, axis=0, keepdims=True)
                part = mxu(value_t[h * head_dim : (h + 1) * head_dim], probs.astype(HALF))
                out.append((new_top, total, acc * scale + part))
            return tuple(out)

        carry = tuple(
            (
                jnp.full((1, q_block), NEG_LARGE, F32),
                jnp.zeros((1, q_block), F32),
                jnp.zeros((head_dim, q_block), F32),
            )
            for _ in range(n_heads)
        )
        ratio = q_block // k_block
        carry = lax.fori_loop(0, index * ratio, lambda kb, c: step(kb, c, False), carry)
        for t in range(ratio):
            carry = step(index * ratio + t, carry, True)
        result_t = jnp.concatenate([acc / total for _, total, acc in carry], axis=0)
        kept_out[q_rows, :] = result_t.T.astype(HALF)
        for h, (top, total, _) in enumerate(carry):
            log_sum = top + jnp.log2(total)
            for t in range(q_block // stat_block):
                log_sums[t, h : h + 1, :] = log_sum[:, t * stat_block : (t + 1) * stat_block]

    @pl.when(index == pl.num_programs(0) - 1)
    def _():
        store_pieces(scalars, out_pieces, kept_out, sem)


def self_forward(scalars, pieces, n_heads, head_dim):
    n, rows = len(pieces), pieces[0].shape[0]
    length, width = n * rows, n_heads * head_dim
    q_block, k_block, stat_block = 1024, 512, 512
    any_spec = pl.BlockSpec(memory_space=pl.ANY)
    result = pl.pallas_call(
        partial(
            self_forward_kernel,
            n=n,
            n_heads=n_heads,
            head_dim=head_dim,
            q_block=q_block,
            k_block=k_block,
            stat_block=stat_block,
        ),
        grid_spec=pltpu.PrefetchScalarGridSpec(
            num_scalar_prefetch=1,
            grid=(length // q_block,),
            in_specs=[any_spec] * n,
            out_specs=[any_spec] * n
            + [
                pl.BlockSpec((length, width), lambda i, s: (0, 0)),
                pl.BlockSpec((q_block // stat_block, n_heads, stat_block), lambda i, s: (i, 0, 0)),
            ],
            scratch_shapes=[
                pltpu.VMEM((length, 3 * width), HALF),
                pltpu.VMEM((length // k_block, width, k_block), HALF),
                pltpu.SemaphoreType.DMA((n,)),
            ],
        ),
        out_shape=[jax.ShapeDtypeStruct((rows, width), HALF)] * n
        + [
            jax.ShapeDtypeStruct((length, width), HALF),
            jax.ShapeDtypeStruct((length // stat_block, n_heads, stat_block), F32),
        ],
        compiler_params=pltpu.CompilerParams(vmem_limit_bytes=VMEM_LIMIT),
        cost_estimate=pl.CostEstimate(
            flops=2 * 2 * length * length * width,
            bytes_accessed=length * width * 10,
            transcendentals=n_heads * length * length // 2,
        ),
        name="self_forward",
    )(scalars, *pieces)
    return result[:n], result[n], result[n + 1]


def self_backward_kernel(scalars, *refs, n, n_heads, head_dim, block):
    pieces, refs = refs[:n], refs[n:]
    grad_pieces, refs = refs[:n], refs[n:]
    kept_out, log_sums, refs = refs[0], refs[1], refs[2:]
    out_pieces, refs = refs[:n], refs[n:]
    whole, grads, query_heads, grad_heads, deltas, query_sums, result, sem, grad_sem = refs
    width = n_heads * head_dim
    index = pl.program_id(0)
    blocks = query_heads.shape[1]
    span = scalars[0]

    @pl.when(index == 0)
    def _():
        copies = load_pieces(scalars, pieces, whole, sem)
        copies += load_pieces(scalars, grad_pieces, grads, grad_sem)
        query_sums[...] = jnp.zeros_like(query_sums)
        for copy in copies:
            copy.wait()
        for b in range(blocks):
            rows = slice(b * block, (b + 1) * block)
            query, grad = whole[rows, :width], grads[rows, :]
            products = (grad.astype(F32) * kept_out[rows, :].astype(F32)).T
            for h in range(n_heads):
                deltas[b, h : h + 1, :] = jnp.sum(
                    products[h * head_dim : (h + 1) * head_dim], axis=0, keepdims=True
                )
                query_heads[h, b] = one_head(query, h, n_heads, head_dim)
                grad_heads[h, b] = one_head(grad, h, n_heads, head_dim)

    start = pl.multiple_of(index * block, block)
    k_rows = pl.ds(start, block)
    live = start < span

    @pl.when(jnp.logical_not(live))
    def _():
        result[k_rows, width:] = jnp.zeros((block, 2 * width), HALF)

    @pl.when(live)
    def _():
        keys = whole[k_rows, width : 2 * width]
        values = whole[k_rows, 2 * width :]
        keys_t = keys.T

        def step(qb, carry, masked):
            grad_keys, grad_values = carry
            for h in range(n_heads):
                query, grad = query_heads[h, qb], grad_heads[h, qb]
                scores = mxu(keys, query, NT)
                if masked:
                    scores = causal(scores, start, qb * block)
                probs = jnp.exp2(scores - log_sums[qb, h : h + 1, :])
                grad_probs = mxu(values, grad, NT)
                grad_scores = (probs * (grad_probs - deltas[qb, h : h + 1, :])).astype(HALF)
                grad_values = grad_values + mxu(probs.astype(HALF), grad)
                grad_keys = grad_keys + mxu(grad_scores, query)
                lanes = slice(h * head_dim, (h + 1) * head_dim)
                query_sums[qb, lanes, :] += mxu(keys_t[lanes], grad_scores)
            return grad_keys, grad_values

        zero = jnp.zeros((block, width), F32)
        carry = step(index, (zero, zero), True)
        live_blocks = (span + block - 1) // block
        grad_keys, grad_values = lax.fori_loop(
            index + 1, live_blocks, lambda qb, c: step(qb, c, False), carry
        )
        result[k_rows, width : 2 * width] = (grad_keys * LN2).astype(HALF)
        result[k_rows, 2 * width :] = grad_values.astype(HALF)

    @pl.when(index == pl.num_programs(0) - 1)
    def _():
        for b in range(blocks):
            result[b * block : (b + 1) * block, :width] = (query_sums[b] * 0.125).T.astype(HALF)
        store_pieces(scalars, out_pieces, result, sem)


def self_backward(scalars, pieces, grad_pieces, kept_out, log_sums, n_heads, head_dim):
    n, rows = len(pieces), pieces[0].shape[0]
    length, width = n * rows, n_heads * head_dim
    block = log_sums.shape[2]
    blocks = length // block
    any_spec = pl.BlockSpec(memory_space=pl.ANY)
    return pl.pallas_call(
        partial(self_backward_kernel, n=n, n_heads=n_heads, head_dim=head_dim, block=block),
        grid_spec=pltpu.PrefetchScalarGridSpec(
            num_scalar_prefetch=1,
            grid=(blocks,),
            in_specs=[any_spec] * (2 * n)
            + [
                pl.BlockSpec((length, width), lambda i, s: (0, 0)),
                pl.BlockSpec((blocks, n_heads, block), lambda i, s: (0, 0, 0)),
            ],
            out_specs=[any_spec] * n,
            scratch_shapes=[
                pltpu.VMEM((length, 3 * width), HALF),
                pltpu.VMEM((length, width), HALF),
                pltpu.VMEM((n_heads, blocks, block, width), HALF),
                pltpu.VMEM((n_heads, blocks, block, width), HALF),
                pltpu.VMEM((blocks, n_heads, block), F32),
                pltpu.VMEM((blocks, width, block), F32),
                pltpu.VMEM((length, 3 * width), HALF),
                pltpu.SemaphoreType.DMA((n,)),
                pltpu.SemaphoreType.DMA((n,)),
            ],
        ),
        out_shape=[jax.ShapeDtypeStruct((rows, 3 * width), HALF)] * n,
        compiler_params=pltpu.CompilerParams(vmem_limit_bytes=VMEM_LIMIT),
        cost_estimate=pl.CostEstimate(
            flops=5 * 2 * length * length * width // 2,
            bytes_accessed=length * width * 20,
            transcendentals=n_heads * length * length // 2,
        ),
        name="self_backward",
    )(scalars, *pieces, *grad_pieces, kept_out, log_sums)


def cross_scores(keys, query, mem_count):
    scores = mxu(keys, query, NT)
    padded = scores.shape[0]
    if padded == mem_count:
        return scores
    whole = mem_count // 8 * 8
    tail = scores[whole:]
    position = whole + lax.broadcasted_iota(jnp.int32, tail.shape, 0)
    tail = jnp.where(position < mem_count, tail, NEG_LARGE)
    return jnp.concatenate([scores[:whole], tail], axis=0)


def cross_forward_kernel(scalars, query_ref, key_ref, value_ref, out_ref, log_sums, *, mem_count, head_dim):
    rows, width = query_ref.shape
    live = scalars[1] * rows < scalars[0]

    @pl.when(jnp.logical_not(live))
    def _():
        out_ref[...] = jnp.zeros_like(out_ref)
        log_sums[...] = jnp.zeros_like(log_sums)

    @pl.when(live)
    def _():
        n_heads = width // head_dim
        query, keys = query_ref[...], key_ref[...]
        values_t = value_ref[...].T
        results = []
        for h in range(n_heads):
            scores = cross_scores(keys, one_head(query, h, n_heads, head_dim), mem_count)
            top = jnp.max(scores, axis=0, keepdims=True)
            probs = jnp.exp2(scores - top)
            total = jnp.sum(probs, axis=0, keepdims=True)
            lanes = slice(h * head_dim, (h + 1) * head_dim)
            results.append(mxu(values_t[lanes], probs.astype(HALF)) / total)
            log_sums[0, h : h + 1, :] = top + jnp.log2(total)
        out_ref[...] = jnp.concatenate(results, axis=0).T.astype(HALF)


def cross_forward(scalars, query, keys, values, mem_count, head_dim):
    rows, model_width = query.shape
    padded = keys.shape[0]
    width = 128
    groups, n_heads = model_width // width, width // head_dim
    column = lambda count: pl.BlockSpec((count, width), lambda g, s: (0, g))
    return pl.pallas_call(
        partial(cross_forward_kernel, mem_count=mem_count, head_dim=head_dim),
        grid_spec=pltpu.PrefetchScalarGridSpec(
            num_scalar_prefetch=1,
            grid=(groups,),
            in_specs=[column(rows), column(padded), column(padded)],
            out_specs=[column(rows), pl.BlockSpec((1, n_heads, rows), lambda g, s: (g, 0, 0))],
        ),
        out_shape=[
            jax.ShapeDtypeStruct((rows, model_width), HALF),
            jax.ShapeDtypeStruct((groups, n_heads, rows), F32),
        ],
        compiler_params=pltpu.CompilerParams(vmem_limit_bytes=VMEM_LIMIT),
        cost_estimate=pl.CostEstimate(
            flops=4 * 2 * rows * padded * model_width,
            bytes_accessed=(rows + padded) * model_width * 4,
            transcendentals=rows * padded * model_width // head_dim,
        ),
        name="cross_forward",
    )(scalars, query, keys, values)


def cross_backward_kernel(
    scalars,
    query_ref,
    key_ref,
    value_ref,
    grad_ref,
    out_ref,
    log_sums,
    grad_query,
    grad_key,
    grad_value,
    *,
    mem_count,
    head_dim,
):
    rows, width = query_ref.shape
    padded = key_ref.shape[0]
    live = scalars[1] * rows < scalars[0]

    @pl.when(jnp.logical_not(live))
    def _():
        grad_query[...] = jnp.zeros_like(grad_query)
        grad_key[...] = jnp.zeros_like(grad_key)
        grad_value[...] = jnp.zeros_like(grad_value)

    @pl.when(live)
    def _():
        n_heads = width // head_dim
        query_all, keys, values, grad_all = query_ref[...], key_ref[...], value_ref[...], grad_ref[...]
        keys_t = keys.T
        products = (grad_all.astype(F32) * out_ref[...].astype(F32)).T
        query_parts = []
        key_sum = jnp.zeros((padded, width), F32)
        value_sum = jnp.zeros((padded, width), F32)
        for h in range(n_heads):
            lanes = slice(h * head_dim, (h + 1) * head_dim)
            query = one_head(query_all, h, n_heads, head_dim)
            grad = one_head(grad_all, h, n_heads, head_dim)
            delta = jnp.sum(products[lanes], axis=0, keepdims=True)
            scores = cross_scores(keys, query, mem_count)
            probs = jnp.exp2(scores - log_sums[0, h : h + 1, :])
            grad_probs = mxu(values, grad, NT)
            grad_scores = (probs * (grad_probs - delta)).astype(HALF)
            value_sum = value_sum + mxu(probs.astype(HALF), grad)
            key_sum = key_sum + mxu(grad_scores, query)
            query_parts.append(mxu(keys_t[lanes], grad_scores))
        grad_query[...] = (jnp.concatenate(query_parts, axis=0) * 0.125).T.astype(HALF)
        grad_key[...] = (key_sum * LN2).astype(HALF)
        grad_value[...] = value_sum.astype(HALF)


def cross_backward(scalars, query, keys, values, grad, kept_out, log_sums, mem_count, head_dim):
    rows, model_width = query.shape
    padded = keys.shape[0]
    width = 128
    groups, n_heads = model_width // width, width // head_dim
    column = lambda count: pl.BlockSpec((count, width), lambda g, s: (0, g))
    return pl.pallas_call(
        partial(cross_backward_kernel, mem_count=mem_count, head_dim=head_dim),
        grid_spec=pltpu.PrefetchScalarGridSpec(
            num_scalar_prefetch=1,
            grid=(groups,),
            in_specs=[
                column(rows),
                column(padded),
                column(padded),
                column(rows),
                column(rows),
                pl.BlockSpec((1, n_heads, rows), lambda g, s: (g, 0, 0)),
            ],
            out_specs=[column(rows), column(padded), column(padded)],
        ),
        out_shape=[
            jax.ShapeDtypeStruct((rows, model_width), HALF),
            jax.ShapeDtypeStruct((padded, model_width), HALF),
            jax.ShapeDtypeStruct((padded, model_width), HALF),
        ],
        compiler_params=pltpu.CompilerParams(vmem_limit_bytes=VMEM_LIMIT),
        cost_estimate=pl.CostEstimate(
            flops=10 * 2 * rows * padded * model_width,
            bytes_accessed=(rows + padded) * model_width * 10,
            transcendentals=rows * padded * model_width // head_dim,
        ),
        name="cross_backward",
    )(scalars, query, keys, values, grad, kept_out, log_sums)


def exchange(columns, n, me):
    width = columns.shape[1] // n
    pieces = []
    for step in range(n):
        piece = lax.dynamic_slice_in_dim(columns, lax.bitwise_xor(me, step) * width, width, 1)
        pieces.append(swap(piece, step, n))
    return pieces


def swap(piece, step, n):
    if step == 0:
        return piece
    return lax.ppermute(piece, "blk", [(k, k ^ step) for k in range(n)])


def gather_columns(pieces, n, me):
    rows, width = pieces[0].shape
    whole = jnp.zeros((rows, n * width), pieces[0].dtype)
    for step, piece in enumerate(pieces):
        received = swap(piece, step, n)
        whole = lax.dynamic_update_slice_in_dim(
            whole, received, lax.bitwise_xor(me, step) * width, 1
        )
    return whole


def normalized(vector):
    centre = vector - jnp.mean(vector, axis=-1, keepdims=True)
    spread = jnp.mean(centre * centre, axis=-1, keepdims=True)
    inverse = lax.rsqrt(spread + EPSILON)
    return centre * inverse, inverse


def norm_backward(unit, inverse, gain, grad):
    scaled = grad * gain
    first = jnp.mean(scaled, axis=-1, keepdims=True)
    second = jnp.mean(scaled * unit, axis=-1, keepdims=True)
    grad_in = inverse * (scaled - first - unit * second)
    return grad_in, jnp.sum(grad * unit, axis=0), jnp.sum(grad, axis=0)


def col_sums(tensor):
    return jnp.sum(tensor.astype(F32), axis=0)


def shards(
    tokens,
    memory,
    end_only,
    lengths,
    norm_gain,
    norm_bias,
    self_qkv,
    self_out,
    cross_q,
    cross_kv,
    cross_out,
    fc_in,
    fc_out,
    fc_in_bias,
    proj_bias,
    cotangent,
    *,
    n,
):
    seqs, rows, model_width = tokens.shape
    mem_count, shard_width = memory.shape[1], memory.shape[2]
    head_dim = model_width // HEADS
    n_heads = HEADS // n
    width = n_heads * head_dim
    flat = seqs * rows
    me = lax.axis_index("blk")
    offset = me * rows
    span = jnp.where(end_only == 1, 1, lengths)
    scalars = [jnp.stack([span[s], me]).astype(jnp.int32) for s in range(seqs)]
    positions = offset + jnp.arange(rows, dtype=jnp.int32)
    row_mask = (positions[None, :] < span[:, None]).astype(F32).reshape(flat, 1)
    q_scale = 0.125 * LOG2E

    qkv_weights = (
        self_qkv.reshape(model_width, 3, n, width).transpose(0, 2, 1, 3).reshape(model_width, -1)
    )
    zeros = jnp.zeros((model_width,), F32)
    qkv_bias = jnp.stack([proj_bias[0], zeros, proj_bias[1]])
    qkv_bias = qkv_bias.reshape(3, n, width).transpose(1, 0, 2).reshape(-1)
    qkv_scale = jnp.broadcast_to(jnp.array([q_scale, 1.0, 1.0], F32)[None, :, None], (n, 3, width))
    qkv_scale = qkv_scale.reshape(-1)

    stream_in = tokens.astype(F32).reshape(flat, model_width)
    unit_self, inverse_self = normalized(stream_in)
    normed_self = (unit_self * norm_gain[0] + norm_bias[0]).astype(HALF)
    kept = []
    for s in range(seqs):
        projected = mxu(normed_self[s * rows : (s + 1) * rows], qkv_weights)
        projected = ((projected + qkv_bias) * qkv_scale).astype(HALF)
        kept.append(exchange(projected, n, me))

    whole_memory = lax.all_gather(memory, "blk", axis=2, tiled=True)
    padded = -(-mem_count // 16) * 16
    whole_memory = jnp.pad(whole_memory, ((0, 0), (0, padded - mem_count), (0, 0)))
    mem_proj = mxu(whole_memory.reshape(seqs * padded, model_width), cross_kv)
    cross_keys = mem_proj[:, :model_width].astype(HALF).reshape(seqs, padded, model_width)
    cross_values = (mem_proj[:, model_width:] + proj_bias[4]).astype(HALF)
    cross_values = cross_values.reshape(seqs, padded, model_width)

    self_saved, attended = [], []
    for s in range(seqs):
        out_pieces, kept_out, log_sums = self_forward(scalars[s], kept[s], n_heads, head_dim)
        self_saved.append((kept_out, log_sums))
        attended.append(gather_columns(out_pieces, n, me))

    mids, crosses, cross_saved = [], [], []
    for s in range(seqs):
        mid = stream_in[s * rows : (s + 1) * rows] + mxu(attended[s], self_out) + proj_bias[2]
        unit, _ = normalized(mid)
        normed = (unit * norm_gain[1] + norm_bias[1]).astype(HALF)
        query = ((mxu(normed, cross_q) + proj_bias[3]) * q_scale).astype(HALF)
        crossed, log_sums = cross_forward(
            scalars[s], query, cross_keys[s], cross_values[s], mem_count, head_dim
        )
        mids.append(mid)
        crosses.append(crossed)
        cross_saved.append((query, log_sums))
    attended = jnp.concatenate(attended, axis=0)
    crossed = jnp.concatenate(crosses, axis=0)
    stream_mid = jnp.concatenate(mids, axis=0)

    stream_late = stream_mid + mxu(crossed, cross_out) + proj_bias[5]
    unit_mlp, inverse_mlp = normalized(stream_late)
    normed_mlp = (unit_mlp * norm_gain[2] + norm_bias[2]).astype(HALF)
    hidden_pre = mxu(normed_mlp, fc_in) + fc_in_bias
    gate = 0.5 * (1.0 + lax.erf(hidden_pre * (0.5**0.5)))
    hidden_act = (hidden_pre * gate).astype(HALF)
    slope = (gate + hidden_pre * (jnp.exp(-0.5 * hidden_pre * hidden_pre) * 0.3989422804014327)).astype(HALF)
    stream_out = stream_late + mxu(hidden_act, fc_out) + proj_bias[6]
    result = (stream_out * row_mask).reshape(seqs, rows, model_width).astype(HALF)

    grad_late = cotangent.astype(F32).reshape(flat, model_width) * row_mask
    grad_mlp = grad_late.astype(HALF)
    grad_fc_out = mxu(hidden_act, grad_mlp, TN)
    grad_pre = (slope.astype(F32) * mxu(grad_mlp, fc_out, NT)).astype(HALF)
    grad_fc_in = mxu(normed_mlp, grad_pre, TN)
    grad_fc_bias = col_sums(grad_pre)
    grad_x2, gain_two, shift_two = norm_backward(
        unit_mlp, inverse_mlp, norm_gain[2], mxu(grad_pre, fc_in, NT)
    )
    grad_two = grad_late + grad_x2
    grad_cross = grad_two.astype(HALF)
    grad_cross_out = mxu(crossed, grad_cross, TN)

    cq_grads, ckv_parts, ones, selfs, dq_pieces = [], [], [], [], []
    gain_one, shift_one = 0.0, 0.0
    normed_cross = []
    self_grads = []
    for s in range(seqs):
        part = slice(s * rows, (s + 1) * rows)
        grad_crossed = mxu(grad_cross[part], cross_out, NT).astype(HALF)
        query, log_sums = cross_saved[s]
        grad_cq, grad_ck, grad_cv = cross_backward(
            scalars[s],
            query,
            cross_keys[s],
            cross_values[s],
            grad_crossed,
            crosses[s],
            log_sums,
            mem_count,
            head_dim,
        )
        cq_grads.append(grad_cq)
        ckv_parts.append(jnp.concatenate([grad_ck, grad_cv], axis=1))
        unit, inverse = normalized(mids[s])
        normed_cross.append((unit * norm_gain[1] + norm_bias[1]).astype(HALF))
        grad_x1, gain, shift = norm_backward(unit, inverse, norm_gain[1], mxu(grad_cq, cross_q, NT))
        gain_one, shift_one = gain_one + gain, shift_one + shift
        grad_one = grad_two[part] + grad_x1
        ones.append(grad_one)
        grad_self = grad_one.astype(HALF)
        selfs.append(grad_self)
        grad_attended = mxu(grad_self, self_out, NT).astype(HALF)
        self_grads.append(exchange(grad_attended, n, me))
    qkv_grads = []
    for s in range(seqs):
        kept_out, log_sums = self_saved[s]
        pieces = self_backward(
            scalars[s], kept[s], self_grads[s], kept_out, log_sums, n_heads, head_dim
        )
        qkv_grads.append(gather_columns(pieces, n, me))

    grad_ckv = lax.psum(jnp.stack(ckv_parts), "blk").reshape(seqs * padded, 2 * model_width)
    own_rows = lax.dynamic_slice_in_dim(cross_kv, me * shard_width, shard_width, 0)
    grad_memory = mxu(grad_ckv, own_rows, NT).reshape(seqs, padded, shard_width)[:, :mem_count]
    own_memory = jnp.pad(memory, ((0, 0), (0, padded - mem_count), (0, 0)))
    grad_cross_kv = mxu(own_memory.reshape(seqs * padded, shard_width), grad_ckv, TN)
    column_own = (jnp.arange(model_width, dtype=jnp.int32) // shard_width == me).astype(F32)
    bias_cross_v = col_sums(grad_ckv[:, model_width:]) * column_own

    grad_cq = jnp.concatenate(cq_grads, axis=0)
    grad_cross_q = mxu(jnp.concatenate(normed_cross, axis=0), grad_cq, TN)
    grad_self = jnp.concatenate(selfs, axis=0)
    grad_self_out = mxu(attended, grad_self, TN)
    grad_qkv = jnp.concatenate(qkv_grads, axis=0)
    grad_self_qkv = mxu(normed_self, grad_qkv, TN)
    grad_x0, gain_zero, shift_zero = norm_backward(
        unit_self, inverse_self, norm_gain[0], mxu(grad_qkv, qkv_weights, NT)
    )
    grad_tokens = (jnp.concatenate(ones, axis=0) + grad_x0).reshape(seqs, rows, model_width)
    qkv_sums = col_sums(grad_qkv).reshape(n, 3, width)
    gain_terms = jnp.stack([gain_zero, gain_one, gain_two])
    shift_terms = jnp.stack([shift_zero, shift_one, shift_two])
    bias_terms = jnp.stack(
        [
            qkv_sums[:, 0].reshape(-1),
            qkv_sums[:, 2].reshape(-1),
            col_sums(grad_self),
            col_sums(grad_cq),
            bias_cross_v,
            col_sums(grad_cross),
            col_sums(grad_mlp),
        ]
    )

    def scatter(tensor, axis):
        return lax.psum_scatter(tensor.astype(HALF), "blk", scatter_dimension=axis, tiled=True)

    def over_pages(tensor):
        return lax.psum(tensor.astype(HALF), "page").astype(F32)

    small = jnp.concatenate(
        [gain_terms, shift_terms, bias_terms, grad_fc_bias.reshape(n, 4, -1).transpose(1, 0, 2).reshape(4, -1)],
        axis=0,
    )
    small = over_pages(scatter(small, 1))
    total_qkv = over_pages(scatter(grad_self_qkv, 0))
    total_qkv = total_qkv.reshape(-1, n, 3, width).transpose(0, 2, 1, 3).reshape(-1, 3 * model_width)
    return (
        result,
        grad_tokens,
        grad_memory,
        small[0:3],
        small[3:6],
        total_qkv,
        over_pages(scatter(grad_self_out, 0)),
        over_pages(scatter(grad_cross_q, 0)),
        over_pages(grad_cross_kv),
        over_pages(scatter(grad_cross_out, 0)),
        over_pages(scatter(grad_fc_in, 0)),
        over_pages(scatter(grad_fc_out, 0)),
        small[13:17].reshape(-1),
        small[6:13],
    )


def solution(mesh):
    rows_spec = P("page", "blk", None)
    return jax.shard_map(
        partial(shards, n=mesh.shape["blk"]),
        mesh=mesh,
        in_specs=(rows_spec, P("page", None, "blk"), P("page"), P("page"))
        + (P(),) * 11
        + (rows_spec,),
        out_specs=(
            rows_spec,
            rows_spec,
            P("page", None, "blk"),
            P(None, "blk"),
            P(None, "blk"),
            P("blk", None),
            P("blk", None),
            P("blk", None),
            P("blk", None),
            P("blk", None),
            P("blk", None),
            P("blk", None),
            P("blk"),
            P(None, "blk"),
        ),
        check_vma=False,
    )
```

```python
from functools import partial

import jax
import jax.numpy as jnp
from jax import lax
from jax.experimental import pallas as pl
from jax.experimental.pallas import tpu as pltpu
from jax.sharding import PartitionSpec as P

HEADS = 16
EPSILON = 1e-05
NEG_LARGE = -1e30
HALF = jnp.bfloat16
F32 = jnp.float32
LOG2E = 1.4426950408889634
LN2 = 0.6931471805599453
NT = (((1,), (1,)), ((), ()))
NN = (((1,), (0,)), ((), ()))
TN = (((0,), (0,)), ((), ()))
VMEM_LIMIT = 56 * 2**20


def mxu(left_op, right_op, dims=NN):
    return lax.dot_general(left_op, right_op, dims, preferred_element_type=F32)


def head_lanes(width, head, head_dim):
    lane = lax.broadcasted_iota(jnp.int32, (1, width), 1)
    return (lane >= head * head_dim) & (lane < (head + 1) * head_dim)


def one_head(tensor, head, n_heads, head_dim):
    if n_heads == 1:
        return tensor
    return jnp.where(
        head_lanes(tensor.shape[-1], head, head_dim), tensor, jnp.zeros_like(tensor)
    )


def causal(scores, key_start, query_start):
    key_pos = key_start + lax.broadcasted_iota(jnp.int32, scores.shape, 0)
    query_pos = query_start + lax.broadcasted_iota(jnp.int32, scores.shape, 1)
    return jnp.where(key_pos <= query_pos, scores, NEG_LARGE)


def load_pieces(scalars, pieces, whole, sem):
    rows = pieces[0].shape[1]
    copies = []
    for t, piece in enumerate(pieces):
        for u in range(2):
            owner = lax.bitwise_xor(scalars[1], 2 * t + u)
            start = pl.multiple_of(owner * rows, rows)
            copies.append(
                pltpu.make_async_copy(
                    piece.at[u], whole.at[pl.ds(start, rows)], sem.at[2 * t + u]
                )
            )
    for copy in copies:
        copy.start()
    return copies


def store_pieces(scalars, own, other, whole, sem):
    count, rows = own.shape[0], own.shape[1]
    copies = []
    for t in range(count):
        for u, target in enumerate((own, other)):
            start = pl.multiple_of(lax.bitwise_xor(scalars[1], 2 * t + u) * rows, rows)
            copies.append(
                pltpu.make_async_copy(
                    whole.at[pl.ds(start, rows)], target.at[t], sem.at[2 * t + u]
                )
            )
    for copy in copies:
        copy.start()
    return copies


def load_columns(scalars, pieces, whole, sem, parts):
    if len(pieces[0].shape) == 2:
        copies = [pltpu.make_async_copy(pieces[0], whole, sem.at[0])]
        copies[0].start()
        return copies
    width = pieces[0].shape[2] // parts
    model_width = width * 2 * len(pieces)
    copies = []
    for t, piece in enumerate(pieces):
        for u in range(2):
            owner = lax.bitwise_xor(scalars[1], 2 * t + u)
            for part in range(parts):
                start = pl.multiple_of(part * model_width + owner * width, width)
                copies.append(
                    pltpu.make_async_copy(
                        piece.at[u, :, part * width : (part + 1) * width],
                        whole.at[:, pl.ds(start, width)],
                        sem.at[(2 * t + u) * parts + part],
                    )
                )
    for copy in copies:
        copy.start()
    return copies


def self_forward_kernel(scalars, *refs, count, n_heads, head_dim, q_block, k_block, stat_block):
    pieces, refs = refs[:count], refs[count:]
    own, other, kept_out, log_sums, whole, values_t, sem = refs
    width = n_heads * head_dim
    index = pl.program_id(0)
    k_blocks = values_t.shape[0]

    @pl.when(index == 0)
    def _():
        for copy in load_pieces(scalars, pieces, whole, sem):
            copy.wait()
        for b in range(k_blocks):
            values_t[b] = whole[b * k_block : (b + 1) * k_block, 2 * width :].T

    start = pl.multiple_of(index * q_block, q_block)
    q_rows = pl.ds(start, q_block)
    live = start < scalars[0]

    @pl.when(jnp.logical_not(live))
    def _():
        kept_out[q_rows, :] = jnp.zeros((q_block, width), HALF)
        log_sums[...] = jnp.zeros_like(log_sums)

    @pl.when(live)
    def _():
        query = whole[q_rows, :width]
        queries = [one_head(query, h, n_heads, head_dim) for h in range(n_heads)]

        def step(kb, carry, masked):
            keys = whole[pl.ds(pl.multiple_of(kb * k_block, k_block), k_block), width : 2 * width]
            value_t = values_t[kb]
            out = []
            for h in range(n_heads):
                top, total, acc = carry[h]
                scores = mxu(keys, queries[h], NT)
                if masked:
                    scores = causal(scores, kb * k_block, start)
                new_top = jnp.maximum(top, jnp.max(scores, axis=0, keepdims=True))
                probs = jnp.exp2(scores - new_top)
                scale = jnp.exp2(top - new_top)
                total = total * scale + jnp.sum(probs, axis=0, keepdims=True)
                part = mxu(value_t[h * head_dim : (h + 1) * head_dim], probs.astype(HALF))
                out.append((new_top, total, acc * scale + part))
            return tuple(out)

        carry = tuple(
            (
                jnp.full((1, q_block), NEG_LARGE, F32),
                jnp.zeros((1, q_block), F32),
                jnp.zeros((head_dim, q_block), F32),
            )
            for _ in range(n_heads)
        )
        ratio = q_block // k_block
        carry = lax.fori_loop(0, index * ratio, lambda kb, c: step(kb, c, False), carry)
        for t in range(ratio):
            carry = step(index * ratio + t, carry, True)
        result_t = jnp.concatenate([acc / total for _, total, acc in carry], axis=0)
        kept_out[q_rows, :] = result_t.T.astype(HALF)
        for h, (top, total, _) in enumerate(carry):
            log_sum = top + jnp.log2(total)
            for t in range(q_block // stat_block):
                log_sums[t, h : h + 1, :] = log_sum[:, t * stat_block : (t + 1) * stat_block]

    @pl.when(index == pl.num_programs(0) - 1)
    def _():
        for copy in store_pieces(scalars, own, other, kept_out, sem):
            copy.wait()


def self_forward(scalars, pieces, n_heads, head_dim):
    count, rows = len(pieces), pieces[0].shape[1]
    n = 2 * count
    length, width = n * rows, n_heads * head_dim
    q_block, k_block, stat_block = 1024, 512, 512
    any_spec = pl.BlockSpec(memory_space=pl.ANY)
    return pl.pallas_call(
        partial(
            self_forward_kernel,
            count=count,
            n_heads=n_heads,
            head_dim=head_dim,
            q_block=q_block,
            k_block=k_block,
            stat_block=stat_block,
        ),
        grid_spec=pltpu.PrefetchScalarGridSpec(
            num_scalar_prefetch=1,
            grid=(length // q_block,),
            in_specs=[any_spec] * count,
            out_specs=[any_spec] * 2
            + [
                pl.BlockSpec((length, width), lambda i, s: (0, 0)),
                pl.BlockSpec((q_block // stat_block, n_heads, stat_block), lambda i, s: (i, 0, 0)),
            ],
            scratch_shapes=[
                pltpu.VMEM((length, 3 * width), HALF),
                pltpu.VMEM((length // k_block, width, k_block), HALF),
                pltpu.SemaphoreType.DMA((n,)),
            ],
        ),
        out_shape=[jax.ShapeDtypeStruct((count, rows, width), HALF)] * 2
        + [
            jax.ShapeDtypeStruct((length, width), HALF),
            jax.ShapeDtypeStruct((length // stat_block, n_heads, stat_block), F32),
        ],
        compiler_params=pltpu.CompilerParams(vmem_limit_bytes=VMEM_LIMIT),
        cost_estimate=pl.CostEstimate(
            flops=2 * 2 * length * length * width,
            bytes_accessed=length * width * 10,
            transcendentals=n_heads * length * length // 2,
        ),
        name="self_forward",
    )(scalars, *pieces)


def self_backward_kernel(scalars, *refs, count, n_heads, head_dim, block, last):
    pieces, refs = refs[:count], refs[count:]
    grad_pieces, refs = refs[:count], refs[count:]
    kept_out, log_sums, normed_ref, refs = *refs[:3], refs[3:]
    if last:
        earlier, earlier_sums, refs = refs[0], refs[1], refs[2:]
        own, other, columns_own, columns_other, sums, refs = *refs[:5], refs[5:]
        total, refs = refs[0], refs[1:]
    else:
        own, other, total, sums, refs = *refs[:4], refs[4:]
    result, whole, grads, query_heads, grad_heads, deltas, query_sums, sem, grad_sem = refs
    width = n_heads * head_dim
    index = pl.program_id(0)
    blocks = query_heads.shape[1]
    model_width = total.shape[1]
    span = scalars[0]

    @pl.when(index == 0)
    def _():
        copies = load_pieces(scalars, pieces, whole, sem)
        copies += load_pieces(scalars, grad_pieces, grads, grad_sem)
        query_sums[...] = jnp.zeros_like(query_sums)
        total[...] = earlier[...] if last else jnp.zeros_like(total)
        sums[...] = earlier_sums[...] if last else jnp.zeros_like(sums)
        for copy in copies:
            copy.wait()

        @pl.loop(0, (span + block - 1) // block)
        def _(b):
            rows = pl.ds(pl.multiple_of(b * block, block), block)
            query, grad = whole[rows, :width], grads[rows, :]
            products = (grad.astype(F32) * kept_out[rows, :].astype(F32)).T
            for h in range(n_heads):
                deltas[b, h : h + 1, :] = jnp.sum(
                    products[h * head_dim : (h + 1) * head_dim], axis=0, keepdims=True
                )
                query_heads[h, b] = one_head(query, h, n_heads, head_dim)
                grad_heads[h, b] = one_head(grad, h, n_heads, head_dim)

    start = pl.multiple_of(index * block, block)
    k_rows = pl.ds(start, block)
    live = start < span

    @pl.when(jnp.logical_not(live))
    def _():
        result[k_rows, :] = jnp.zeros((block, 3 * width), HALF)

    @pl.when(live)
    def _():
        keys = whole[k_rows, width : 2 * width]
        values = whole[k_rows, 2 * width :]
        keys_t = keys.T

        def step(qb, carry, masked):
            grad_keys, grad_values = carry
            for h in range(n_heads):
                query, grad = query_heads[h, qb], grad_heads[h, qb]
                scores = mxu(keys, query, NT)
                if masked:
                    scores = causal(scores, start, qb * block)
                probs = jnp.exp2(scores - log_sums[qb, h : h + 1, :])
                grad_probs = mxu(values, grad, NT)
                grad_scores = (probs * (grad_probs - deltas[qb, h : h + 1, :])).astype(HALF)
                grad_values = grad_values + mxu(probs.astype(HALF), grad)
                grad_keys = grad_keys + mxu(grad_scores, query)
                lanes = slice(h * head_dim, (h + 1) * head_dim)
                query_sums[qb, lanes, :] += mxu(keys_t[lanes], grad_scores)
            return grad_keys, grad_values

        zero = jnp.zeros((block, width), F32)
        carry = step(index, (zero, zero), True)
        live_blocks = (span + block - 1) // block
        grad_keys, grad_values = lax.fori_loop(
            index + 1, live_blocks, lambda qb, c: step(qb, c, False), carry
        )
        query_t = (query_sums[index] * 0.125).astype(HALF)
        grad_queries = query_t.T
        grad_keys = (grad_keys * LN2).astype(HALF)
        grad_values = grad_values.astype(HALF)
        result[k_rows, :width] = grad_queries
        result[k_rows, width : 2 * width] = grad_keys
        result[k_rows, 2 * width :] = grad_values
        sums[0:1] += jnp.sum(grad_queries.astype(F32), axis=0, keepdims=True)
        sums[1:2] += jnp.sum(grad_values.astype(F32), axis=0, keepdims=True)
        normed = normed_ref[...].reshape(block, model_width)
        for part, tensor in enumerate((query_t, grad_keys.T, grad_values.T)):
            total[part * width : (part + 1) * width] += mxu(tensor, normed)

    @pl.when(index == pl.num_programs(0) - 1)
    def _():
        copies = store_pieces(scalars, own, other, result, sem)
        if last:
            shard = columns_own.shape[1]
            chip, core = scalars[1] // 2, lax.bitwise_and(scalars[1], 1)
            for p in range(count):
                tile = total[:, p * 2 * shard : (p + 1) * 2 * shard].T.astype(HALF)
                slot = lax.bitwise_xor(chip, p)
                columns_own[slot], columns_other[slot] = row_split(core, tile, shard)
        for copy in copies:
            copy.wait()


def self_backward(
    scalars, pieces, grad_pieces, kept_out, log_sums, normed, seq, n_heads, head_dim, earlier
):
    count, rows = len(pieces), pieces[0].shape[1]
    n, model_width = 2 * count, normed.shape[3]
    length, width = n * rows, n_heads * head_dim
    block = log_sums.shape[2]
    blocks = length // block
    last = earlier is not None
    any_spec = pl.BlockSpec(memory_space=pl.ANY)
    fixed = lambda shape: pl.BlockSpec(shape, lambda i, s: (0,) * len(shape))
    total, sums = (3 * width, model_width), (8, width)
    packed = (count, model_width // n, 3 * width)
    return pl.pallas_call(
        partial(
            self_backward_kernel,
            count=count,
            n_heads=n_heads,
            head_dim=head_dim,
            block=block,
            last=last,
        ),
        grid_spec=pltpu.PrefetchScalarGridSpec(
            num_scalar_prefetch=1,
            grid=(blocks,),
            in_specs=[any_spec] * (2 * count)
            + [
                fixed((length, width)),
                fixed((blocks, n_heads, block)),
                pl.BlockSpec(
                    (block // rows, 1, rows, model_width), lambda i, s: (i, seq, 0, 0)
                ),
            ]
            + ([fixed(total), fixed(sums)] if last else []),
            out_specs=[any_spec] * 2
            + [fixed(shape) for shape in ((packed, packed, sums) if last else (total, sums))],
            scratch_shapes=([pltpu.VMEM(total, F32)] if last else [])
            + [
                pltpu.VMEM((length, 3 * width), HALF),
                pltpu.VMEM((length, 3 * width), HALF),
                pltpu.VMEM((length, width), HALF),
                pltpu.VMEM((n_heads, blocks, block, width), HALF),
                pltpu.VMEM((n_heads, blocks, block, width), HALF),
                pltpu.VMEM((blocks, n_heads, block), F32),
                pltpu.VMEM((blocks, width, block), F32),
                pltpu.SemaphoreType.DMA((n,)),
                pltpu.SemaphoreType.DMA((n,)),
            ],
        ),
        out_shape=[jax.ShapeDtypeStruct((count, rows, 3 * width), HALF)] * 2
        + (
            [jax.ShapeDtypeStruct(packed, HALF)] * 2
            if last
            else [jax.ShapeDtypeStruct(total, F32)]
        )
        + [jax.ShapeDtypeStruct(sums, F32)],
        compiler_params=pltpu.CompilerParams(vmem_limit_bytes=VMEM_LIMIT),
        cost_estimate=pl.CostEstimate(
            flops=5 * 2 * length * length * width // 2,
            bytes_accessed=length * width * 20,
            transcendentals=n_heads * length * length // 2,
        ),
        name="self_backward",
    )(scalars, *pieces, *grad_pieces, kept_out, log_sums, normed, *(earlier or ()))


def cross_scores(keys, query, mem_count):
    scores = mxu(keys, query, NT)
    padded = scores.shape[0]
    if padded == mem_count:
        return scores
    whole = mem_count // 8 * 8
    tail = scores[whole:]
    position = whole + lax.broadcasted_iota(jnp.int32, tail.shape, 0)
    tail = jnp.where(position < mem_count, tail, NEG_LARGE)
    return jnp.concatenate([scores[:whole], tail], axis=0)


def cross_forward_kernel(scalars, query_ref, key_ref, value_ref, out_ref, log_sums, *, mem_count, head_dim):
    rows, width = query_ref.shape
    live = scalars[1] * rows < scalars[0]

    @pl.when(jnp.logical_not(live))
    def _():
        out_ref[...] = jnp.zeros_like(out_ref)
        log_sums[...] = jnp.zeros_like(log_sums)

    @pl.when(live)
    def _():
        n_heads = width // head_dim
        query, keys = query_ref[...], key_ref[...]
        values_t = value_ref[...].T
        results = []
        for h in range(n_heads):
            scores = cross_scores(keys, one_head(query, h, n_heads, head_dim), mem_count)
            top = jnp.max(scores, axis=0, keepdims=True)
            probs = jnp.exp2(scores - top)
            total = jnp.sum(probs, axis=0, keepdims=True)
            lanes = slice(h * head_dim, (h + 1) * head_dim)
            results.append(mxu(values_t[lanes], probs.astype(HALF)) / total)
            log_sums[0, h : h + 1, :] = top + jnp.log2(total)
        out_ref[...] = jnp.concatenate(results, axis=0).T.astype(HALF)


def cross_forward(scalars, query, keys, values, mem_count, head_dim):
    rows, model_width = query.shape
    padded = keys.shape[0]
    width = 128
    groups, n_heads = model_width // width, width // head_dim
    column = lambda count: pl.BlockSpec((count, width), lambda g, s: (0, g))
    return pl.pallas_call(
        partial(cross_forward_kernel, mem_count=mem_count, head_dim=head_dim),
        grid_spec=pltpu.PrefetchScalarGridSpec(
            num_scalar_prefetch=1,
            grid=(groups,),
            in_specs=[column(rows), column(padded), column(padded)],
            out_specs=[column(rows), pl.BlockSpec((1, n_heads, rows), lambda g, s: (g, 0, 0))],
        ),
        out_shape=[
            jax.ShapeDtypeStruct((rows, model_width), HALF),
            jax.ShapeDtypeStruct((groups, n_heads, rows), F32),
        ],
        compiler_params=pltpu.CompilerParams(vmem_limit_bytes=VMEM_LIMIT),
        cost_estimate=pl.CostEstimate(
            flops=4 * 2 * rows * padded * model_width,
            bytes_accessed=(rows + padded) * model_width * 4,
            transcendentals=rows * padded * model_width // head_dim,
        ),
        name="cross_forward",
    )(scalars, query, keys, values)


def cross_backward_kernel(
    scalars,
    query_ref,
    key_ref,
    value_ref,
    grad_ref,
    out_ref,
    log_sums,
    grad_query,
    grad_key,
    grad_value,
    *,
    mem_count,
    head_dim,
):
    rows, width = query_ref.shape
    padded = key_ref.shape[0]
    live = scalars[1] * rows < scalars[0]

    @pl.when(jnp.logical_not(live))
    def _():
        grad_query[...] = jnp.zeros_like(grad_query)
        grad_key[...] = jnp.zeros_like(grad_key)
        grad_value[...] = jnp.zeros_like(grad_value)

    @pl.when(live)
    def _():
        n_heads = width // head_dim
        query_all, keys, values, grad_all = query_ref[...], key_ref[...], value_ref[...], grad_ref[...]
        keys_t = keys.T
        products = (grad_all.astype(F32) * out_ref[...].astype(F32)).T
        query_parts = []
        key_sum = jnp.zeros((padded, width), F32)
        value_sum = jnp.zeros((padded, width), F32)
        for h in range(n_heads):
            lanes = slice(h * head_dim, (h + 1) * head_dim)
            query = one_head(query_all, h, n_heads, head_dim)
            grad = one_head(grad_all, h, n_heads, head_dim)
            delta = jnp.sum(products[lanes], axis=0, keepdims=True)
            scores = cross_scores(keys, query, mem_count)
            probs = jnp.exp2(scores - log_sums[0, h : h + 1, :])
            grad_probs = mxu(values, grad, NT)
            grad_scores = (probs * (grad_probs - delta)).astype(HALF)
            value_sum = value_sum + mxu(probs.astype(HALF), grad)
            key_sum = key_sum + mxu(grad_scores, query)
            query_parts.append(mxu(keys_t[lanes], grad_scores))
        grad_query[...] = (jnp.concatenate(query_parts, axis=0) * 0.125).T.astype(HALF)
        grad_key[...] = (key_sum * LN2).astype(HALF)
        grad_value[...] = value_sum.astype(HALF)


def cross_backward(scalars, query, keys, values, grad, kept_out, log_sums, mem_count, head_dim):
    rows, model_width = query.shape
    padded = keys.shape[0]
    width = 128
    groups, n_heads = model_width // width, width // head_dim
    column = lambda count: pl.BlockSpec((count, width), lambda g, s: (0, g))
    return pl.pallas_call(
        partial(cross_backward_kernel, mem_count=mem_count, head_dim=head_dim),
        grid_spec=pltpu.PrefetchScalarGridSpec(
            num_scalar_prefetch=1,
            grid=(groups,),
            in_specs=[
                column(rows),
                column(padded),
                column(padded),
                column(rows),
                column(rows),
                pl.BlockSpec((1, n_heads, rows), lambda g, s: (g, 0, 0)),
            ],
            out_specs=[column(rows), column(padded), column(padded)],
        ),
        out_shape=[
            jax.ShapeDtypeStruct((rows, model_width), HALF),
            jax.ShapeDtypeStruct((padded, model_width), HALF),
            jax.ShapeDtypeStruct((padded, model_width), HALF),
        ],
        compiler_params=pltpu.CompilerParams(vmem_limit_bytes=VMEM_LIMIT),
        cost_estimate=pl.CostEstimate(
            flops=10 * 2 * rows * padded * model_width,
            bytes_accessed=(rows + padded) * model_width * 10,
            transcendentals=rows * padded * model_width // head_dim,
        ),
        name="cross_backward",
    )(scalars, query, keys, values, grad, kept_out, log_sums)


def exchange(own, other, n):
    return chips(own, cores(other, n), n)


def cores(other, n):
    return lax.ppermute(other, "blk", [(k, k ^ 1) for k in range(n)])


def chips(own, sibling, n):
    received = []
    for t in range(n // 2):
        message = jnp.stack([own[t], sibling[t]])
        if t:
            message = lax.ppermute(message, "blk", [(k, k ^ (2 * t)) for k in range(n)])
        received.append(message)
    return received


def columns_of(pieces, me, parts):
    rows, width = pieces[0].shape[1], pieces[0].shape[2] // parts
    if width % 128 == 0:
        return pieces
    n = 2 * len(pieces)
    order = lax.bitwise_xor(jnp.arange(n, dtype=jnp.int32), me)
    whole = jnp.concatenate(pieces, axis=0).reshape(n, rows, parts, width)
    whole = jnp.take(whole, order, axis=0)
    return [whole.transpose(1, 2, 0, 3).reshape(rows, parts * n * width)]


def halve(axis, step, size):
    def run(tensor):
        bit = lax.bitwise_and(lax.axis_index(axis), step) // step
        halves = tensor.reshape((2, -1) + tensor.shape[1:])
        sent = lax.dynamic_index_in_dim(halves, 1 - bit, 0, keepdims=False)
        received = lax.ppermute(sent, axis, [(k, k ^ step) for k in range(size)])
        own = lax.dynamic_index_in_dim(halves, bit, 0, keepdims=False)
        return (own.astype(F32) + received.astype(F32)).astype(tensor.dtype)

    return run


def join(axis, step, size):
    def run(tensor):
        bit = lax.bitwise_and(lax.axis_index(axis), step) // step
        received = lax.ppermute(tensor, axis, [(k, k ^ step) for k in range(size)])
        first = jnp.where(bit == 0, tensor, received)
        second = jnp.where(bit == 0, received, tensor)
        return jnp.concatenate([first, second], axis=0)

    return run


def page_steps(pages):
    steps = [1 << b for b in range(pages.bit_length() - 1)]
    return [halve("page", step, pages) for step in steps] + [
        join("page", step, pages) for step in reversed(steps)
    ]


def fold_chips(bit, n, low):
    def run(tensor):
        half = tensor.shape[0] // 2
        pairs = [(k, k ^ (2 << bit)) for k in range(n)]
        axis = 1 if low else 0
        halves = tensor.reshape(((half, 2) if low else (2, half)) + tensor.shape[1:])
        received = lax.ppermute(lax.index_in_dim(halves, 1, axis, keepdims=False), "blk", pairs)
        return add_half(lax.index_in_dim(halves, 0, axis, keepdims=False), received)

    return run


class Chain:
    def __init__(self, tensor, steps):
        self.tensor, self.steps = tensor, list(steps)

    def advance(self):
        if self.steps:
            self.tensor = self.steps.pop(0)(self.tensor)

    def complete(self):
        while self.steps:
            self.advance()
        return self.tensor


def add_half(left, right):
    return (left.astype(F32) + right.astype(F32)).astype(HALF)


def tick(chains):
    for chain in chains:
        chain.advance()


def after(chains, value):
    value, tensors = lax.optimization_barrier((value, [chain.tensor for chain in chains]))
    for chain, tensor in zip(chains, tensors):
        chain.tensor = tensor
    return value


def small_sums(tensor, n, pages):
    me, page = lax.axis_index("blk"), lax.axis_index("page")
    step = n // 2
    while step:
        bit = lax.bitwise_and(me, step) // step
        halves = tensor.reshape((2, -1) + tensor.shape[1:])
        sent = lax.dynamic_index_in_dim(halves, 1 - bit, 0, keepdims=False)
        received = lax.ppermute(sent, "blk", [(k, k ^ step) for k in range(n)])
        tensor = lax.dynamic_index_in_dim(halves, bit, 0, keepdims=False) + received
        step //= 2
    step = 1
    while step < pages:
        tensor = tensor + lax.ppermute(tensor, "page", [(k, k ^ step) for k in range(pages)])
        step *= 2
    return tensor[0]


def normalized(vector):
    centre = vector - jnp.mean(vector, axis=-1, keepdims=True)
    spread = jnp.mean(centre * centre, axis=-1, keepdims=True)
    inverse = lax.rsqrt(spread + EPSILON)
    return centre * inverse, inverse


def norm_backward(unit, inverse, gain, grad):
    scaled = grad * gain
    first = jnp.mean(scaled, axis=-1, keepdims=True)
    second = jnp.mean(scaled * unit, axis=-1, keepdims=True)
    grad_in = inverse * (scaled - first - unit * second)
    return grad_in, jnp.sum(grad * unit, axis=0), jnp.sum(grad, axis=0)


def by_parity(core, tensor, width):
    even, odd = tensor[:, :width], tensor[:, width:]
    return jnp.where(core == 0, even, odd), jnp.where(core == 0, odd, even)


def row_split(core, tensor, width):
    even, odd = tensor[:width], tensor[width:]
    return jnp.where(core == 0, even, odd), jnp.where(core == 0, odd, even)


GROUP_TILE = 512


def placed(parts):
    found, row = [], 0
    for part in parts:
        column = 0
        for array in part if isinstance(part, tuple) else (part,):
            found.append((array, row, column))
            column += array.shape[1]
        row += array.shape[0]
    return found, row, column


def weights_kernel(scalars, *refs, phases, places):
    hbm = []
    for spots in places:
        hbm.append(refs[: len(spots)])
        refs = refs[len(spots) :]
    own, other, refs = refs[0], refs[1], refs[2:]
    held, turned, sems = refs[: len(places)], refs[len(places)], refs[len(places) + 1 :]
    step = pl.program_id(0)
    count, width, _ = own.shape
    chip, core = scalars[1] // 2, lax.bitwise_and(scalars[1], 1)

    def copies(k):
        found = []
        for i, (row, column) in enumerate(places[k]):
            source = hbm[k][i]
            rows, columns = source.shape
            target = held[k].at[row : row + rows, column : column + columns]
            found.append(pltpu.make_async_copy(source, target, sems[k].at[i]))
        return found

    @pl.when(step == 0)
    def _():
        for k in range(len(places)):
            for copy in copies(k):
                copy.start()
        for k, spots in enumerate(places):
            filled = max(row + source.shape[0] for (row, _), source in zip(spots, hbm[k]))
            if filled < held[k].shape[0]:
                held[k][filled:, :] = jnp.zeros((held[k].shape[0] - filled, held[k].shape[1]), HALF)

    for k, (depth, first, tiles) in enumerate(phases):
        left, right = held[2 * k], held[2 * k + 1 if depth else 2 * k - 1]

        @pl.when(step == first)
        def _(k=k, depth=depth, left=left):
            for copy in copies(2 * k) + (copies(2 * k + 1) if depth else []):
                copy.wait()
            if depth:
                turned[:, :depth] = left[...].T

        @pl.when((step >= first) & (step < first + tiles))
        def _(depth=depth, first=first, left=left, right=right):
            at = pl.multiple_of((step - first) * GROUP_TILE, GROUP_TILE)
            for p in range(count):
                rows = slice(p * 2 * width, (p + 1) * 2 * width)
                if depth:
                    tile = mxu(turned[rows, :depth], right[:depth, pl.ds(at, GROUP_TILE)])
                else:
                    tile = mxu(left[rows, :], right[pl.ds(at, GROUP_TILE), :], NT)
                slot = lax.bitwise_xor(chip, p)
                own[slot], other[slot] = row_split(core, tile.astype(HALF), width)


def weight_grads(scalars, pairs, memory_weights, n):
    operands, places, buffers, phases = [], [], [], []

    def hold(parts, multiple):
        spots, rows, columns = placed(parts)
        operands.extend(array for array, _, _ in spots)
        places.append([(row, column) for _, row, column in spots])
        rows = -(-rows // multiple) * multiple
        buffers.append(pltpu.VMEM((rows, columns), HALF))
        return rows, columns

    first = 0
    for left, right in pairs:
        depth, model_width = hold(left, 128)
        rows, columns = hold(right, GROUP_TILE)
        phases.append((depth, first, columns // GROUP_TILE))
        first += phases[-1][2]
    if memory_weights is not None:
        hold([memory_weights], 128)
        phases.append((0, first, rows // GROUP_TILE))
        first += phases[-1][2]
    depth = max(phase[0] for phase in phases)
    count, width = n // 2, model_width // n
    block = pl.BlockSpec((count, width, GROUP_TILE), lambda j, s: (0, 0, j))
    shape = jax.ShapeDtypeStruct((count, width, first * GROUP_TILE), HALF)
    return pl.pallas_call(
        partial(weights_kernel, phases=phases, places=places),
        grid_spec=pltpu.PrefetchScalarGridSpec(
            num_scalar_prefetch=1,
            grid=(first,),
            in_specs=[pl.BlockSpec(memory_space=pl.ANY)] * len(operands),
            out_specs=[block, block],
            scratch_shapes=buffers
            + [pltpu.VMEM((model_width, depth), HALF)]
            + [pltpu.SemaphoreType.DMA((len(spots),)) for spots in places],
        ),
        out_shape=[shape, shape],
        compiler_params=pltpu.CompilerParams(vmem_limit_bytes=VMEM_LIMIT),
        cost_estimate=pl.CostEstimate(
            flops=2 * model_width * depth * first * GROUP_TILE,
            bytes_accessed=2 * model_width * (2 * depth + first * GROUP_TILE),
            transcendentals=0,
        ),
        name="weight_grads",
    )(scalars, *operands)


def rows_kernel(scalars, left_ref, right_ref, own, other, turned):
    @pl.when(pl.program_id(0) == 0)
    def _():
        turned[...] = left_ref[...].T

    core = lax.bitwise_and(scalars[1], 1)
    width = own.shape[2]
    left = turned[...]
    even = mxu(left, right_ref[:, :width]).astype(HALF)
    odd = mxu(left, right_ref[:, width:]).astype(HALF)
    own[0] = jnp.where(core == 0, even, odd)
    other[0] = jnp.where(core == 0, odd, even)


def row_grads(scalars, left, right, n):
    rows, model_width = left.shape
    count, width = n // 2, right.shape[1] // n
    block = pl.BlockSpec(
        (1, model_width, width), lambda p, s: (lax.bitwise_xor(p, s[1] // 2), 0, 0)
    )
    shape = jax.ShapeDtypeStruct((count, model_width, width), HALF)
    return pl.pallas_call(
        rows_kernel,
        grid_spec=pltpu.PrefetchScalarGridSpec(
            num_scalar_prefetch=1,
            grid=(count,),
            in_specs=[
                pl.BlockSpec((rows, model_width), lambda p, s: (0, 0)),
                pl.BlockSpec((rows, 2 * width), lambda p, s: (0, p)),
            ],
            out_specs=[block, block],
            scratch_shapes=[pltpu.VMEM((model_width, rows), HALF)],
        ),
        out_shape=[shape, shape],
        compiler_params=pltpu.CompilerParams(vmem_limit_bytes=VMEM_LIMIT),
        cost_estimate=pl.CostEstimate(
            flops=2 * rows * model_width * right.shape[1],
            bytes_accessed=2 * (rows + model_width) * right.shape[1],
            transcendentals=0,
        ),
        name="row_grads",
    )(scalars, left, right)


def project_kernel(scalars, x_ref, norm_ref, bias_ref, q_ref, k_ref, v_ref, normed_ref, own, other, *, q_scale):
    width = own.shape[2] // 3
    core = lax.bitwise_and(scalars[1], 1)

    @pl.when(pl.program_id(0) == 0)
    def _():
        unit, _ = normalized(x_ref[0].astype(F32))
        normed_ref[...] = (unit * norm_ref[0:1] + norm_ref[1:2]).astype(HALF)

    normed = normed_ref[...]
    query = ((mxu(normed, q_ref[...]) + bias_ref[0:1]) * q_scale).astype(HALF)
    keys = mxu(normed, k_ref[...]).astype(HALF)
    values = (mxu(normed, v_ref[...]) + bias_ref[1:2]).astype(HALF)
    for part, tensor in enumerate((query, keys, values)):
        lanes = slice(part * width, (part + 1) * width)
        own[0, :, lanes], other[0, :, lanes] = by_parity(core, tensor, width)


def project(scalars, x, norm, bias, weights, n, q_scale):
    rows, model_width = x.shape[1:]
    count, width = n // 2, model_width // n
    fixed = lambda shape: pl.BlockSpec(shape, lambda p, s: (0, 0))
    column = lambda part: pl.BlockSpec(
        (model_width, 2 * width), lambda p, s, part=part: (0, part * count + p)
    )
    packed = pl.BlockSpec(
        (1, rows, 3 * width), lambda p, s: (lax.bitwise_xor(p, s[1] // 2), 0, 0)
    )
    return pl.pallas_call(
        partial(project_kernel, q_scale=q_scale),
        grid_spec=pltpu.PrefetchScalarGridSpec(
            num_scalar_prefetch=1,
            grid=(count,),
            in_specs=[
                pl.BlockSpec((1, rows, model_width), lambda p, s: (s[2], 0, 0)),
                fixed((2, model_width)),
                pl.BlockSpec((2, 2 * width), lambda p, s: (0, p)),
                column(0),
                column(1),
                column(2),
            ],
            out_specs=[fixed((rows, model_width)), packed, packed],
        ),
        out_shape=[jax.ShapeDtypeStruct((rows, model_width), HALF)]
        + [jax.ShapeDtypeStruct((count, rows, 3 * width), HALF)] * 2,
        compiler_params=pltpu.CompilerParams(vmem_limit_bytes=VMEM_LIMIT),
        cost_estimate=pl.CostEstimate(
            flops=2 * rows * model_width * 3 * model_width,
            bytes_accessed=model_width * (6 * model_width + 8 * rows),
            transcendentals=0,
        ),
        name="project",
    )(scalars, x, norm, bias, weights, weights, weights)


TILE = 256


def middle_kernel(scalars, *refs, count, q_scale):
    pieces, refs = refs[:count], refs[count:]
    x_ref, params, out_hbm, query_hbm, attended, mid_ref, normed_ref, query_ref = refs[:8]
    out_weights, query_weights, sem, weight_sem = refs[8:]
    copies = load_columns(scalars, pieces, attended, sem, 1)
    first = pltpu.make_async_copy(out_hbm, out_weights, weight_sem.at[0])
    second = pltpu.make_async_copy(query_hbm, query_weights, weight_sem.at[1])
    first.start()
    second.start()
    for copy in copies:
        copy.wait()
    first.wait()
    left = attended[...]
    model_width = left.shape[1]
    for j in range(model_width // TILE):
        cols = slice(j * TILE, (j + 1) * TILE)
        mid_ref[:, cols] = (
            x_ref[:, cols].astype(F32) + mxu(left, out_weights[:, cols]) + params[2:3, cols]
        )
    unit, _ = normalized(mid_ref[...])
    normed_ref[...] = (unit * params[0:1] + params[1:2]).astype(HALF)
    second.wait()
    left = normed_ref[...]
    for j in range(model_width // TILE):
        cols = slice(j * TILE, (j + 1) * TILE)
        query_ref[:, cols] = (
            (mxu(left, query_weights[:, cols]) + params[3:4, cols]) * q_scale
        ).astype(HALF)


def middle(scalars, pieces, x, params, out_weights, query_weights, q_scale):
    rows, model_width = x.shape
    count = len(pieces)
    any_spec = pl.BlockSpec(memory_space=pl.ANY)
    vmem = pl.BlockSpec(memory_space=pltpu.VMEM)
    return pl.pallas_call(
        partial(middle_kernel, count=count, q_scale=q_scale),
        in_specs=[pl.BlockSpec(memory_space=pltpu.SMEM)] + [any_spec] * count + [vmem, vmem, any_spec, any_spec],
        out_specs=[vmem] * 4,
        out_shape=[
            jax.ShapeDtypeStruct((rows, model_width), HALF),
            jax.ShapeDtypeStruct((rows, model_width), F32),
            jax.ShapeDtypeStruct((rows, model_width), HALF),
            jax.ShapeDtypeStruct((rows, model_width), HALF),
        ],
        scratch_shapes=[
            pltpu.VMEM((model_width, model_width), HALF),
            pltpu.VMEM((model_width, model_width), HALF),
            pltpu.SemaphoreType.DMA((2 * count,)),
            pltpu.SemaphoreType.DMA((2,)),
        ],
        compiler_params=pltpu.CompilerParams(vmem_limit_bytes=VMEM_LIMIT),
        cost_estimate=pl.CostEstimate(
            flops=4 * rows * model_width * model_width,
            bytes_accessed=model_width * (4 * model_width + 12 * rows),
            transcendentals=0,
        ),
        name="middle",
    )(scalars, *pieces, x, params, out_weights, query_weights)


def turn_kernel(
    scalars, grad_query, mid_ref, grad_ref, params, query_hbm, out_hbm,
    grad_mid, half_ref, own, other, sums,
    query_weights, out_weights, back, weight_sem,
):
    first = pltpu.make_async_copy(query_hbm, query_weights, weight_sem.at[0])
    second = pltpu.make_async_copy(out_hbm, out_weights, weight_sem.at[1])
    first.start()
    second.start()
    count, _, width = own.shape
    chip, core = scalars[1] // 2, lax.bitwise_and(scalars[1], 1)
    unit, inverse = normalized(mid_ref[...])
    first.wait()
    left = grad_query[...]
    model_width = left.shape[1]
    for j in range(model_width // TILE):
        cols = slice(j * TILE, (j + 1) * TILE)
        back[:, cols] = mxu(left, query_weights[cols, :], NT)
    grad_in, gain, shift = norm_backward(unit, inverse, params[0:1], back[...])
    total = grad_ref[...] + grad_in
    grad_mid[...] = total
    half = total.astype(HALF)
    half_ref[...] = half
    sums[0:1] = gain[None]
    sums[1:2] = shift[None]
    sums[2:3] = jnp.sum(half.astype(F32), axis=0, keepdims=True)
    sums[3:4] = jnp.sum(left.astype(F32), axis=0, keepdims=True)
    sums[4:8] = jnp.zeros((4, model_width), F32)
    second.wait()
    for p in range(count):
        tile = mxu(half, out_weights[p * 2 * width : (p + 1) * 2 * width, :], NT).astype(HALF)
        slot = lax.bitwise_xor(chip, p)
        own[slot], other[slot] = by_parity(core, tile, width)


def turn(scalars, grad_query, mid, grad, params, query_weights, out_weights, n):
    rows, model_width = mid.shape
    count, width = n // 2, model_width // n
    any_spec = pl.BlockSpec(memory_space=pl.ANY)
    vmem = pl.BlockSpec(memory_space=pltpu.VMEM)
    return pl.pallas_call(
        turn_kernel,
        in_specs=[pl.BlockSpec(memory_space=pltpu.SMEM)] + [vmem] * 4 + [any_spec] * 2,
        out_specs=[vmem] * 5,
        out_shape=[
            jax.ShapeDtypeStruct((rows, model_width), F32),
            jax.ShapeDtypeStruct((rows, model_width), HALF),
            jax.ShapeDtypeStruct((count, rows, width), HALF),
            jax.ShapeDtypeStruct((count, rows, width), HALF),
            jax.ShapeDtypeStruct((8, model_width), F32),
        ],
        scratch_shapes=[
            pltpu.VMEM((model_width, model_width), HALF),
            pltpu.VMEM((model_width, model_width), HALF),
            pltpu.VMEM((rows, model_width), F32),
            pltpu.SemaphoreType.DMA((2,)),
        ],
        compiler_params=pltpu.CompilerParams(vmem_limit_bytes=VMEM_LIMIT),
        cost_estimate=pl.CostEstimate(
            flops=4 * rows * model_width * model_width,
            bytes_accessed=model_width * (4 * model_width + 20 * rows),
            transcendentals=0,
        ),
        name="turn",
    )(scalars, grad_query, mid, grad, params, query_weights, out_weights)


def finish_kernel(scalars, *refs, count):
    pieces, refs = refs[:count], refs[count:]
    x_ref, grad_ref, params, weights_hbm, grad_x, sums = refs[:6]
    grads, weights, back, sem, weight_sem = refs[6:]
    copies = load_columns(scalars, pieces, grads, sem, 3)
    fetch = pltpu.make_async_copy(weights_hbm, weights, weight_sem.at[0])
    fetch.start()
    unit, inverse = normalized(x_ref[...].astype(F32))
    for copy in copies:
        copy.wait()
    fetch.wait()
    left = grads[...]
    model_width = back.shape[1]
    for j in range(model_width // TILE):
        cols = slice(j * TILE, (j + 1) * TILE)
        back[:, cols] = mxu(left, weights[cols, :], NT)
    grad_in, gain, shift = norm_backward(unit, inverse, params[0:1], back[...])
    grad_x[...] = grad_ref[...] + grad_in
    sums[0:1] = gain[None]
    sums[1:2] = shift[None]
    sums[2:8] = jnp.zeros((6, model_width), F32)


def finish(scalars, pieces, x, grad, params, weights):
    rows, model_width = x.shape
    count = len(pieces)
    any_spec = pl.BlockSpec(memory_space=pl.ANY)
    vmem = pl.BlockSpec(memory_space=pltpu.VMEM)
    return pl.pallas_call(
        partial(finish_kernel, count=count),
        in_specs=[pl.BlockSpec(memory_space=pltpu.SMEM)] + [any_spec] * count + [vmem] * 3 + [any_spec],
        out_specs=[vmem] * 2,
        out_shape=[
            jax.ShapeDtypeStruct((rows, model_width), F32),
            jax.ShapeDtypeStruct((8, model_width), F32),
        ],
        scratch_shapes=[
            pltpu.VMEM((rows, 3 * model_width), HALF),
            pltpu.VMEM((model_width, 3 * model_width), HALF),
            pltpu.VMEM((rows, model_width), F32),
            pltpu.SemaphoreType.DMA((6 * count,)),
            pltpu.SemaphoreType.DMA((1,)),
        ],
        compiler_params=pltpu.CompilerParams(vmem_limit_bytes=VMEM_LIMIT),
        cost_estimate=pl.CostEstimate(
            flops=6 * rows * model_width * model_width,
            bytes_accessed=model_width * (6 * model_width + 16 * rows),
            transcendentals=0,
        ),
        name="finish",
    )(scalars, *pieces, x, grad, params, weights)


def col_sums(tensor):
    return jnp.sum(tensor.astype(F32), axis=0)


def shards(
    tokens,
    memory,
    end_only,
    lengths,
    norm_gain,
    norm_bias,
    self_qkv,
    self_out,
    cross_q,
    cross_kv,
    cross_out,
    fc_in,
    fc_out,
    fc_in_bias,
    proj_bias,
    cotangent,
    *,
    n,
    pages,
):
    seqs, rows, model_width = tokens.shape
    mem_count, shard_width = memory.shape[1], memory.shape[2]
    head_dim = model_width // HEADS
    n_heads = HEADS // n
    width = n_heads * head_dim
    flat = seqs * rows
    me = lax.axis_index("blk")
    offset = me * rows
    span = jnp.where(end_only == 1, 1, lengths)
    order = jnp.argsort(-span, stable=True).astype(jnp.int32)
    place = jnp.argsort(order).astype(jnp.int32)
    span = jnp.take(span, order)
    scalars = [jnp.stack([span[s], me, order[s]]).astype(jnp.int32) for s in range(seqs)]
    positions = offset + jnp.arange(rows, dtype=jnp.int32)

    def arranged(tensors, index):
        found = []
        for s in range(seqs):
            item = tensors[0]
            for t in range(1, seqs):
                item = jnp.where(index[s] == t, tensors[t], item)
            found.append(item)
        return found

    row_mask = (positions[None, :] < span[:, None]).astype(F32).reshape(flat, 1)
    q_scale = 0.125 * LOG2E

    ordered = lax.optimization_barrier
    x = arranged(tokens, order)

    whole_memory = lax.all_gather(memory, "blk", axis=2, tiled=True)
    self_norm = jnp.stack([norm_gain[0], norm_bias[0]])
    normed_self, kept = [], []
    for s in range(seqs):
        normed, own, other = project(scalars[s], tokens, self_norm, proj_bias[:2], self_qkv, n, q_scale)
        normed_self.append(normed)
        kept.append(exchange(own, other, n))
    normed_self = jnp.stack(normed_self).reshape(flat, model_width)

    padded = -(-mem_count // 16) * 16
    whole_memory = jnp.stack(arranged(whole_memory, order))
    whole_memory = jnp.pad(whole_memory, ((0, 0), (0, padded - mem_count), (0, 0)))
    whole_memory = whole_memory.reshape(seqs * padded, model_width)
    mem_proj = mxu(whole_memory, cross_kv)
    cross_keys = mem_proj[:, :model_width].astype(HALF).reshape(seqs, padded, model_width)
    cross_values = (mem_proj[:, model_width:] + proj_bias[4]).astype(HALF)
    cross_values = cross_values.reshape(seqs, padded, model_width)

    kept[0], normed_self, cross_keys, cross_values = ordered(
        (kept[0], normed_self, cross_keys, cross_values)
    )
    normed_whole = lax.all_gather(normed_self, "blk", axis=0, tiled=True)
    self_saved, attended = [], []
    for s in range(seqs):
        own, other, kept_out, log_sums = self_forward(scalars[s], kept[s], n_heads, head_dim)
        sibling = cores(other, n)
        if s + 1 < seqs:
            kept[s + 1], log_sums, sibling = ordered((kept[s + 1], log_sums, sibling))
        self_saved.append((kept_out, log_sums))
        attended.append(chips(own, sibling, n))

    mids, crosses, cross_saved, normed_cross = [], [], [], []
    middle_params = jnp.stack([norm_gain[1], norm_bias[1], proj_bias[2], proj_bias[3]])
    for s in range(seqs):
        attended[s], mid, normed, query = middle(
            scalars[s], columns_of(attended[s], me, 1), x[s], middle_params, self_out, cross_q, q_scale
        )
        crossed, log_sums = cross_forward(
            scalars[s], query, cross_keys[s], cross_values[s], mem_count, head_dim
        )
        mids.append(mid)
        normed_cross.append(normed)
        crosses.append(crossed)
        cross_saved.append((query, log_sums))
    crossed = jnp.concatenate(crosses, axis=0)
    stream_mid = jnp.concatenate(mids, axis=0)
    stream_mid, normed_whole = ordered((stream_mid, normed_whole))

    stream_late = stream_mid + mxu(crossed, cross_out) + proj_bias[5]
    unit_mlp, inverse_mlp = normalized(stream_late)
    normed_mlp = (unit_mlp * norm_gain[2] + norm_bias[2]).astype(HALF)
    hidden_pre = mxu(normed_mlp, fc_in) + fc_in_bias
    gate = 0.5 * (1.0 + lax.erf(hidden_pre * (0.5**0.5)))
    hidden_act = (hidden_pre * gate).astype(HALF)
    slope = (gate + hidden_pre * (jnp.exp(-0.5 * hidden_pre * hidden_pre) * 0.3989422804014327)).astype(HALF)
    grad_late = jnp.concatenate(arranged(cotangent, order), axis=0).astype(F32) * row_mask
    grad_mlp = grad_late.astype(HALF)
    out_own, out_other = row_grads(scalars[0], grad_mlp, hidden_act, n)
    grad_pre = (slope.astype(F32) * mxu(grad_mlp, fc_out, NT)).astype(HALF)
    in_own, in_other = weight_grads(scalars[0], [([normed_mlp], [grad_pre])], None, n)
    bits = n.bit_length() - 2
    fold_steps = [fold_chips(b, n, False) for b in reversed(range(bits))]
    other_steps = [fold_chips(b, n, True) for b in range(bits)]
    out_other, in_other = cores(out_other, n), cores(in_other, n)
    grad_fc_bias = col_sums(grad_pre)
    grad_x2, gain_two, shift_two = norm_backward(
        unit_mlp, inverse_mlp, norm_gain[2], mxu(grad_pre, fc_in, NT)
    )
    grad_two = grad_late + grad_x2
    grad_cross = grad_two.astype(HALF)
    grad_crossed = mxu(grad_cross, cross_out, NT).astype(HALF)
    grad_crossed, out_other, in_other = ordered((grad_crossed, out_other, in_other))
    fc_row = Chain(add_half(out_own, out_other), fold_steps)
    fc_col = Chain(add_half(in_own, in_other), other_steps)
    fc = [fc_row, fc_col]
    tick(fc)

    cq_grads, ckv_parts, ones, selfs, self_grads = [], [], [], [], []
    turn_sums = 0.0
    for s in range(seqs):
        part = slice(s * rows, (s + 1) * rows)
        query, log_sums = cross_saved[s]
        grad_cq, grad_ck, grad_cv = cross_backward(
            scalars[s],
            query,
            cross_keys[s],
            cross_values[s],
            grad_crossed[part],
            crosses[s],
            log_sums,
            mem_count,
            head_dim,
        )
        cq_grads.append(grad_cq)
        ckv_parts.append((grad_ck, grad_cv))
        grad_one, half, own, other, sums = turn(
            scalars[s], grad_cq, mids[s], grad_two[part], norm_gain[1:2], cross_q, self_out, n
        )
        if s == 1:
            half = after(fc, half)
            tick(fc)
        ones.append(grad_one)
        selfs.append(half)
        turn_sums = turn_sums + sums
        self_grads.append(exchange(own, other, n))

    bias_cross_v = sum(col_sums(grad_cv) for _, grad_cv in ckv_parts)
    own, other = weight_grads(
        scalars[0],
        [
            (crosses, [grad_cross]),
            (normed_cross, cq_grads),
            (attended, selfs),
            ([whole_memory], ckv_parts),
        ],
        cross_kv,
        n,
    )
    sibling = cores(other, n)
    self_grads[0], sibling = ordered((self_grads[0], sibling))
    self_grads[0] = after(fc, self_grads[0])
    row_sum, col_sum = fc_row.complete()[0], fc_col.complete()[0]
    fc = Chain(
        jnp.concatenate([row_sum.reshape(shard_width, -1), col_sum], axis=1), page_steps(pages)
    )
    group = Chain(add_half(own, sibling), fold_steps)
    tick([fc, group])

    normed_whole = normed_whole.reshape(n, seqs, rows, model_width)
    earlier, received = None, []
    for s in range(seqs):
        kept_out, log_sums = self_saved[s]
        own, other, *columns, qkv_sums = self_backward(
            scalars[s],
            kept[s],
            self_grads[s],
            kept_out,
            log_sums,
            normed_whole,
            s,
            n_heads,
            head_dim,
            earlier,
        )
        earlier = (*columns, qkv_sums)
        sibling = cores(other, n)
        own = after([fc, group], own)
        tick([fc, group])
        if s == 0:
            hidden_act, own = ordered((hidden_act, own))
            stream_out = mxu(hidden_act, fc_out)
            stream_out, sibling = ordered((stream_out, sibling))
            stream_out = after([fc, group], stream_out)
            folded = group.complete()[0]
            memory_columns = folded[:, 5 * model_width : 5 * model_width + seqs * padded]
            group = Chain(folded[:, : 5 * model_width], page_steps(pages))
            tick([fc, group])
            self_grads[1:], stream_out = ordered((self_grads[1:], stream_out))
            received.append(chips(own, sibling, n))

    column_sibling = cores(columns[1], n)
    own, *received[0] = ordered((own, *received[0]))
    outs, finish_sums = [], 0.0
    for s in range(seqs):
        grad_x, sums = finish(
            scalars[s], columns_of(received[s], me, 3), x[s], ones[s], norm_gain[0:1], self_qkv
        )
        outs.append(grad_x)
        finish_sums = finish_sums + sums
        if s + 2 == seqs:
            outs[s], column_sibling, sibling = ordered((outs[s], column_sibling, sibling))
            qkv = jnp.concatenate(
                [piece[u] for piece in chips(columns[0], column_sibling, n) for u in range(2)],
                axis=1,
            )
            received.append(chips(own, sibling, n))
            outs[s] = after([group], outs[s])
            tick([group])
    stream_out = stream_out + stream_late + proj_bias[6]
    result = (stream_out * row_mask).reshape(seqs, rows, model_width).astype(HALF)
    result = jnp.stack(arranged(result, place))
    qkv = Chain(qkv, page_steps(pages))
    grad_tokens = jnp.stack(arranged(outs, place))

    def own_columns(vector):
        return lax.dynamic_update_slice(jnp.zeros((model_width,), F32), vector, (me * width,))

    small = jnp.concatenate(
        [
            jnp.stack(
                [
                    finish_sums[0],
                    turn_sums[0],
                    gain_two,
                    finish_sums[1],
                    turn_sums[1],
                    shift_two,
                    own_columns(qkv_sums[0]),
                    own_columns(qkv_sums[1]),
                    turn_sums[2],
                    turn_sums[3],
                    bias_cross_v,
                    col_sums(grad_cross),
                    col_sums(grad_mlp),
                ]
            ),
            grad_fc_bias.reshape(n, 4, -1).transpose(1, 0, 2).reshape(4, -1),
        ],
        axis=0,
    )
    small = jnp.pad(small, ((0, -small.shape[0] % 8), (0, 0)))
    small = small_sums(small.reshape(-1, n, shard_width).transpose(1, 0, 2), n, pages)

    total_qkv = qkv.complete()
    owners = lax.bitwise_xor(jnp.arange(n, dtype=jnp.int32), me)
    total_qkv = jnp.take(total_qkv.reshape(shard_width, n, 3, width), owners, axis=1)
    total_qkv = total_qkv.transpose(0, 2, 1, 3).reshape(shard_width, 3 * model_width)
    total_fc = fc.complete().astype(F32)
    total_out = total_fc[:, : fc_out.shape[0]].reshape(model_width, -1).T
    total_in = total_fc[:, fc_out.shape[0] :]
    wide = model_width
    group = group.complete().astype(F32)
    grad_memory = memory_columns.astype(F32).T
    grad_memory = grad_memory.reshape(seqs, padded, shard_width)[:, :mem_count]
    grad_memory = jnp.stack(arranged(grad_memory, place))
    return (
        result,
        grad_tokens,
        grad_memory,
        small[0:3],
        small[3:6],
        total_qkv.astype(F32),
        group[:, 2 * wide : 3 * wide],
        group[:, wide : 2 * wide],
        group[:, 3 * wide :],
        group[:, :wide],
        total_in,
        total_out,
        small[13:17].reshape(-1),
        small[6:13],
    )


def solution(mesh):
    rows_spec = P("page", "blk", None)
    return jax.shard_map(
        partial(shards, n=mesh.shape["blk"], pages=mesh.shape["page"]),
        mesh=mesh,
        in_specs=(rows_spec, P("page", None, "blk"), P("page"), P("page"))
        + (P(),) * 11
        + (rows_spec,),
        out_specs=(
            rows_spec,
            rows_spec,
            P("page", None, "blk"),
            P(None, "blk"),
            P(None, "blk"),
            P("blk", None),
            P("blk", None),
            P("blk", None),
            P("blk", None),
            P("blk", None),
            P("blk", None),
            P("blk", None),
            P("blk"),
            P(None, "blk"),
        ),
        check_vma=False,
    )
```

```python
from functools import partial

import jax
import jax.numpy as jnp
from jax import lax
from jax.experimental import pallas as pl
from jax.experimental.pallas import tpu as pltpu
from jax.sharding import PartitionSpec as P

HEADS = 16
EPSILON = 1e-05
NEG_LARGE = -1e30
HALF = jnp.bfloat16
F32 = jnp.float32
LOG2E = 1.4426950408889634
LN2 = 0.6931471805599453
NT = (((1,), (1,)), ((), ()))
NN = (((1,), (0,)), ((), ()))
TN = (((0,), (0,)), ((), ()))
VMEM_LIMIT = 56 * 2**20


def mxu(left_op, right_op, dims=NN):
    return lax.dot_general(left_op, right_op, dims, preferred_element_type=F32)


def head_lanes(width, head, head_dim):
    lane = lax.broadcasted_iota(jnp.int32, (1, width), 1)
    return (lane >= head * head_dim) & (lane < (head + 1) * head_dim)


def one_head(tensor, head, n_heads, head_dim):
    if n_heads == 1:
        return tensor
    return jnp.where(
        head_lanes(tensor.shape[-1], head, head_dim), tensor, jnp.zeros_like(tensor)
    )


def causal(scores, key_start, query_start):
    key_pos = key_start + lax.broadcasted_iota(jnp.int32, scores.shape, 0)
    query_pos = query_start + lax.broadcasted_iota(jnp.int32, scores.shape, 1)
    return jnp.where(key_pos <= query_pos, scores, NEG_LARGE)


def load_pieces(scalars, pieces, whole, sem):
    rows = pieces[0].shape[1]
    copies = []
    for t, piece in enumerate(pieces):
        for u in range(2):
            owner = lax.bitwise_xor(scalars[1], 2 * t + u)
            start = pl.multiple_of(owner * rows, rows)
            copies.append(
                pltpu.make_async_copy(
                    piece.at[u], whole.at[pl.ds(start, rows)], sem.at[2 * t + u]
                )
            )
    for copy in copies:
        copy.start()
    return copies


def store_pieces(scalars, own, other, whole, sem):
    count = own.shape[0]
    rows = whole.shape[0] // (2 * count)
    copies = []
    for t in range(count):
        for u, target in enumerate((own, other)):
            start = pl.multiple_of(lax.bitwise_xor(scalars[1], 2 * t + u) * rows, rows)
            copies.append(
                pltpu.make_async_copy(
                    whole.at[pl.ds(start, rows)], target.at[t, 0:rows], sem.at[2 * t + u]
                )
            )
    for copy in copies:
        copy.start()
    return copies


def load_columns(scalars, pieces, whole, sem, parts):
    if len(pieces[0].shape) == 2:
        copies = [pltpu.make_async_copy(pieces[0], whole, sem.at[0])]
        copies[0].start()
        return copies
    width = pieces[0].shape[2] // parts
    model_width = width * 2 * len(pieces)
    copies = []
    for t, piece in enumerate(pieces):
        for u in range(2):
            owner = lax.bitwise_xor(scalars[1], 2 * t + u)
            for part in range(parts):
                start = pl.multiple_of(part * model_width + owner * width, width)
                copies.append(
                    pltpu.make_async_copy(
                        piece.at[u, 0 : whole.shape[0], part * width : (part + 1) * width],
                        whole.at[:, pl.ds(start, width)],
                        sem.at[(2 * t + u) * parts + part],
                    )
                )
    for copy in copies:
        copy.start()
    return copies


def self_forward_kernel(scalars, *refs, count, n_heads, head_dim, q_block, k_block, stat_block):
    pieces, refs = refs[:count], refs[count:]
    own, other, kept_out, log_sums, whole, values_t, sem = refs
    width = n_heads * head_dim
    index = pl.program_id(0)
    k_blocks = values_t.shape[0]

    @pl.when(index == 0)
    def _():
        for copy in load_pieces(scalars, pieces, whole, sem):
            copy.wait()
        for b in range(k_blocks):
            values_t[b] = whole[b * k_block : (b + 1) * k_block, 2 * width :].T

    start = pl.multiple_of(index * q_block, q_block)
    q_rows = pl.ds(start, q_block)
    live = start < scalars[0]

    @pl.when(jnp.logical_not(live))
    def _():
        kept_out[q_rows, :] = jnp.zeros((q_block, width), HALF)
        log_sums[...] = jnp.zeros_like(log_sums)

    @pl.when(live)
    def _():
        query = whole[q_rows, :width]
        queries = [one_head(query, h, n_heads, head_dim) for h in range(n_heads)]

        def step(key_start, key_count, carry, cols, masked):
            keys = whole[pl.ds(key_start, key_count), width : 2 * width]
            first = key_start // k_block
            out = []
            for h in range(n_heads):
                top, total, acc = carry[h]
                scores = mxu(keys, queries[h][cols], NT)
                if masked:
                    scores = causal(scores, 0, 0)
                new_top = jnp.maximum(top, jnp.max(scores, axis=0, keepdims=True))
                probs = jnp.exp2(scores - new_top)
                scale = jnp.exp2(top - new_top)
                total = total * scale + jnp.sum(probs, axis=0, keepdims=True)
                probs = probs.astype(HALF)
                acc = acc * scale
                for t in range(key_count // k_block):
                    value_t = values_t[first + t][h * head_dim : (h + 1) * head_dim]
                    acc = acc + mxu(value_t, probs[t * k_block : (t + 1) * k_block])
                out.append((new_top, total, acc))
            return tuple(out)

        carry = tuple(
            (
                jnp.full((1, q_block), NEG_LARGE, F32),
                jnp.zeros((1, q_block), F32),
                jnp.zeros((head_dim, q_block), F32),
            )
            for _ in range(n_heads)
        )
        every = slice(0, q_block)
        carry = lax.fori_loop(
            0,
            index,
            lambda kb, c: step(pl.multiple_of(kb * q_block, q_block), q_block, c, every, False),
            carry,
        )
        ratio = q_block // k_block
        parts = []
        for i in range(ratio):
            cols = slice(i * k_block, (i + 1) * k_block)
            part = tuple(tuple(item[:, cols] for item in head) for head in carry)
            for t in range(i + 1):
                key_start = pl.multiple_of(start + t * k_block, k_block)
                part = step(key_start, k_block, part, cols, t == i)
            parts.append(part)
        carry = tuple(
            tuple(
                jnp.concatenate([part[h][item] for part in parts], axis=1) for item in range(3)
            )
            for h in range(n_heads)
        )
        result_t = jnp.concatenate([acc / total for _, total, acc in carry], axis=0)
        kept_out[q_rows, :] = result_t.T.astype(HALF)
        for h, (top, total, _) in enumerate(carry):
            log_sum = top + jnp.log2(total)
            for t in range(q_block // stat_block):
                log_sums[t, h : h + 1, :] = log_sum[:, t * stat_block : (t + 1) * stat_block]

    @pl.when(index == pl.num_programs(0) - 1)
    def _():
        for copy in store_pieces(scalars, own, other, kept_out, sem):
            copy.wait()


def self_forward(scalars, pieces, n_heads, head_dim):
    count, rows = len(pieces), pieces[0].shape[1]
    n = 2 * count
    length, width = n * rows, n_heads * head_dim
    q_block, k_block, stat_block = 1024, 512, 512
    any_spec = pl.BlockSpec(memory_space=pl.ANY)
    return pl.pallas_call(
        partial(
            self_forward_kernel,
            count=count,
            n_heads=n_heads,
            head_dim=head_dim,
            q_block=q_block,
            k_block=k_block,
            stat_block=stat_block,
        ),
        grid_spec=pltpu.PrefetchScalarGridSpec(
            num_scalar_prefetch=1,
            grid=(length // q_block,),
            in_specs=[any_spec] * count,
            out_specs=[any_spec] * 2
            + [
                pl.BlockSpec((length, width), lambda i, s: (0, 0)),
                pl.BlockSpec((q_block // stat_block, n_heads, stat_block), lambda i, s: (i, 0, 0)),
            ],
            scratch_shapes=[
                pltpu.VMEM((length, 3 * width), HALF),
                pltpu.VMEM((length // k_block, width, k_block), HALF),
                pltpu.SemaphoreType.DMA((n,)),
            ],
        ),
        out_shape=[jax.ShapeDtypeStruct((count, rows, width), HALF)] * 2
        + [
            jax.ShapeDtypeStruct((length, width), HALF),
            jax.ShapeDtypeStruct((length // stat_block, n_heads, stat_block), F32),
        ],
        compiler_params=pltpu.CompilerParams(vmem_limit_bytes=VMEM_LIMIT),
        cost_estimate=pl.CostEstimate(
            flops=2 * 2 * length * length * width,
            bytes_accessed=length * width * 10,
            transcendentals=n_heads * length * length // 2,
        ),
        name="self_forward",
    )(scalars, *pieces)


def self_backward_kernel(scalars, *refs, count, n_heads, head_dim, block, last):
    pieces, refs = refs[:count], refs[count:]
    grad_pieces, refs = refs[:count], refs[count:]
    kept_out, log_sums, normed_ref, refs = *refs[:3], refs[3:]
    if last:
        earlier, earlier_sums, refs = refs[0], refs[1], refs[2:]
        own, other, sums, refs = *refs[:3], refs[3:]
        total, columns_own, columns_other, column_sem, refs = *refs[:4], refs[4:]
    else:
        own, other, total, sums, refs = *refs[:4], refs[4:]
    result, whole, grads, query_heads, grad_heads, deltas, query_sums, sem, grad_sem = refs
    width = n_heads * head_dim
    index = pl.program_id(0)
    blocks = query_heads.shape[1]
    model_width = total.shape[1]
    span = scalars[0]

    @pl.when(index == 0)
    def _():
        copies = load_pieces(scalars, pieces, whole, sem)
        copies += load_pieces(scalars, grad_pieces, grads, grad_sem)
        query_sums[...] = jnp.zeros_like(query_sums)
        total[...] = earlier[...] if last else jnp.zeros_like(total)
        sums[...] = earlier_sums[...] if last else jnp.zeros_like(sums)
        for copy in copies:
            copy.wait()

        @pl.loop(0, (span + block - 1) // block)
        def _(b):
            rows = pl.ds(pl.multiple_of(b * block, block), block)
            query, grad = whole[rows, :width], grads[rows, :]
            products = (grad.astype(F32) * kept_out[rows, :].astype(F32)).T
            for h in range(n_heads):
                deltas[b, h : h + 1, :] = jnp.sum(
                    products[h * head_dim : (h + 1) * head_dim], axis=0, keepdims=True
                )
                query_heads[h, b] = one_head(query, h, n_heads, head_dim)
                grad_heads[h, b] = one_head(grad, h, n_heads, head_dim)

    start = pl.multiple_of(index * block, block)
    k_rows = pl.ds(start, block)
    live = start < span

    @pl.when(jnp.logical_not(live))
    def _():
        result[k_rows, :] = jnp.zeros((block, 3 * width), HALF)

    @pl.when(live)
    def _():
        keys = whole[k_rows, width : 2 * width]
        values = whole[k_rows, 2 * width :]
        keys_t = keys.T

        def step(qb, carry, masked):
            grad_keys, grad_values = carry
            for h in range(n_heads):
                query, grad = query_heads[h, qb], grad_heads[h, qb]
                scores = mxu(keys, query, NT)
                if masked:
                    scores = causal(scores, start, qb * block)
                probs = jnp.exp2(scores - log_sums[qb, h : h + 1, :])
                grad_probs = mxu(values, grad, NT)
                grad_scores = (probs * (grad_probs - deltas[qb, h : h + 1, :])).astype(HALF)
                grad_values = grad_values + mxu(probs.astype(HALF), grad)
                grad_keys = grad_keys + mxu(grad_scores, query)
                lanes = slice(h * head_dim, (h + 1) * head_dim)
                query_sums[qb, lanes, :] += mxu(keys_t[lanes], grad_scores)
            return grad_keys, grad_values

        zero = jnp.zeros((block, width), F32)
        carry = step(index, (zero, zero), True)
        live_blocks = (span + block - 1) // block
        grad_keys, grad_values = lax.fori_loop(
            index + 1, live_blocks, lambda qb, c: step(qb, c, False), carry
        )
        query_t = (query_sums[index] * 0.125).astype(HALF)
        grad_queries = query_t.T
        grad_keys = (grad_keys * LN2).astype(HALF)
        grad_values = grad_values.astype(HALF)
        result[k_rows, :width] = grad_queries
        result[k_rows, width : 2 * width] = grad_keys
        result[k_rows, 2 * width :] = grad_values
        sums[0:1] += jnp.sum(grad_queries.astype(F32), axis=0, keepdims=True)
        sums[1:2] += jnp.sum(grad_values.astype(F32), axis=0, keepdims=True)
        normed = normed_ref[...].reshape(block, model_width)
        for part, tensor in enumerate((query_t, grad_keys.T, grad_values.T)):
            total[part * width : (part + 1) * width] += mxu(tensor, normed)

    @pl.when(index == pl.num_programs(0) - 1)
    def _():
        copies = store_pieces(scalars, own, other, result, sem)
        if last:
            shard = columns_own.shape[1]
            chip, core = scalars[1] // 2, lax.bitwise_and(scalars[1], 1)
            for p in range(count):
                tile = total[:, p * 2 * shard : (p + 1) * 2 * shard].T.astype(HALF)
                slot = lax.bitwise_xor(chip, p)
                columns_own[slot], columns_other[slot] = row_split(core, tile, shard)
            rows = own.shape[1] - shard
            for u, (source, target) in enumerate(((columns_own, own), (columns_other, other))):
                copy = pltpu.make_async_copy(
                    source, target.at[:, rows : rows + shard], column_sem.at[u]
                )
                copy.start()
                copies.append(copy)
        for copy in copies:
            copy.wait()


def self_backward(
    scalars, pieces, grad_pieces, kept_out, log_sums, normed, seq, n_heads, head_dim, earlier
):
    count, rows = len(pieces), pieces[0].shape[1]
    n, model_width = 2 * count, normed.shape[3]
    length, width = n * rows, n_heads * head_dim
    block = log_sums.shape[2]
    blocks = length // block
    last = earlier is not None
    any_spec = pl.BlockSpec(memory_space=pl.ANY)
    fixed = lambda shape: pl.BlockSpec(shape, lambda i, s: (0,) * len(shape))
    total, sums = (3 * width, model_width), (8, width)
    packed = (count, model_width // n, 3 * width)
    return pl.pallas_call(
        partial(
            self_backward_kernel,
            count=count,
            n_heads=n_heads,
            head_dim=head_dim,
            block=block,
            last=last,
        ),
        grid_spec=pltpu.PrefetchScalarGridSpec(
            num_scalar_prefetch=1,
            grid=(blocks,),
            in_specs=[any_spec] * (2 * count)
            + [
                fixed((length, width)),
                fixed((blocks, n_heads, block)),
                pl.BlockSpec(
                    (block // rows, 1, rows, model_width), lambda i, s: (i, seq, 0, 0)
                ),
            ]
            + ([fixed(total), fixed(sums)] if last else []),
            out_specs=[any_spec] * 2
            + [fixed(shape) for shape in ((sums,) if last else (total, sums))],
            scratch_shapes=(
                [
                    pltpu.VMEM(total, F32),
                    pltpu.VMEM(packed, HALF),
                    pltpu.VMEM(packed, HALF),
                    pltpu.SemaphoreType.DMA((2,)),
                ]
                if last
                else []
            )
            + [
                pltpu.VMEM((length, 3 * width), HALF),
                pltpu.VMEM((length, 3 * width), HALF),
                pltpu.VMEM((length, width), HALF),
                pltpu.VMEM((n_heads, blocks, block, width), HALF),
                pltpu.VMEM((n_heads, blocks, block, width), HALF),
                pltpu.VMEM((blocks, n_heads, block), F32),
                pltpu.VMEM((blocks, width, block), F32),
                pltpu.SemaphoreType.DMA((n,)),
                pltpu.SemaphoreType.DMA((n,)),
            ],
        ),
        out_shape=[
            jax.ShapeDtypeStruct((count, rows + (packed[1] if last else 0), 3 * width), HALF)
        ]
        * 2
        + ([] if last else [jax.ShapeDtypeStruct(total, F32)])
        + [jax.ShapeDtypeStruct(sums, F32)],
        compiler_params=pltpu.CompilerParams(vmem_limit_bytes=VMEM_LIMIT),
        cost_estimate=pl.CostEstimate(
            flops=5 * 2 * length * length * width // 2,
            bytes_accessed=length * width * 20,
            transcendentals=n_heads * length * length // 2,
        ),
        name="self_backward",
    )(scalars, *pieces, *grad_pieces, kept_out, log_sums, normed, *(earlier or ()))


def cross_scores(keys, query, mem_count):
    scores = mxu(keys, query, NT)
    padded = scores.shape[0]
    if padded == mem_count:
        return scores
    whole = mem_count // 8 * 8
    tail = scores[whole:]
    position = whole + lax.broadcasted_iota(jnp.int32, tail.shape, 0)
    tail = jnp.where(position < mem_count, tail, NEG_LARGE)
    return jnp.concatenate([scores[:whole], tail], axis=0)


def cross_forward_kernel(scalars, query_ref, key_ref, value_ref, out_ref, log_sums, *, mem_count, head_dim):
    rows, width = query_ref.shape
    live = scalars[1] * rows < scalars[0]

    @pl.when(jnp.logical_not(live))
    def _():
        out_ref[...] = jnp.zeros_like(out_ref)
        log_sums[...] = jnp.zeros_like(log_sums)

    @pl.when(live)
    def _():
        n_heads = width // head_dim
        query, keys = query_ref[...], key_ref[...]
        values_t = value_ref[...].T
        results = []
        for h in range(n_heads):
            scores = cross_scores(keys, one_head(query, h, n_heads, head_dim), mem_count)
            top = jnp.max(scores, axis=0, keepdims=True)
            probs = jnp.exp2(scores - top)
            total = jnp.sum(probs, axis=0, keepdims=True)
            lanes = slice(h * head_dim, (h + 1) * head_dim)
            results.append(mxu(values_t[lanes], probs.astype(HALF)) / total)
            log_sums[0, h : h + 1, :] = top + jnp.log2(total)
        out_ref[...] = jnp.concatenate(results, axis=0).T.astype(HALF)


def cross_forward(scalars, query, keys, values, mem_count, head_dim):
    rows, model_width = query.shape
    padded = keys.shape[0]
    width = 128
    groups, n_heads = model_width // width, width // head_dim
    column = lambda count: pl.BlockSpec((count, width), lambda g, s: (0, g))
    return pl.pallas_call(
        partial(cross_forward_kernel, mem_count=mem_count, head_dim=head_dim),
        grid_spec=pltpu.PrefetchScalarGridSpec(
            num_scalar_prefetch=1,
            grid=(groups,),
            in_specs=[column(rows), column(padded), column(padded)],
            out_specs=[column(rows), pl.BlockSpec((1, n_heads, rows), lambda g, s: (g, 0, 0))],
        ),
        out_shape=[
            jax.ShapeDtypeStruct((rows, model_width), HALF),
            jax.ShapeDtypeStruct((groups, n_heads, rows), F32),
        ],
        compiler_params=pltpu.CompilerParams(vmem_limit_bytes=VMEM_LIMIT),
        cost_estimate=pl.CostEstimate(
            flops=4 * 2 * rows * padded * model_width,
            bytes_accessed=(rows + padded) * model_width * 4,
            transcendentals=rows * padded * model_width // head_dim,
        ),
        name="cross_forward",
    )(scalars, query, keys, values)


def cross_backward_kernel(
    scalars,
    query_ref,
    key_ref,
    value_ref,
    grad_ref,
    out_ref,
    log_sums,
    grad_query,
    grad_key,
    grad_value,
    *,
    mem_count,
    head_dim,
):
    rows, width = query_ref.shape
    padded = key_ref.shape[0]
    live = scalars[1] * rows < scalars[0]

    @pl.when(jnp.logical_not(live))
    def _():
        grad_query[...] = jnp.zeros_like(grad_query)
        grad_key[...] = jnp.zeros_like(grad_key)
        grad_value[...] = jnp.zeros_like(grad_value)

    @pl.when(live)
    def _():
        n_heads = width // head_dim
        query_all, keys, values, grad_all = query_ref[...], key_ref[...], value_ref[...], grad_ref[...]
        keys_t = keys.T
        products = (grad_all.astype(F32) * out_ref[...].astype(F32)).T
        query_parts = []
        key_sum = jnp.zeros((padded, width), F32)
        value_sum = jnp.zeros((padded, width), F32)
        for h in range(n_heads):
            lanes = slice(h * head_dim, (h + 1) * head_dim)
            query = one_head(query_all, h, n_heads, head_dim)
            grad = one_head(grad_all, h, n_heads, head_dim)
            delta = jnp.sum(products[lanes], axis=0, keepdims=True)
            scores = cross_scores(keys, query, mem_count)
            probs = jnp.exp2(scores - log_sums[0, h : h + 1, :])
            grad_probs = mxu(values, grad, NT)
            grad_scores = (probs * (grad_probs - delta)).astype(HALF)
            value_sum = value_sum + mxu(probs.astype(HALF), grad)
            key_sum = key_sum + mxu(grad_scores, query)
            query_parts.append(mxu(keys_t[lanes], grad_scores))
        grad_query[...] = (jnp.concatenate(query_parts, axis=0) * 0.125).T.astype(HALF)
        grad_key[...] = (key_sum * LN2).astype(HALF)
        grad_value[...] = value_sum.astype(HALF)


def cross_backward(scalars, query, keys, values, grad, kept_out, log_sums, mem_count, head_dim):
    rows, model_width = query.shape
    padded = keys.shape[0]
    width = 128
    groups, n_heads = model_width // width, width // head_dim
    column = lambda count: pl.BlockSpec((count, width), lambda g, s: (0, g))
    return pl.pallas_call(
        partial(cross_backward_kernel, mem_count=mem_count, head_dim=head_dim),
        grid_spec=pltpu.PrefetchScalarGridSpec(
            num_scalar_prefetch=1,
            grid=(groups,),
            in_specs=[
                column(rows),
                column(padded),
                column(padded),
                column(rows),
                column(rows),
                pl.BlockSpec((1, n_heads, rows), lambda g, s: (g, 0, 0)),
            ],
            out_specs=[column(rows), column(padded), column(padded)],
        ),
        out_shape=[
            jax.ShapeDtypeStruct((rows, model_width), HALF),
            jax.ShapeDtypeStruct((padded, model_width), HALF),
            jax.ShapeDtypeStruct((padded, model_width), HALF),
        ],
        compiler_params=pltpu.CompilerParams(vmem_limit_bytes=VMEM_LIMIT),
        cost_estimate=pl.CostEstimate(
            flops=10 * 2 * rows * padded * model_width,
            bytes_accessed=(rows + padded) * model_width * 10,
            transcendentals=rows * padded * model_width // head_dim,
        ),
        name="cross_backward",
    )(scalars, query, keys, values, grad, kept_out, log_sums)


def exchange(own, other, n):
    return chips(own, cores(other, n), n)


def cores(other, n):
    return lax.ppermute(other, "blk", [(k, k ^ 1) for k in range(n)])


def chips(own, sibling, n):
    received = []
    for t in range(n // 2):
        message = jnp.stack([own[t], sibling[t]])
        if t:
            message = lax.ppermute(message, "blk", [(k, k ^ (2 * t)) for k in range(n)])
        received.append(message)
    return received


def columns_of(pieces, me, parts, rows):
    width = pieces[0].shape[2] // parts
    if width % 128 == 0:
        return pieces
    pieces = [piece[:, :rows] for piece in pieces]
    n = 2 * len(pieces)
    order = lax.bitwise_xor(jnp.arange(n, dtype=jnp.int32), me)
    whole = jnp.concatenate(pieces, axis=0).reshape(n, rows, parts, width)
    whole = jnp.take(whole, order, axis=0)
    return [whole.transpose(1, 2, 0, 3).reshape(rows, parts * n * width)]


class Halve:
    def __init__(self, axis, step, size):
        self.axis, self.step = axis, step
        self.pairs = [(k, k ^ step) for k in range(size)]

    def bit(self):
        return lax.bitwise_and(lax.axis_index(self.axis), self.step) // self.step

    def prepare(self, tensor):
        halves = tensor.reshape((2, -1) + tensor.shape[1:])
        return lax.dynamic_index_in_dim(halves, 1 - self.bit(), 0, keepdims=False), halves

    def complete(self, halves, received):
        own = lax.dynamic_index_in_dim(halves, self.bit(), 0, keepdims=False)
        return (own.astype(F32) + received.astype(F32)).astype(halves.dtype)


class Join(Halve):
    def prepare(self, tensor):
        return tensor, tensor

    def complete(self, tensor, received):
        first = jnp.where(self.bit() == 0, tensor, received)
        second = jnp.where(self.bit() == 0, received, tensor)
        return jnp.concatenate([first, second], axis=0)


class Fold:
    axis = "blk"

    def __init__(self, bit, n, low):
        self.low = low
        self.pairs = [(k, k ^ (2 << bit)) for k in range(n)]

    def part(self, tensors, index):
        half = tensors[0].shape[0] // 2
        shape = ((half, 2) if self.low else (2, half)) + tensors[0].shape[1:]
        found = [
            lax.index_in_dim(item.reshape(shape), index, int(self.low), keepdims=False).astype(F32)
            for item in tensors
        ]
        return sum(found[1:], found[0])

    def prepare(self, tensor):
        tensors = tensor if isinstance(tensor, tuple) else (tensor,)
        return self.part(tensors, 1).astype(HALF), tensors

    def complete(self, tensors, received):
        return (self.part(tensors, 0) + received.astype(F32)).astype(HALF)


def page_steps(pages):
    steps = [1 << b for b in range(pages.bit_length() - 1)]
    return [Halve("page", step, pages) for step in steps] + [
        Join("page", step, pages) for step in reversed(steps)
    ]


class Chain:
    def __init__(self, tensor, steps):
        self.tensor, self.steps = tensor, list(steps)

    def complete(self):
        while self.steps:
            launch([self], ())
        return self.tensor


def launch(chains, value, messages=()):
    chains = [chain for chain in chains if chain.steps]
    steps = [chain.steps.pop(0) for chain in chains]
    ready = [step.prepare(chain.tensor) for step, chain in zip(steps, chains)]
    value, sent, extra = lax.optimization_barrier(
        (value, [send for send, _ in ready], [tensor for tensor, _ in messages])
    )
    for chain, step, send, (_, kept) in zip(chains, steps, sent, ready):
        chain.tensor = step.complete(kept, lax.ppermute(send, step.axis, step.pairs))
    if messages:
        return value, [
            lax.ppermute(tensor, "blk", pairs) if pairs else tensor
            for tensor, (_, pairs) in zip(extra, messages)
        ]
    return value


def after(chains, value):
    value, tensors = lax.optimization_barrier((value, [chain.tensor for chain in chains]))
    for chain, tensor in zip(chains, tensors):
        chain.tensor = tensor
    return value


def chip_messages(own, sibling, n):
    return [
        (jnp.stack([own[t], sibling[t]]), [(k, k ^ (2 * t)) for k in range(n)] if t else None)
        for t in range(n // 2)
    ]


def small_sums(tensor, n, pages):
    me, page = lax.axis_index("blk"), lax.axis_index("page")
    step = n // 2
    while step:
        bit = lax.bitwise_and(me, step) // step
        halves = tensor.reshape((2, -1) + tensor.shape[1:])
        sent = lax.dynamic_index_in_dim(halves, 1 - bit, 0, keepdims=False)
        received = lax.ppermute(sent, "blk", [(k, k ^ step) for k in range(n)])
        tensor = lax.dynamic_index_in_dim(halves, bit, 0, keepdims=False) + received
        step //= 2
    step = 1
    while step < pages:
        tensor = tensor + lax.ppermute(tensor, "page", [(k, k ^ step) for k in range(pages)])
        step *= 2
    return tensor[0]


def normalized(vector):
    centre = vector - jnp.mean(vector, axis=-1, keepdims=True)
    spread = jnp.mean(centre * centre, axis=-1, keepdims=True)
    inverse = lax.rsqrt(spread + EPSILON)
    return centre * inverse, inverse


def norm_backward(unit, inverse, gain, grad):
    scaled = grad * gain
    first = jnp.mean(scaled, axis=-1, keepdims=True)
    second = jnp.mean(scaled * unit, axis=-1, keepdims=True)
    grad_in = inverse * (scaled - first - unit * second)
    return grad_in, jnp.sum(grad * unit, axis=0), jnp.sum(grad, axis=0)


def by_parity(core, tensor, width):
    even, odd = tensor[:, :width], tensor[:, width:]
    return jnp.where(core == 0, even, odd), jnp.where(core == 0, odd, even)


def row_split(core, tensor, width):
    even, odd = tensor[:width], tensor[width:]
    return jnp.where(core == 0, even, odd), jnp.where(core == 0, odd, even)


GROUP_TILE = 512


def placed(parts):
    found, row = [], 0
    for part in parts:
        column = 0
        for array in part if isinstance(part, tuple) else (part,):
            found.append((array, row, column))
            column += array.shape[1]
        row += array.shape[0]
    return found, row, column


def weights_kernel(scalars, *refs, phases, places):
    hbm = []
    for spots in places:
        hbm.append(refs[: len(spots)])
        refs = refs[len(spots) :]
    own, other, refs = refs[0], refs[1], refs[2:]
    held, turned, sems = refs[: len(places)], refs[len(places)], refs[len(places) + 1 :]
    step = pl.program_id(0)
    count, width, _ = own.shape
    chip, core = scalars[1] // 2, lax.bitwise_and(scalars[1], 1)

    def copies(k):
        found = []
        for i, (row, column) in enumerate(places[k]):
            source = hbm[k][i]
            rows, columns = source.shape
            target = held[k].at[row : row + rows, column : column + columns]
            found.append(pltpu.make_async_copy(source, target, sems[k].at[i]))
        return found

    @pl.when(step == 0)
    def _():
        for k in range(len(places)):
            for copy in copies(k):
                copy.start()
        for k, spots in enumerate(places):
            filled = max(row + source.shape[0] for (row, _), source in zip(spots, hbm[k]))
            if filled < held[k].shape[0]:
                held[k][filled:, :] = jnp.zeros((held[k].shape[0] - filled, held[k].shape[1]), HALF)

    for k, (depth, first, tiles) in enumerate(phases):
        left, right = held[2 * k], held[2 * k + 1 if depth else 2 * k - 1]

        @pl.when(step == first)
        def _(k=k, depth=depth, left=left):
            for copy in copies(2 * k) + (copies(2 * k + 1) if depth else []):
                copy.wait()
            if depth:
                turned[:, :depth] = left[...].T

        @pl.when((step >= first) & (step < first + tiles))
        def _(depth=depth, first=first, left=left, right=right):
            at = pl.multiple_of((step - first) * GROUP_TILE, GROUP_TILE)
            for p in range(count):
                rows = slice(p * 2 * width, (p + 1) * 2 * width)
                if depth:
                    tile = mxu(turned[rows, :depth], right[:depth, pl.ds(at, GROUP_TILE)])
                else:
                    tile = mxu(left[rows, :], right[pl.ds(at, GROUP_TILE), :], NT)
                slot = lax.bitwise_xor(chip, p)
                own[slot], other[slot] = row_split(core, tile.astype(HALF), width)


def weight_grads(scalars, pairs, memory_weights, n):
    operands, places, buffers, phases = [], [], [], []

    def hold(parts, multiple):
        spots, rows, columns = placed(parts)
        operands.extend(array for array, _, _ in spots)
        places.append([(row, column) for _, row, column in spots])
        rows = -(-rows // multiple) * multiple
        buffers.append(pltpu.VMEM((rows, columns), HALF))
        return rows, columns

    first = 0
    for left, right in pairs:
        depth, model_width = hold(left, 128)
        rows, columns = hold(right, GROUP_TILE)
        phases.append((depth, first, columns // GROUP_TILE))
        first += phases[-1][2]
    if memory_weights is not None:
        hold([memory_weights], 128)
        phases.append((0, first, rows // GROUP_TILE))
        first += phases[-1][2]
    depth = max(phase[0] for phase in phases)
    count, width = n // 2, model_width // n
    block = pl.BlockSpec((count, width, GROUP_TILE), lambda j, s: (0, 0, j))
    shape = jax.ShapeDtypeStruct((count, width, first * GROUP_TILE), HALF)
    return pl.pallas_call(
        partial(weights_kernel, phases=phases, places=places),
        grid_spec=pltpu.PrefetchScalarGridSpec(
            num_scalar_prefetch=1,
            grid=(first,),
            in_specs=[pl.BlockSpec(memory_space=pl.ANY)] * len(operands),
            out_specs=[block, block],
            scratch_shapes=buffers
            + [pltpu.VMEM((model_width, depth), HALF)]
            + [pltpu.SemaphoreType.DMA((len(spots),)) for spots in places],
        ),
        out_shape=[shape, shape],
        compiler_params=pltpu.CompilerParams(vmem_limit_bytes=VMEM_LIMIT),
        cost_estimate=pl.CostEstimate(
            flops=2 * model_width * depth * first * GROUP_TILE,
            bytes_accessed=2 * model_width * (2 * depth + first * GROUP_TILE),
            transcendentals=0,
        ),
        name="weight_grads",
    )(scalars, *operands)


def rows_kernel(scalars, left_ref, right_ref, own, other, turned):
    @pl.when(pl.program_id(0) == 0)
    def _():
        turned[...] = left_ref[...].T

    core = lax.bitwise_and(scalars[1], 1)
    width, shard = right_ref.shape[1] // 2, own.shape[1]
    left = turned[...]
    even = mxu(left, right_ref[:, :width]).astype(HALF)
    odd = mxu(left, right_ref[:, width:]).astype(HALF)
    mine, theirs = jnp.where(core == 0, even, odd), jnp.where(core == 0, odd, even)
    for q in range(left.shape[0] // shard):
        rows, cols = slice(q * shard, (q + 1) * shard), slice(q * width, (q + 1) * width)
        own[0, :, cols], other[0, :, cols] = mine[rows], theirs[rows]


def row_grads(scalars, left, right, n):
    rows, model_width = left.shape
    count, width = n // 2, right.shape[1] // n
    block = pl.BlockSpec(
        (1, model_width // n, n * width), lambda p, s: (lax.bitwise_xor(p, s[1] // 2), 0, 0)
    )
    shape = jax.ShapeDtypeStruct((count, model_width // n, n * width), HALF)
    return pl.pallas_call(
        rows_kernel,
        grid_spec=pltpu.PrefetchScalarGridSpec(
            num_scalar_prefetch=1,
            grid=(count,),
            in_specs=[
                pl.BlockSpec((rows, model_width), lambda p, s: (0, 0)),
                pl.BlockSpec((rows, 2 * width), lambda p, s: (0, p)),
            ],
            out_specs=[block, block],
            scratch_shapes=[pltpu.VMEM((model_width, rows), HALF)],
        ),
        out_shape=[shape, shape],
        compiler_params=pltpu.CompilerParams(vmem_limit_bytes=VMEM_LIMIT),
        cost_estimate=pl.CostEstimate(
            flops=2 * rows * model_width * right.shape[1],
            bytes_accessed=2 * (rows + model_width) * right.shape[1],
            transcendentals=0,
        ),
        name="row_grads",
    )(scalars, left, right)


def project_kernel(scalars, x_ref, norm_ref, bias_ref, q_ref, k_ref, v_ref, normed_ref, own, other, *, q_scale):
    width = own.shape[2] // 3
    core = lax.bitwise_and(scalars[1], 1)

    @pl.when(pl.program_id(0) == 0)
    def _():
        unit, _ = normalized(x_ref[0].astype(F32))
        normed_ref[...] = (unit * norm_ref[0:1] + norm_ref[1:2]).astype(HALF)

    normed = normed_ref[...]
    query = ((mxu(normed, q_ref[...]) + bias_ref[0:1]) * q_scale).astype(HALF)
    keys = mxu(normed, k_ref[...]).astype(HALF)
    values = (mxu(normed, v_ref[...]) + bias_ref[1:2]).astype(HALF)
    for part, tensor in enumerate((query, keys, values)):
        lanes = slice(part * width, (part + 1) * width)
        own[0, :, lanes], other[0, :, lanes] = by_parity(core, tensor, width)


def project(scalars, x, norm, bias, weights, n, q_scale):
    rows, model_width = x.shape[1:]
    count, width = n // 2, model_width // n
    fixed = lambda shape: pl.BlockSpec(shape, lambda p, s: (0, 0))
    column = lambda part: pl.BlockSpec(
        (model_width, 2 * width), lambda p, s, part=part: (0, part * count + p)
    )
    packed = pl.BlockSpec(
        (1, rows, 3 * width), lambda p, s: (lax.bitwise_xor(p, s[1] // 2), 0, 0)
    )
    return pl.pallas_call(
        partial(project_kernel, q_scale=q_scale),
        grid_spec=pltpu.PrefetchScalarGridSpec(
            num_scalar_prefetch=1,
            grid=(count,),
            in_specs=[
                pl.BlockSpec((1, rows, model_width), lambda p, s: (s[2], 0, 0)),
                fixed((2, model_width)),
                pl.BlockSpec((2, 2 * width), lambda p, s: (0, p)),
                column(0),
                column(1),
                column(2),
            ],
            out_specs=[fixed((rows, model_width)), packed, packed],
        ),
        out_shape=[jax.ShapeDtypeStruct((rows, model_width), HALF)]
        + [jax.ShapeDtypeStruct((count, rows, 3 * width), HALF)] * 2,
        compiler_params=pltpu.CompilerParams(vmem_limit_bytes=VMEM_LIMIT),
        cost_estimate=pl.CostEstimate(
            flops=2 * rows * model_width * 3 * model_width,
            bytes_accessed=model_width * (6 * model_width + 8 * rows),
            transcendentals=0,
        ),
        name="project",
    )(scalars, x, norm, bias, weights, weights, weights)


TILE = 256


def middle_kernel(scalars, *refs, count, q_scale):
    pieces, refs = refs[:count], refs[count:]
    x_ref, params, out_hbm, query_hbm, attended, mid_ref, normed_ref, query_ref = refs[:8]
    out_weights, query_weights, sem, weight_sem = refs[8:]
    copies = load_columns(scalars, pieces, attended, sem, 1)
    first = pltpu.make_async_copy(out_hbm, out_weights, weight_sem.at[0])
    second = pltpu.make_async_copy(query_hbm, query_weights, weight_sem.at[1])
    first.start()
    second.start()
    for copy in copies:
        copy.wait()
    first.wait()
    left = attended[...]
    model_width = left.shape[1]
    for j in range(model_width // TILE):
        cols = slice(j * TILE, (j + 1) * TILE)
        mid_ref[:, cols] = (
            x_ref[:, cols].astype(F32) + mxu(left, out_weights[:, cols]) + params[2:3, cols]
        )
    unit, _ = normalized(mid_ref[...])
    normed_ref[...] = (unit * params[0:1] + params[1:2]).astype(HALF)
    second.wait()
    left = normed_ref[...]
    for j in range(model_width // TILE):
        cols = slice(j * TILE, (j + 1) * TILE)
        query_ref[:, cols] = (
            (mxu(left, query_weights[:, cols]) + params[3:4, cols]) * q_scale
        ).astype(HALF)


def middle(scalars, pieces, x, params, out_weights, query_weights, q_scale):
    rows, model_width = x.shape
    count = len(pieces)
    any_spec = pl.BlockSpec(memory_space=pl.ANY)
    vmem = pl.BlockSpec(memory_space=pltpu.VMEM)
    return pl.pallas_call(
        partial(middle_kernel, count=count, q_scale=q_scale),
        in_specs=[pl.BlockSpec(memory_space=pltpu.SMEM)] + [any_spec] * count + [vmem, vmem, any_spec, any_spec],
        out_specs=[vmem] * 4,
        out_shape=[
            jax.ShapeDtypeStruct((rows, model_width), HALF),
            jax.ShapeDtypeStruct((rows, model_width), F32),
            jax.ShapeDtypeStruct((rows, model_width), HALF),
            jax.ShapeDtypeStruct((rows, model_width), HALF),
        ],
        scratch_shapes=[
            pltpu.VMEM((model_width, model_width), HALF),
            pltpu.VMEM((model_width, model_width), HALF),
            pltpu.SemaphoreType.DMA((2 * count,)),
            pltpu.SemaphoreType.DMA((2,)),
        ],
        compiler_params=pltpu.CompilerParams(vmem_limit_bytes=VMEM_LIMIT),
        cost_estimate=pl.CostEstimate(
            flops=4 * rows * model_width * model_width,
            bytes_accessed=model_width * (4 * model_width + 12 * rows),
            transcendentals=0,
        ),
        name="middle",
    )(scalars, *pieces, x, params, out_weights, query_weights)


def turn_kernel(
    scalars, grad_query, mid_ref, grad_ref, params, query_hbm, out_hbm,
    grad_mid, half_ref, own, other, sums,
    query_weights, out_weights, back, weight_sem,
):
    first = pltpu.make_async_copy(query_hbm, query_weights, weight_sem.at[0])
    second = pltpu.make_async_copy(out_hbm, out_weights, weight_sem.at[1])
    first.start()
    second.start()
    count, _, width = own.shape
    chip, core = scalars[1] // 2, lax.bitwise_and(scalars[1], 1)
    unit, inverse = normalized(mid_ref[...])
    first.wait()
    left = grad_query[...]
    model_width = left.shape[1]
    for j in range(model_width // TILE):
        cols = slice(j * TILE, (j + 1) * TILE)
        back[:, cols] = mxu(left, query_weights[cols, :], NT)
    grad_in, gain, shift = norm_backward(unit, inverse, params[0:1], back[...])
    total = grad_ref[...] + grad_in
    grad_mid[...] = total
    half = total.astype(HALF)
    half_ref[...] = half
    sums[0:1] = gain[None]
    sums[1:2] = shift[None]
    sums[2:3] = jnp.sum(half.astype(F32), axis=0, keepdims=True)
    sums[3:4] = jnp.sum(left.astype(F32), axis=0, keepdims=True)
    sums[4:8] = jnp.zeros((4, model_width), F32)
    second.wait()
    for p in range(count):
        tile = mxu(half, out_weights[p * 2 * width : (p + 1) * 2 * width, :], NT).astype(HALF)
        slot = lax.bitwise_xor(chip, p)
        own[slot], other[slot] = by_parity(core, tile, width)


def turn(scalars, grad_query, mid, grad, params, query_weights, out_weights, n):
    rows, model_width = mid.shape
    count, width = n // 2, model_width // n
    any_spec = pl.BlockSpec(memory_space=pl.ANY)
    vmem = pl.BlockSpec(memory_space=pltpu.VMEM)
    return pl.pallas_call(
        turn_kernel,
        in_specs=[pl.BlockSpec(memory_space=pltpu.SMEM)] + [vmem] * 4 + [any_spec] * 2,
        out_specs=[vmem] * 5,
        out_shape=[
            jax.ShapeDtypeStruct((rows, model_width), F32),
            jax.ShapeDtypeStruct((rows, model_width), HALF),
            jax.ShapeDtypeStruct((count, rows, width), HALF),
            jax.ShapeDtypeStruct((count, rows, width), HALF),
            jax.ShapeDtypeStruct((8, model_width), F32),
        ],
        scratch_shapes=[
            pltpu.VMEM((model_width, model_width), HALF),
            pltpu.VMEM((model_width, model_width), HALF),
            pltpu.VMEM((rows, model_width), F32),
            pltpu.SemaphoreType.DMA((2,)),
        ],
        compiler_params=pltpu.CompilerParams(vmem_limit_bytes=VMEM_LIMIT),
        cost_estimate=pl.CostEstimate(
            flops=4 * rows * model_width * model_width,
            bytes_accessed=model_width * (4 * model_width + 20 * rows),
            transcendentals=0,
        ),
        name="turn",
    )(scalars, grad_query, mid, grad, params, query_weights, out_weights)


def finish_kernel(scalars, *refs, count):
    pieces, refs = refs[:count], refs[count:]
    x_ref, grad_ref, params, weights_hbm, grad_x, sums = refs[:6]
    grads, weights, back, sem, weight_sem = refs[6:]
    copies = load_columns(scalars, pieces, grads, sem, 3)
    fetch = pltpu.make_async_copy(weights_hbm, weights, weight_sem.at[0])
    fetch.start()
    unit, inverse = normalized(x_ref[...].astype(F32))
    for copy in copies:
        copy.wait()
    fetch.wait()
    left = grads[...]
    model_width = back.shape[1]
    for j in range(model_width // TILE):
        cols = slice(j * TILE, (j + 1) * TILE)
        back[:, cols] = mxu(left, weights[cols, :], NT)
    grad_in, gain, shift = norm_backward(unit, inverse, params[0:1], back[...])
    grad_x[...] = grad_ref[...] + grad_in
    sums[0:1] = gain[None]
    sums[1:2] = shift[None]
    sums[2:8] = jnp.zeros((6, model_width), F32)


def finish(scalars, pieces, x, grad, params, weights):
    rows, model_width = x.shape
    count = len(pieces)
    any_spec = pl.BlockSpec(memory_space=pl.ANY)
    vmem = pl.BlockSpec(memory_space=pltpu.VMEM)
    return pl.pallas_call(
        partial(finish_kernel, count=count),
        in_specs=[pl.BlockSpec(memory_space=pltpu.SMEM)] + [any_spec] * count + [vmem] * 3 + [any_spec],
        out_specs=[vmem] * 2,
        out_shape=[
            jax.ShapeDtypeStruct((rows, model_width), F32),
            jax.ShapeDtypeStruct((8, model_width), F32),
        ],
        scratch_shapes=[
            pltpu.VMEM((rows, 3 * model_width), HALF),
            pltpu.VMEM((model_width, 3 * model_width), HALF),
            pltpu.VMEM((rows, model_width), F32),
            pltpu.SemaphoreType.DMA((6 * count,)),
            pltpu.SemaphoreType.DMA((1,)),
        ],
        compiler_params=pltpu.CompilerParams(vmem_limit_bytes=VMEM_LIMIT),
        cost_estimate=pl.CostEstimate(
            flops=6 * rows * model_width * model_width,
            bytes_accessed=model_width * (6 * model_width + 16 * rows),
            transcendentals=0,
        ),
        name="finish",
    )(scalars, *pieces, x, grad, params, weights)


def col_sums(tensor):
    return jnp.sum(tensor.astype(F32), axis=0)


def shards(
    tokens,
    memory,
    end_only,
    lengths,
    norm_gain,
    norm_bias,
    self_qkv,
    self_out,
    cross_q,
    cross_kv,
    cross_out,
    fc_in,
    fc_out,
    fc_in_bias,
    proj_bias,
    cotangent,
    *,
    n,
    pages,
):
    seqs, rows, model_width = tokens.shape
    mem_count, shard_width = memory.shape[1], memory.shape[2]
    head_dim = model_width // HEADS
    n_heads = HEADS // n
    width = n_heads * head_dim
    flat = seqs * rows
    me = lax.axis_index("blk")
    offset = me * rows
    span = jnp.where(end_only == 1, 1, lengths)
    order = jnp.argsort(-span, stable=True).astype(jnp.int32)
    place = jnp.argsort(order).astype(jnp.int32)
    span = jnp.take(span, order)
    scalars = [jnp.stack([span[s], me, order[s]]).astype(jnp.int32) for s in range(seqs)]
    positions = offset + jnp.arange(rows, dtype=jnp.int32)

    def arranged(tensors, index):
        found = []
        for s in range(seqs):
            item = tensors[0]
            for t in range(1, seqs):
                item = jnp.where(index[s] == t, tensors[t], item)
            found.append(item)
        return found

    row_mask = (positions[None, :] < span[:, None]).astype(F32).reshape(flat, 1)
    q_scale = 0.125 * LOG2E

    ordered = lax.optimization_barrier
    x = arranged(tokens, order)

    whole_memory = lax.all_gather(memory, "blk", axis=2, tiled=True)
    self_norm = jnp.stack([norm_gain[0], norm_bias[0]])
    normed_self, kept = [], []
    for s in range(seqs):
        normed, own, other = project(scalars[s], tokens, self_norm, proj_bias[:2], self_qkv, n, q_scale)
        normed_self.append(normed)
        kept.append(exchange(own, other, n))
    normed_self = jnp.stack(normed_self).reshape(flat, model_width)

    padded = -(-mem_count // 16) * 16
    whole_memory = jnp.stack(arranged(whole_memory, order))
    whole_memory = jnp.pad(whole_memory, ((0, 0), (0, padded - mem_count), (0, 0)))
    whole_memory = whole_memory.reshape(seqs * padded, model_width)
    mem_proj = mxu(whole_memory, cross_kv)
    cross_keys = mem_proj[:, :model_width].astype(HALF).reshape(seqs, padded, model_width)
    cross_values = (mem_proj[:, model_width:] + proj_bias[4]).astype(HALF)
    cross_values = cross_values.reshape(seqs, padded, model_width)

    kept[0], normed_self, cross_keys, cross_values = ordered(
        (kept[0], normed_self, cross_keys, cross_values)
    )
    normed_whole = lax.all_gather(normed_self, "blk", axis=0, tiled=True)
    self_saved, attended = [], []
    for s in range(seqs):
        own, other, kept_out, log_sums = self_forward(scalars[s], kept[s], n_heads, head_dim)
        sibling = cores(other, n)
        if s + 1 < seqs:
            kept[s + 1], log_sums, sibling = ordered((kept[s + 1], log_sums, sibling))
        self_saved.append((kept_out, log_sums))
        attended.append(chips(own, sibling, n))

    mids, crosses, cross_saved, normed_cross = [], [], [], []
    middle_params = jnp.stack([norm_gain[1], norm_bias[1], proj_bias[2], proj_bias[3]])
    for s in range(seqs):
        attended[s], mid, normed, query = middle(
            scalars[s], columns_of(attended[s], me, 1, rows), x[s], middle_params, self_out, cross_q, q_scale
        )
        crossed, log_sums = cross_forward(
            scalars[s], query, cross_keys[s], cross_values[s], mem_count, head_dim
        )
        mids.append(mid)
        normed_cross.append(normed)
        crosses.append(crossed)
        cross_saved.append((query, log_sums))
    crossed = jnp.concatenate(crosses, axis=0)
    stream_mid = jnp.concatenate(mids, axis=0)
    stream_mid, normed_whole = ordered((stream_mid, normed_whole))

    stream_late = stream_mid + mxu(crossed, cross_out) + proj_bias[5]
    unit_mlp, inverse_mlp = normalized(stream_late)
    normed_mlp = (unit_mlp * norm_gain[2] + norm_bias[2]).astype(HALF)
    hidden_pre = mxu(normed_mlp, fc_in) + fc_in_bias
    gate = 0.5 * (1.0 + lax.erf(hidden_pre * (0.5**0.5)))
    hidden_act = (hidden_pre * gate).astype(HALF)
    slope = (gate + hidden_pre * (jnp.exp(-0.5 * hidden_pre * hidden_pre) * 0.3989422804014327)).astype(HALF)
    grad_late = jnp.concatenate(arranged(cotangent, order), axis=0).astype(F32) * row_mask
    grad_mlp = grad_late.astype(HALF)
    out_own, out_other = row_grads(scalars[0], grad_mlp, hidden_act, n)
    grad_pre = (slope.astype(F32) * mxu(grad_mlp, fc_out, NT)).astype(HALF)
    grad_fc_bias = col_sums(grad_pre)
    grad_x2, gain_two, shift_two = norm_backward(
        unit_mlp, inverse_mlp, norm_gain[2], mxu(grad_pre, fc_in, NT)
    )
    grad_two = grad_late + grad_x2
    grad_cross = grad_two.astype(HALF)
    in_own, in_other = weight_grads(
        scalars[0], [([normed_mlp], [grad_pre]), (crosses, [grad_cross])], None, n
    )
    bits = n.bit_length() - 2
    fold_steps = [Fold(b, n, False) for b in reversed(range(bits))]
    other_steps = [Fold(b, n, True) for b in range(bits)]
    out_other, in_other = cores(out_other, n), cores(in_other, n)
    grad_crossed = mxu(grad_cross, cross_out, NT).astype(HALF)
    grad_crossed, out_other, in_other = ordered((grad_crossed, out_other, in_other))
    fc_row = Chain((out_own, out_other), fold_steps)
    fc_col = Chain((in_own, in_other), other_steps)
    fc = [fc_row, fc_col]
    grad_crossed = launch(fc, grad_crossed)

    cq_grads, ckv_parts, ones, selfs, self_grads = [], [], [], [], []
    turn_sums = 0.0
    for s in range(seqs):
        part = slice(s * rows, (s + 1) * rows)
        query, log_sums = cross_saved[s]
        grad_cq, grad_ck, grad_cv = cross_backward(
            scalars[s],
            query,
            cross_keys[s],
            cross_values[s],
            grad_crossed[part],
            crosses[s],
            log_sums,
            mem_count,
            head_dim,
        )
        cq_grads.append(grad_cq)
        ckv_parts.append((grad_ck, grad_cv))
        grad_one, half, own, other, sums = turn(
            scalars[s], grad_cq, mids[s], grad_two[part], norm_gain[1:2], cross_q, self_out, n
        )
        if s == 1:
            half = after(fc, half)
            grad_cross = launch(fc, grad_cross)
        ones.append(grad_one)
        selfs.append(half)
        turn_sums = turn_sums + sums
        self_grads.append(exchange(own, other, n))

    bias_cross_v = sum(col_sums(grad_cv) for _, grad_cv in ckv_parts)
    own, other = weight_grads(
        scalars[0],
        [
            (normed_cross, cq_grads),
            (attended, selfs),
            ([whole_memory], ckv_parts),
        ],
        cross_kv,
        n,
    )
    own = after(fc, own)
    row_sum, col_sum = fc_row.complete()[0], fc_col.complete()[0]
    fc = Chain(jnp.concatenate([row_sum, col_sum], axis=1), page_steps(pages))
    hidden_act, own, other = ordered((hidden_act, own, other))
    hidden_act = launch([fc], hidden_act)
    sibling = cores(other, n)
    stream_out = mxu(hidden_act, fc_out)
    stream_out, sibling = after([fc], (stream_out, sibling))
    self_grads[0], stream_out = ordered((self_grads[0], stream_out))
    group = Chain((own, sibling), fold_steps)
    self_grads[0] = launch([fc, group], self_grads[0])

    normed_whole = normed_whole.reshape(n, seqs, rows, model_width)
    earlier, received = None, []
    for s in range(seqs):
        kept_out, log_sums = self_saved[s]
        own, other, *columns = self_backward(
            scalars[s],
            kept[s],
            self_grads[s],
            kept_out,
            log_sums,
            normed_whole,
            s,
            n_heads,
            head_dim,
            earlier,
        )
        earlier, qkv_sums = columns, columns[-1]
        own, other = after([fc, group], (own, other))
        if s + 1 == seqs:
            folded = group.complete()[0]
            memory_columns = folded[:, 4 * model_width : 4 * model_width + seqs * padded]
            group = Chain(folded[:, : 4 * model_width], page_steps(pages))
            other = launch([fc, group], other)
            sibling = cores(other, n)
            received[0], sibling = after([group], (received[0], sibling))
            messages = chip_messages(own, sibling, n)
            received[0], pieces = launch([group], received[0], messages)
        else:
            messages = chip_messages(own, cores(other, n), n)
            self_grads[s + 1], pieces = launch([fc, group], self_grads[s + 1], messages)
        received.append(pieces)

    outs, finish_sums = [], 0.0
    for s in range(seqs):
        grad_x, sums = finish(
            scalars[s], columns_of(received[s], me, 3, rows), x[s], ones[s], norm_gain[0:1], self_qkv
        )
        if s + 2 == seqs:
            grad_x = after([group], grad_x)
            grad_x = launch([group], grad_x)
            grad_x, received[s + 1] = after([group], (grad_x, received[s + 1]))
            qkv = [piece[u, rows:] for piece in received[s + 1] for u in range(2)]
            qkv = Chain(jnp.concatenate(qkv, axis=1), page_steps(pages))
            ones[s + 1] = launch([qkv, group], ones[s + 1])
        outs.append(grad_x)
        finish_sums = finish_sums + sums
    stream_out = stream_out + stream_late + proj_bias[6]
    result = (stream_out * row_mask).reshape(seqs, rows, model_width).astype(HALF)
    result = jnp.stack(arranged(result, place))
    grad_tokens = jnp.stack(arranged(outs, place))

    def own_columns(vector):
        return lax.dynamic_update_slice(jnp.zeros((model_width,), F32), vector, (me * width,))

    small = jnp.concatenate(
        [
            jnp.stack(
                [
                    finish_sums[0],
                    turn_sums[0],
                    gain_two,
                    finish_sums[1],
                    turn_sums[1],
                    shift_two,
                    own_columns(qkv_sums[0]),
                    own_columns(qkv_sums[1]),
                    turn_sums[2],
                    turn_sums[3],
                    bias_cross_v,
                    col_sums(grad_cross),
                    col_sums(grad_mlp),
                ]
            ),
            grad_fc_bias.reshape(n, 4, -1).transpose(1, 0, 2).reshape(4, -1),
        ],
        axis=0,
    )
    small = jnp.pad(small, ((0, -small.shape[0] % 8), (0, 0)))
    small = small_sums(small.reshape(-1, n, shard_width).transpose(1, 0, 2), n, pages)

    total_qkv = qkv.complete()
    owners = lax.bitwise_xor(jnp.arange(n, dtype=jnp.int32), me)
    total_qkv = jnp.take(total_qkv.reshape(shard_width, n, 3, width), owners, axis=1)
    total_qkv = total_qkv.transpose(0, 2, 1, 3).reshape(shard_width, 3 * model_width)
    total_fc = fc.complete().astype(F32)
    total_out = total_fc[:, : fc_out.shape[0]].reshape(shard_width, n, -1).transpose(2, 1, 0)
    total_out = total_out.reshape(-1, model_width)
    total_in = total_fc[:, fc_out.shape[0] : 2 * fc_out.shape[0]]
    wide = model_width
    group = group.complete().astype(F32)
    grad_memory = memory_columns.astype(F32).T
    grad_memory = grad_memory.reshape(seqs, padded, shard_width)[:, :mem_count]
    grad_memory = jnp.stack(arranged(grad_memory, place))
    return (
        result,
        grad_tokens,
        grad_memory,
        small[0:3],
        small[3:6],
        total_qkv.astype(F32),
        group[:, wide : 2 * wide],
        group[:, :wide],
        group[:, 2 * wide :],
        total_fc[:, 2 * fc_out.shape[0] :],
        total_in,
        total_out,
        small[13:17].reshape(-1),
        small[6:13],
    )


def solution(mesh):
    rows_spec = P("page", "blk", None)
    return jax.shard_map(
        partial(shards, n=mesh.shape["blk"], pages=mesh.shape["page"]),
        mesh=mesh,
        in_specs=(rows_spec, P("page", None, "blk"), P("page"), P("page"))
        + (P(),) * 11
        + (rows_spec,),
        out_specs=(
            rows_spec,
            rows_spec,
            P("page", None, "blk"),
            P(None, "blk"),
            P(None, "blk"),
            P("blk", None),
            P("blk", None),
            P("blk", None),
            P("blk", None),
            P("blk", None),
            P("blk", None),
            P("blk", None),
            P("blk"),
            P(None, "blk"),
        ),
        check_vma=False,
    )
```

```python
from functools import partial

import jax
import jax.numpy as jnp
from jax import lax
from jax.experimental import pallas as pl
from jax.experimental.pallas import tpu as pltpu
from jax.sharding import PartitionSpec as P

HEADS = 16
EPSILON = 1e-05
NEG_LARGE = -1e30
HALF = jnp.bfloat16
F32 = jnp.float32
LOG2E = 1.4426950408889634
LN2 = 0.6931471805599453
NT = (((1,), (1,)), ((), ()))
NN = (((1,), (0,)), ((), ()))
TN = (((0,), (0,)), ((), ()))
VMEM_LIMIT = 56 * 2**20


def mxu(left_op, right_op, dims=NN):
    return lax.dot_general(left_op, right_op, dims, preferred_element_type=F32)


def head_lanes(width, head, head_dim):
    lane = lax.broadcasted_iota(jnp.int32, (1, width), 1)
    return (lane >= head * head_dim) & (lane < (head + 1) * head_dim)


def one_head(tensor, head, n_heads, head_dim):
    if n_heads == 1:
        return tensor
    return jnp.where(
        head_lanes(tensor.shape[-1], head, head_dim), tensor, jnp.zeros_like(tensor)
    )


def causal(scores, key_start, query_start):
    key_pos = key_start + lax.broadcasted_iota(jnp.int32, scores.shape, 0)
    query_pos = query_start + lax.broadcasted_iota(jnp.int32, scores.shape, 1)
    return jnp.where(key_pos <= query_pos, scores, NEG_LARGE)


def load_pieces(scalars, pieces, whole, sem):
    rows = pieces[0].shape[1]
    copies = []
    for t, piece in enumerate(pieces):
        for u in range(2):
            owner = lax.bitwise_xor(scalars[1], 2 * t + u)
            start = pl.multiple_of(owner * rows, rows)
            copies.append(
                pltpu.make_async_copy(
                    piece.at[u], whole.at[pl.ds(start, rows)], sem.at[2 * t + u]
                )
            )
    for copy in copies:
        copy.start()
    return copies


def store_pieces(scalars, own, other, whole, sem):
    count = own.shape[0]
    rows = whole.shape[0] // (2 * count)
    copies = []
    for t in range(count):
        for u, target in enumerate((own, other)):
            start = pl.multiple_of(lax.bitwise_xor(scalars[1], 2 * t + u) * rows, rows)
            copies.append(
                pltpu.make_async_copy(
                    whole.at[pl.ds(start, rows)], target.at[t, 0:rows], sem.at[2 * t + u]
                )
            )
    for copy in copies:
        copy.start()
    return copies


def load_columns(scalars, pieces, whole, sem, parts):
    if len(pieces[0].shape) == 2:
        copies = [pltpu.make_async_copy(pieces[0], whole, sem.at[0])]
        copies[0].start()
        return copies
    width = pieces[0].shape[2] // parts
    model_width = width * 2 * len(pieces)
    copies = []
    for t, piece in enumerate(pieces):
        for u in range(2):
            owner = lax.bitwise_xor(scalars[1], 2 * t + u)
            for part in range(parts):
                start = pl.multiple_of(part * model_width + owner * width, width)
                copies.append(
                    pltpu.make_async_copy(
                        piece.at[u, 0 : whole.shape[0], part * width : (part + 1) * width],
                        whole.at[:, pl.ds(start, width)],
                        sem.at[(2 * t + u) * parts + part],
                    )
                )
    for copy in copies:
        copy.start()
    return copies


def self_forward_kernel(scalars, *refs, count, n_heads, head_dim, q_block, k_block, stat_block):
    pieces, refs = refs[:count], refs[count:]
    own, other, kept_out, log_sums, whole, values_t, sem = refs
    width = n_heads * head_dim
    index = pl.program_id(0)
    k_blocks = values_t.shape[0]

    @pl.when(index == 0)
    def _():
        for copy in load_pieces(scalars, pieces, whole, sem):
            copy.wait()
        for b in range(k_blocks):
            values_t[b] = whole[b * k_block : (b + 1) * k_block, 2 * width :].T

    start = pl.multiple_of(index * q_block, q_block)
    q_rows = pl.ds(start, q_block)
    live = start < scalars[0]

    @pl.when(jnp.logical_not(live))
    def _():
        kept_out[q_rows, :] = jnp.zeros((q_block, width), HALF)
        log_sums[...] = jnp.zeros_like(log_sums)

    @pl.when(live)
    def _():
        query = whole[q_rows, :width]
        queries = [one_head(query, h, n_heads, head_dim) for h in range(n_heads)]

        def step(key_start, key_count, carry, cols, masked):
            keys = whole[pl.ds(key_start, key_count), width : 2 * width]
            first = key_start // k_block
            out = []
            for h in range(n_heads):
                top, total, acc = carry[h]
                scores = mxu(keys, queries[h][cols], NT)
                if masked:
                    scores = causal(scores, 0, 0)
                new_top = jnp.maximum(top, jnp.max(scores, axis=0, keepdims=True))
                probs = jnp.exp2(scores - new_top)
                scale = jnp.exp2(top - new_top)
                total = total * scale + jnp.sum(probs, axis=0, keepdims=True)
                probs = probs.astype(HALF)
                acc = acc * scale
                for t in range(key_count // k_block):
                    value_t = values_t[first + t][h * head_dim : (h + 1) * head_dim]
                    acc = acc + mxu(value_t, probs[t * k_block : (t + 1) * k_block])
                out.append((new_top, total, acc))
            return tuple(out)

        carry = tuple(
            (
                jnp.full((1, q_block), NEG_LARGE, F32),
                jnp.zeros((1, q_block), F32),
                jnp.zeros((head_dim, q_block), F32),
            )
            for _ in range(n_heads)
        )
        every = slice(0, q_block)
        carry = lax.fori_loop(
            0,
            index,
            lambda kb, c: step(pl.multiple_of(kb * q_block, q_block), q_block, c, every, False),
            carry,
        )
        ratio = q_block // k_block
        parts = []
        for i in range(ratio):
            cols = slice(i * k_block, (i + 1) * k_block)
            part = tuple(tuple(item[:, cols] for item in head) for head in carry)
            for t in range(i + 1):
                key_start = pl.multiple_of(start + t * k_block, k_block)
                part = step(key_start, k_block, part, cols, t == i)
            parts.append(part)
        carry = tuple(
            tuple(
                jnp.concatenate([part[h][item] for part in parts], axis=1) for item in range(3)
            )
            for h in range(n_heads)
        )
        result_t = jnp.concatenate([acc / total for _, total, acc in carry], axis=0)
        kept_out[q_rows, :] = result_t.T.astype(HALF)
        for h, (top, total, _) in enumerate(carry):
            log_sum = top + jnp.log2(total)
            for t in range(q_block // stat_block):
                log_sums[t, h : h + 1, :] = log_sum[:, t * stat_block : (t + 1) * stat_block]

    @pl.when(index == pl.num_programs(0) - 1)
    def _():
        for copy in store_pieces(scalars, own, other, kept_out, sem):
            copy.wait()


def self_forward(scalars, pieces, n_heads, head_dim):
    count, rows = len(pieces), pieces[0].shape[1]
    n = 2 * count
    length, width = n * rows, n_heads * head_dim
    q_block, k_block, stat_block = 1024, 512, 512
    any_spec = pl.BlockSpec(memory_space=pl.ANY)
    return pl.pallas_call(
        partial(
            self_forward_kernel,
            count=count,
            n_heads=n_heads,
            head_dim=head_dim,
            q_block=q_block,
            k_block=k_block,
            stat_block=stat_block,
        ),
        grid_spec=pltpu.PrefetchScalarGridSpec(
            num_scalar_prefetch=1,
            grid=(length // q_block,),
            in_specs=[any_spec] * count,
            out_specs=[any_spec] * 2
            + [
                pl.BlockSpec((length, width), lambda i, s: (0, 0)),
                pl.BlockSpec((q_block // stat_block, n_heads, stat_block), lambda i, s: (i, 0, 0)),
            ],
            scratch_shapes=[
                pltpu.VMEM((length, 3 * width), HALF),
                pltpu.VMEM((length // k_block, width, k_block), HALF),
                pltpu.SemaphoreType.DMA((n,)),
            ],
        ),
        out_shape=[jax.ShapeDtypeStruct((count, rows, width), HALF)] * 2
        + [
            jax.ShapeDtypeStruct((length, width), HALF),
            jax.ShapeDtypeStruct((length // stat_block, n_heads, stat_block), F32),
        ],
        compiler_params=pltpu.CompilerParams(vmem_limit_bytes=VMEM_LIMIT),
        cost_estimate=pl.CostEstimate(
            flops=2 * 2 * length * length * width,
            bytes_accessed=length * width * 10,
            transcendentals=n_heads * length * length // 2,
        ),
        name="self_forward",
    )(scalars, *pieces)


def self_backward_kernel(scalars, *refs, count, n_heads, head_dim, block, last):
    pieces, refs = refs[:count], refs[count:]
    grad_pieces, refs = refs[:count], refs[count:]
    kept_out, log_sums, normed_ref, refs = *refs[:3], refs[3:]
    if last:
        earlier, earlier_sums, refs = refs[0], refs[1], refs[2:]
        own, other, sums, refs = *refs[:3], refs[3:]
        total, columns_own, columns_other, column_sem, refs = *refs[:4], refs[4:]
    else:
        own, other, total, sums, refs = *refs[:4], refs[4:]
    result, whole, grads, query_heads, grad_heads, deltas, query_sums, sem, grad_sem = refs
    width = n_heads * head_dim
    index = pl.program_id(0)
    blocks = query_heads.shape[1]
    model_width = total.shape[1]
    span = scalars[0]

    @pl.when(index == 0)
    def _():
        copies = load_pieces(scalars, pieces, whole, sem)
        copies += load_pieces(scalars, grad_pieces, grads, grad_sem)
        query_sums[...] = jnp.zeros_like(query_sums)
        total[...] = earlier[...] if last else jnp.zeros_like(total)
        sums[...] = earlier_sums[...] if last else jnp.zeros_like(sums)
        for copy in copies:
            copy.wait()

        @pl.loop(0, (span + block - 1) // block)
        def _(b):
            rows = pl.ds(pl.multiple_of(b * block, block), block)
            query, grad = whole[rows, :width], grads[rows, :]
            products = (grad.astype(F32) * kept_out[rows, :].astype(F32)).T
            for h in range(n_heads):
                deltas[b, h : h + 1, :] = jnp.sum(
                    products[h * head_dim : (h + 1) * head_dim], axis=0, keepdims=True
                )
                query_heads[h, b] = one_head(query, h, n_heads, head_dim)
                grad_heads[h, b] = one_head(grad, h, n_heads, head_dim)

    start = pl.multiple_of(index * block, block)
    k_rows = pl.ds(start, block)
    live = start < span

    @pl.when(jnp.logical_not(live))
    def _():
        result[k_rows, :] = jnp.zeros((block, 3 * width), HALF)

    @pl.when(live)
    def _():
        keys = whole[k_rows, width : 2 * width]
        values = whole[k_rows, 2 * width :]
        keys_t = keys.T

        def step(qb, carry, masked):
            grad_keys, grad_values = carry
            for h in range(n_heads):
                query, grad = query_heads[h, qb], grad_heads[h, qb]
                scores = mxu(keys, query, NT)
                if masked:
                    scores = causal(scores, start, qb * block)
                probs = jnp.exp2(scores - log_sums[qb, h : h + 1, :])
                grad_probs = mxu(values, grad, NT)
                grad_scores = (probs * (grad_probs - deltas[qb, h : h + 1, :])).astype(HALF)
                grad_values = grad_values + mxu(probs.astype(HALF), grad)
                grad_keys = grad_keys + mxu(grad_scores, query)
                lanes = slice(h * head_dim, (h + 1) * head_dim)
                query_sums[qb, lanes, :] += mxu(keys_t[lanes], grad_scores)
            return grad_keys, grad_values

        zero = jnp.zeros((block, width), F32)
        carry = step(index, (zero, zero), True)
        live_blocks = (span + block - 1) // block
        grad_keys, grad_values = lax.fori_loop(
            index + 1, live_blocks, lambda qb, c: step(qb, c, False), carry
        )
        query_t = (query_sums[index] * 0.125).astype(HALF)
        grad_queries = query_t.T
        grad_keys = (grad_keys * LN2).astype(HALF)
        grad_values = grad_values.astype(HALF)
        result[k_rows, :width] = grad_queries
        result[k_rows, width : 2 * width] = grad_keys
        result[k_rows, 2 * width :] = grad_values
        sums[0:1] += jnp.sum(grad_queries.astype(F32), axis=0, keepdims=True)
        sums[1:2] += jnp.sum(grad_values.astype(F32), axis=0, keepdims=True)
        normed = normed_ref[...].reshape(block, model_width)
        for part, tensor in enumerate((query_t, grad_keys.T, grad_values.T)):
            total[part * width : (part + 1) * width] += mxu(tensor, normed)

    @pl.when(index == pl.num_programs(0) - 1)
    def _():
        copies = store_pieces(scalars, own, other, result, sem)
        if last:
            shard = columns_own.shape[1]
            chip, core = scalars[1] // 2, lax.bitwise_and(scalars[1], 1)
            for p in range(count):
                tile = total[:, p * 2 * shard : (p + 1) * 2 * shard].T.astype(HALF)
                slot = lax.bitwise_xor(chip, p)
                columns_own[slot], columns_other[slot] = row_split(core, tile, shard)
            rows = own.shape[1] - shard
            for u, (source, target) in enumerate(((columns_own, own), (columns_other, other))):
                copy = pltpu.make_async_copy(
                    source, target.at[:, rows : rows + shard], column_sem.at[u]
                )
                copy.start()
                copies.append(copy)
        for copy in copies:
            copy.wait()


def self_backward(
    scalars, pieces, grad_pieces, kept_out, log_sums, normed, seq, n_heads, head_dim, earlier
):
    count, rows = len(pieces), pieces[0].shape[1]
    n, model_width = 2 * count, normed.shape[3]
    length, width = n * rows, n_heads * head_dim
    block = log_sums.shape[2]
    blocks = length // block
    last = earlier is not None
    any_spec = pl.BlockSpec(memory_space=pl.ANY)
    fixed = lambda shape: pl.BlockSpec(shape, lambda i, s: (0,) * len(shape))
    total, sums = (3 * width, model_width), (8, width)
    packed = (count, model_width // n, 3 * width)
    return pl.pallas_call(
        partial(
            self_backward_kernel,
            count=count,
            n_heads=n_heads,
            head_dim=head_dim,
            block=block,
            last=last,
        ),
        grid_spec=pltpu.PrefetchScalarGridSpec(
            num_scalar_prefetch=1,
            grid=(blocks,),
            in_specs=[any_spec] * (2 * count)
            + [
                fixed((length, width)),
                fixed((blocks, n_heads, block)),
                pl.BlockSpec(
                    (block // rows, 1, rows, model_width), lambda i, s: (i, seq, 0, 0)
                ),
            ]
            + ([fixed(total), fixed(sums)] if last else []),
            out_specs=[any_spec] * 2
            + [fixed(shape) for shape in ((sums,) if last else (total, sums))],
            scratch_shapes=(
                [
                    pltpu.VMEM(total, F32),
                    pltpu.VMEM(packed, HALF),
                    pltpu.VMEM(packed, HALF),
                    pltpu.SemaphoreType.DMA((2,)),
                ]
                if last
                else []
            )
            + [
                pltpu.VMEM((length, 3 * width), HALF),
                pltpu.VMEM((length, 3 * width), HALF),
                pltpu.VMEM((length, width), HALF),
                pltpu.VMEM((n_heads, blocks, block, width), HALF),
                pltpu.VMEM((n_heads, blocks, block, width), HALF),
                pltpu.VMEM((blocks, n_heads, block), F32),
                pltpu.VMEM((blocks, width, block), F32),
                pltpu.SemaphoreType.DMA((n,)),
                pltpu.SemaphoreType.DMA((n,)),
            ],
        ),
        out_shape=[
            jax.ShapeDtypeStruct((count, rows + (packed[1] if last else 0), 3 * width), HALF)
        ]
        * 2
        + ([] if last else [jax.ShapeDtypeStruct(total, F32)])
        + [jax.ShapeDtypeStruct(sums, F32)],
        compiler_params=pltpu.CompilerParams(vmem_limit_bytes=VMEM_LIMIT),
        cost_estimate=pl.CostEstimate(
            flops=5 * 2 * length * length * width // 2,
            bytes_accessed=length * width * 20,
            transcendentals=n_heads * length * length // 2,
        ),
        name="self_backward",
    )(scalars, *pieces, *grad_pieces, kept_out, log_sums, normed, *(earlier or ()))


def cross_scores(keys, query, mem_count):
    scores = mxu(keys, query, NT)
    padded = scores.shape[0]
    if padded == mem_count:
        return scores
    whole = mem_count // 8 * 8
    tail = scores[whole:]
    position = whole + lax.broadcasted_iota(jnp.int32, tail.shape, 0)
    tail = jnp.where(position < mem_count, tail, NEG_LARGE)
    return jnp.concatenate([scores[:whole], tail], axis=0)


def cross_forward_kernel(scalars, query_ref, key_ref, value_ref, out_ref, log_sums, *, mem_count, head_dim):
    rows, width = query_ref.shape
    live = scalars[1] * rows < scalars[0]

    @pl.when(jnp.logical_not(live))
    def _():
        out_ref[...] = jnp.zeros_like(out_ref)
        log_sums[...] = jnp.zeros_like(log_sums)

    @pl.when(live)
    def _():
        n_heads = width // head_dim
        query, keys = query_ref[...], key_ref[...]
        values_t = value_ref[...].T
        results = []
        for h in range(n_heads):
            scores = cross_scores(keys, one_head(query, h, n_heads, head_dim), mem_count)
            top = jnp.max(scores, axis=0, keepdims=True)
            probs = jnp.exp2(scores - top)
            total = jnp.sum(probs, axis=0, keepdims=True)
            lanes = slice(h * head_dim, (h + 1) * head_dim)
            results.append(mxu(values_t[lanes], probs.astype(HALF)) / total)
            log_sums[0, h : h + 1, :] = top + jnp.log2(total)
        out_ref[...] = jnp.concatenate(results, axis=0).T.astype(HALF)


def cross_forward(scalars, query, keys, values, mem_count, head_dim):
    rows, model_width = query.shape
    padded = keys.shape[0]
    width = 128
    groups, n_heads = model_width // width, width // head_dim
    column = lambda count: pl.BlockSpec((count, width), lambda g, s: (0, g))
    return pl.pallas_call(
        partial(cross_forward_kernel, mem_count=mem_count, head_dim=head_dim),
        grid_spec=pltpu.PrefetchScalarGridSpec(
            num_scalar_prefetch=1,
            grid=(groups,),
            in_specs=[column(rows), column(padded), column(padded)],
            out_specs=[column(rows), pl.BlockSpec((1, n_heads, rows), lambda g, s: (g, 0, 0))],
        ),
        out_shape=[
            jax.ShapeDtypeStruct((rows, model_width), HALF),
            jax.ShapeDtypeStruct((groups, n_heads, rows), F32),
        ],
        compiler_params=pltpu.CompilerParams(vmem_limit_bytes=VMEM_LIMIT),
        cost_estimate=pl.CostEstimate(
            flops=4 * 2 * rows * padded * model_width,
            bytes_accessed=(rows + padded) * model_width * 4,
            transcendentals=rows * padded * model_width // head_dim,
        ),
        name="cross_forward",
    )(scalars, query, keys, values)


def cross_backward_kernel(
    scalars,
    query_ref,
    key_ref,
    value_ref,
    grad_ref,
    out_ref,
    log_sums,
    grad_query,
    grad_key,
    grad_value,
    *,
    mem_count,
    head_dim,
):
    rows, width = query_ref.shape
    padded = key_ref.shape[0]
    live = scalars[1] * rows < scalars[0]

    @pl.when(jnp.logical_not(live))
    def _():
        grad_query[...] = jnp.zeros_like(grad_query)
        grad_key[...] = jnp.zeros_like(grad_key)
        grad_value[...] = jnp.zeros_like(grad_value)

    @pl.when(live)
    def _():
        n_heads = width // head_dim
        query_all, keys, values, grad_all = query_ref[...], key_ref[...], value_ref[...], grad_ref[...]
        keys_t = keys.T
        products = (grad_all.astype(F32) * out_ref[...].astype(F32)).T
        query_parts = []
        key_sum = jnp.zeros((padded, width), F32)
        value_sum = jnp.zeros((padded, width), F32)
        for h in range(n_heads):
            lanes = slice(h * head_dim, (h + 1) * head_dim)
            query = one_head(query_all, h, n_heads, head_dim)
            grad = one_head(grad_all, h, n_heads, head_dim)
            delta = jnp.sum(products[lanes], axis=0, keepdims=True)
            scores = cross_scores(keys, query, mem_count)
            probs = jnp.exp2(scores - log_sums[0, h : h + 1, :])
            grad_probs = mxu(values, grad, NT)
            grad_scores = (probs * (grad_probs - delta)).astype(HALF)
            value_sum = value_sum + mxu(probs.astype(HALF), grad)
            key_sum = key_sum + mxu(grad_scores, query)
            query_parts.append(mxu(keys_t[lanes], grad_scores))
        grad_query[...] = (jnp.concatenate(query_parts, axis=0) * 0.125).T.astype(HALF)
        grad_key[...] = (key_sum * LN2).astype(HALF)
        grad_value[...] = value_sum.astype(HALF)


def cross_backward(scalars, query, keys, values, grad, kept_out, log_sums, mem_count, head_dim):
    rows, model_width = query.shape
    padded = keys.shape[0]
    width = 128
    groups, n_heads = model_width // width, width // head_dim
    column = lambda count: pl.BlockSpec((count, width), lambda g, s: (0, g))
    return pl.pallas_call(
        partial(cross_backward_kernel, mem_count=mem_count, head_dim=head_dim),
        grid_spec=pltpu.PrefetchScalarGridSpec(
            num_scalar_prefetch=1,
            grid=(groups,),
            in_specs=[
                column(rows),
                column(padded),
                column(padded),
                column(rows),
                column(rows),
                pl.BlockSpec((1, n_heads, rows), lambda g, s: (g, 0, 0)),
            ],
            out_specs=[column(rows), column(padded), column(padded)],
        ),
        out_shape=[
            jax.ShapeDtypeStruct((rows, model_width), HALF),
            jax.ShapeDtypeStruct((padded, model_width), HALF),
            jax.ShapeDtypeStruct((padded, model_width), HALF),
        ],
        compiler_params=pltpu.CompilerParams(vmem_limit_bytes=VMEM_LIMIT),
        cost_estimate=pl.CostEstimate(
            flops=10 * 2 * rows * padded * model_width,
            bytes_accessed=(rows + padded) * model_width * 10,
            transcendentals=rows * padded * model_width // head_dim,
        ),
        name="cross_backward",
    )(scalars, query, keys, values, grad, kept_out, log_sums)


def exchange(own, other, n):
    return chips(own, cores(other, n), n)


def cores(other, n):
    return lax.ppermute(other, "blk", [(k, k ^ 1) for k in range(n)])


def chips(own, sibling, n):
    received = []
    for t in range(n // 2):
        message = jnp.stack([own[t], sibling[t]])
        if t:
            message = lax.ppermute(message, "blk", [(k, k ^ (2 * t)) for k in range(n)])
        received.append(message)
    return received


def columns_of(pieces, me, parts, rows):
    width = pieces[0].shape[2] // parts
    if width % 128 == 0:
        return pieces
    pieces = [piece[:, :rows] for piece in pieces]
    n = 2 * len(pieces)
    order = lax.bitwise_xor(jnp.arange(n, dtype=jnp.int32), me)
    whole = jnp.concatenate(pieces, axis=0).reshape(n, rows, parts, width)
    whole = jnp.take(whole, order, axis=0)
    return [whole.transpose(1, 2, 0, 3).reshape(rows, parts * n * width)]


class Halve:
    def __init__(self, axis, step, size):
        self.axis, self.step = axis, step
        self.pairs = [(k, k ^ step) for k in range(size)]

    def bit(self):
        return lax.bitwise_and(lax.axis_index(self.axis), self.step) // self.step

    def prepare(self, tensor):
        halves = tensor.reshape((2, -1) + tensor.shape[1:])
        return lax.dynamic_index_in_dim(halves, 1 - self.bit(), 0, keepdims=False), halves

    def complete(self, halves, received):
        own = lax.dynamic_index_in_dim(halves, self.bit(), 0, keepdims=False)
        return (own.astype(F32) + received.astype(F32)).astype(halves.dtype)


class Join(Halve):
    def prepare(self, tensor):
        return tensor, tensor

    def complete(self, tensor, received):
        first = jnp.where(self.bit() == 0, tensor, received)
        second = jnp.where(self.bit() == 0, received, tensor)
        return jnp.concatenate([first, second], axis=0)


class Fold:
    axis = "blk"

    def __init__(self, bit, n, low):
        self.low = low
        self.pairs = [(k, k ^ (2 << bit)) for k in range(n)]

    def part(self, tensors, index):
        half = tensors[0].shape[0] // 2
        shape = ((half, 2) if self.low else (2, half)) + tensors[0].shape[1:]
        found = [
            lax.index_in_dim(item.reshape(shape), index, int(self.low), keepdims=False).astype(F32)
            for item in tensors
        ]
        return sum(found[1:], found[0])

    def prepare(self, tensor):
        tensors = tensor if isinstance(tensor, tuple) else (tensor,)
        return self.part(tensors, 1).astype(HALF), tensors

    def complete(self, tensors, received):
        return (self.part(tensors, 0) + received.astype(F32)).astype(HALF)


def page_steps(pages):
    steps = [1 << b for b in range(pages.bit_length() - 1)]
    return [Halve("page", step, pages) for step in steps] + [
        Join("page", step, pages) for step in reversed(steps)
    ]


class Chain:
    def __init__(self, tensor, steps):
        self.tensor, self.steps = tensor, list(steps)

    def complete(self):
        while self.steps:
            launch([self], ())
        return self.tensor


def launch(chains, value, messages=()):
    chains = [chain for chain in chains if chain.steps]
    steps = [chain.steps.pop(0) for chain in chains]
    ready = [step.prepare(chain.tensor) for step, chain in zip(steps, chains)]
    value, sent, extra = lax.optimization_barrier(
        (value, [send for send, _ in ready], [tensor for tensor, _ in messages])
    )
    for chain, step, send, (_, kept) in zip(chains, steps, sent, ready):
        chain.tensor = step.complete(kept, lax.ppermute(send, step.axis, step.pairs))
    if messages:
        return value, [
            lax.ppermute(tensor, "blk", pairs) if pairs else tensor
            for tensor, (_, pairs) in zip(extra, messages)
        ]
    return value


def after(chains, value):
    value, tensors = lax.optimization_barrier((value, [chain.tensor for chain in chains]))
    for chain, tensor in zip(chains, tensors):
        chain.tensor = tensor
    return value


def chip_messages(own, sibling, n):
    return [
        (jnp.stack([own[t], sibling[t]]), [(k, k ^ (2 * t)) for k in range(n)] if t else None)
        for t in range(n // 2)
    ]


def small_sums(tensor, n, pages):
    me, page = lax.axis_index("blk"), lax.axis_index("page")
    step = n // 2
    while step:
        bit = lax.bitwise_and(me, step) // step
        halves = tensor.reshape((2, -1) + tensor.shape[1:])
        sent = lax.dynamic_index_in_dim(halves, 1 - bit, 0, keepdims=False)
        received = lax.ppermute(sent, "blk", [(k, k ^ step) for k in range(n)])
        tensor = lax.dynamic_index_in_dim(halves, bit, 0, keepdims=False) + received
        step //= 2
    step = 1
    while step < pages:
        tensor = tensor + lax.ppermute(tensor, "page", [(k, k ^ step) for k in range(pages)])
        step *= 2
    return tensor[0]


def normalized(vector):
    centre = vector - jnp.mean(vector, axis=-1, keepdims=True)
    spread = jnp.mean(centre * centre, axis=-1, keepdims=True)
    inverse = lax.rsqrt(spread + EPSILON)
    return centre * inverse, inverse


def norm_backward(unit, inverse, gain, grad):
    scaled = grad * gain
    first = jnp.mean(scaled, axis=-1, keepdims=True)
    second = jnp.mean(scaled * unit, axis=-1, keepdims=True)
    grad_in = inverse * (scaled - first - unit * second)
    return grad_in, jnp.sum(grad * unit, axis=0), jnp.sum(grad, axis=0)


def by_parity(core, tensor, width):
    even, odd = tensor[:, :width], tensor[:, width:]
    return jnp.where(core == 0, even, odd), jnp.where(core == 0, odd, even)


def row_split(core, tensor, width):
    even, odd = tensor[:width], tensor[width:]
    return jnp.where(core == 0, even, odd), jnp.where(core == 0, odd, even)


GROUP_TILE = 512


def placed(parts):
    found, row = [], 0
    for part in parts:
        column = 0
        for array in part if isinstance(part, tuple) else (part,):
            found.append((array, row, column))
            column += array.shape[1]
        row += array.shape[0]
    return found, row, column


def weights_kernel(scalars, *refs, phases, places):
    hbm = []
    for spots in places:
        hbm.append(refs[: len(spots)])
        refs = refs[len(spots) :]
    own, other, refs = refs[0], refs[1], refs[2:]
    held, turned, sems = refs[: len(places)], refs[len(places)], refs[len(places) + 1 :]
    step = pl.program_id(0)
    count, width, _ = own.shape
    chip, core = scalars[1] // 2, lax.bitwise_and(scalars[1], 1)

    def copies(k):
        found = []
        for i, (row, column) in enumerate(places[k]):
            source = hbm[k][i]
            rows, columns = source.shape
            target = held[k].at[row : row + rows, column : column + columns]
            found.append(pltpu.make_async_copy(source, target, sems[k].at[i]))
        return found

    @pl.when(step == 0)
    def _():
        for k in range(len(places)):
            for copy in copies(k):
                copy.start()
        for k, spots in enumerate(places):
            filled = max(row + source.shape[0] for (row, _), source in zip(spots, hbm[k]))
            if filled < held[k].shape[0]:
                held[k][filled:, :] = jnp.zeros((held[k].shape[0] - filled, held[k].shape[1]), HALF)

    for k, (depth, first, tiles) in enumerate(phases):
        left, right = held[2 * k], held[2 * k + 1 if depth else 2 * k - 1]

        @pl.when(step == first)
        def _(k=k, depth=depth, left=left):
            for copy in copies(2 * k) + (copies(2 * k + 1) if depth else []):
                copy.wait()
            if depth:
                turned[:, :depth] = left[...].T

        @pl.when((step >= first) & (step < first + tiles))
        def _(depth=depth, first=first, left=left, right=right):
            at = pl.multiple_of((step - first) * GROUP_TILE, GROUP_TILE)
            for p in range(count):
                rows = slice(p * 2 * width, (p + 1) * 2 * width)
                if depth:
                    tile = mxu(turned[rows, :depth], right[:depth, pl.ds(at, GROUP_TILE)])
                else:
                    tile = mxu(left[rows, :], right[pl.ds(at, GROUP_TILE), :], NT)
                slot = lax.bitwise_xor(chip, p)
                own[slot], other[slot] = row_split(core, tile.astype(HALF), width)


def weight_grads(scalars, pairs, memory_weights, n):
    operands, places, buffers, phases = [], [], [], []

    def hold(parts, multiple):
        spots, rows, columns = placed(parts)
        operands.extend(array for array, _, _ in spots)
        places.append([(row, column) for _, row, column in spots])
        rows = -(-rows // multiple) * multiple
        buffers.append(pltpu.VMEM((rows, columns), HALF))
        return rows, columns

    first = 0
    for left, right in pairs:
        depth, model_width = hold(left, 128)
        rows, columns = hold(right, GROUP_TILE)
        phases.append((depth, first, columns // GROUP_TILE))
        first += phases[-1][2]
    if memory_weights is not None:
        hold([memory_weights], 128)
        phases.append((0, first, rows // GROUP_TILE))
        first += phases[-1][2]
    depth = max(phase[0] for phase in phases)
    count, width = n // 2, model_width // n
    block = pl.BlockSpec((count, width, GROUP_TILE), lambda j, s: (0, 0, j))
    shape = jax.ShapeDtypeStruct((count, width, first * GROUP_TILE), HALF)
    return pl.pallas_call(
        partial(weights_kernel, phases=phases, places=places),
        grid_spec=pltpu.PrefetchScalarGridSpec(
            num_scalar_prefetch=1,
            grid=(first,),
            in_specs=[pl.BlockSpec(memory_space=pl.ANY)] * len(operands),
            out_specs=[block, block],
            scratch_shapes=buffers
            + [pltpu.VMEM((model_width, depth), HALF)]
            + [pltpu.SemaphoreType.DMA((len(spots),)) for spots in places],
        ),
        out_shape=[shape, shape],
        compiler_params=pltpu.CompilerParams(vmem_limit_bytes=VMEM_LIMIT),
        cost_estimate=pl.CostEstimate(
            flops=2 * model_width * depth * first * GROUP_TILE,
            bytes_accessed=2 * model_width * (2 * depth + first * GROUP_TILE),
            transcendentals=0,
        ),
        name="weight_grads",
    )(scalars, *operands)


def rows_kernel(scalars, left_ref, right_ref, own, other, turned):
    @pl.when(pl.program_id(0) == 0)
    def _():
        turned[...] = left_ref[...].T

    core = lax.bitwise_and(scalars[1], 1)
    width, shard = right_ref.shape[1] // 2, own.shape[1]
    left = turned[...]
    even = mxu(left, right_ref[:, :width]).astype(HALF)
    odd = mxu(left, right_ref[:, width:]).astype(HALF)
    mine, theirs = jnp.where(core == 0, even, odd), jnp.where(core == 0, odd, even)
    for q in range(left.shape[0] // shard):
        rows, cols = slice(q * shard, (q + 1) * shard), slice(q * width, (q + 1) * width)
        own[0, :, cols], other[0, :, cols] = mine[rows], theirs[rows]


def row_grads(scalars, left, right, n):
    rows, model_width = left.shape
    count, width = n // 2, right.shape[1] // n
    block = pl.BlockSpec(
        (1, model_width // n, n * width), lambda p, s: (lax.bitwise_xor(p, s[1] // 2), 0, 0)
    )
    shape = jax.ShapeDtypeStruct((count, model_width // n, n * width), HALF)
    return pl.pallas_call(
        rows_kernel,
        grid_spec=pltpu.PrefetchScalarGridSpec(
            num_scalar_prefetch=1,
            grid=(count,),
            in_specs=[
                pl.BlockSpec((rows, model_width), lambda p, s: (0, 0)),
                pl.BlockSpec((rows, 2 * width), lambda p, s: (0, p)),
            ],
            out_specs=[block, block],
            scratch_shapes=[pltpu.VMEM((model_width, rows), HALF)],
        ),
        out_shape=[shape, shape],
        compiler_params=pltpu.CompilerParams(vmem_limit_bytes=VMEM_LIMIT),
        cost_estimate=pl.CostEstimate(
            flops=2 * rows * model_width * right.shape[1],
            bytes_accessed=2 * (rows + model_width) * right.shape[1],
            transcendentals=0,
        ),
        name="row_grads",
    )(scalars, left, right)


def project_kernel(scalars, x_ref, norm_ref, bias_ref, q_ref, k_ref, v_ref, normed_ref, own, other, *, q_scale):
    width = own.shape[2] // 3
    core = lax.bitwise_and(scalars[1], 1)

    @pl.when(pl.program_id(0) == 0)
    def _():
        unit, _ = normalized(x_ref[0].astype(F32))
        normed_ref[...] = (unit * norm_ref[0:1] + norm_ref[1:2]).astype(HALF)

    normed = normed_ref[...]
    query = ((mxu(normed, q_ref[...]) + bias_ref[0:1]) * q_scale).astype(HALF)
    keys = mxu(normed, k_ref[...]).astype(HALF)
    values = (mxu(normed, v_ref[...]) + bias_ref[1:2]).astype(HALF)
    for part, tensor in enumerate((query, keys, values)):
        lanes = slice(part * width, (part + 1) * width)
        own[0, :, lanes], other[0, :, lanes] = by_parity(core, tensor, width)


def project(scalars, x, norm, bias, weights, n, q_scale):
    rows, model_width = x.shape[1:]
    count, width = n // 2, model_width // n
    fixed = lambda shape: pl.BlockSpec(shape, lambda p, s: (0, 0))
    column = lambda part: pl.BlockSpec(
        (model_width, 2 * width), lambda p, s, part=part: (0, part * count + p)
    )
    packed = pl.BlockSpec(
        (1, rows, 3 * width), lambda p, s: (lax.bitwise_xor(p, s[1] // 2), 0, 0)
    )
    return pl.pallas_call(
        partial(project_kernel, q_scale=q_scale),
        grid_spec=pltpu.PrefetchScalarGridSpec(
            num_scalar_prefetch=1,
            grid=(count,),
            in_specs=[
                pl.BlockSpec((1, rows, model_width), lambda p, s: (s[2], 0, 0)),
                fixed((2, model_width)),
                pl.BlockSpec((2, 2 * width), lambda p, s: (0, p)),
                column(0),
                column(1),
                column(2),
            ],
            out_specs=[fixed((rows, model_width)), packed, packed],
        ),
        out_shape=[jax.ShapeDtypeStruct((rows, model_width), HALF)]
        + [jax.ShapeDtypeStruct((count, rows, 3 * width), HALF)] * 2,
        compiler_params=pltpu.CompilerParams(vmem_limit_bytes=VMEM_LIMIT),
        cost_estimate=pl.CostEstimate(
            flops=2 * rows * model_width * 3 * model_width,
            bytes_accessed=model_width * (6 * model_width + 8 * rows),
            transcendentals=0,
        ),
        name="project",
    )(scalars, x, norm, bias, weights, weights, weights)


TILE = 256


def middle_kernel(scalars, *refs, count, q_scale):
    pieces, refs = refs[:count], refs[count:]
    x_ref, params, out_hbm, query_hbm, attended, mid_ref, normed_ref, query_ref = refs[:8]
    out_weights, query_weights, sem, weight_sem = refs[8:]
    copies = load_columns(scalars, pieces, attended, sem, 1)
    first = pltpu.make_async_copy(out_hbm, out_weights, weight_sem.at[0])
    second = pltpu.make_async_copy(query_hbm, query_weights, weight_sem.at[1])
    first.start()
    second.start()
    for copy in copies:
        copy.wait()
    first.wait()
    left = attended[...]
    model_width = left.shape[1]
    for j in range(model_width // TILE):
        cols = slice(j * TILE, (j + 1) * TILE)
        mid_ref[:, cols] = (
            x_ref[:, cols].astype(F32) + mxu(left, out_weights[:, cols]) + params[2:3, cols]
        )
    unit, _ = normalized(mid_ref[...])
    normed_ref[...] = (unit * params[0:1] + params[1:2]).astype(HALF)
    second.wait()
    left = normed_ref[...]
    for j in range(model_width // TILE):
        cols = slice(j * TILE, (j + 1) * TILE)
        query_ref[:, cols] = (
            (mxu(left, query_weights[:, cols]) + params[3:4, cols]) * q_scale
        ).astype(HALF)


def middle(scalars, pieces, x, params, out_weights, query_weights, q_scale):
    rows, model_width = x.shape
    count = len(pieces)
    any_spec = pl.BlockSpec(memory_space=pl.ANY)
    vmem = pl.BlockSpec(memory_space=pltpu.VMEM)
    return pl.pallas_call(
        partial(middle_kernel, count=count, q_scale=q_scale),
        in_specs=[pl.BlockSpec(memory_space=pltpu.SMEM)] + [any_spec] * count + [vmem, vmem, any_spec, any_spec],
        out_specs=[vmem] * 4,
        out_shape=[
            jax.ShapeDtypeStruct((rows, model_width), HALF),
            jax.ShapeDtypeStruct((rows, model_width), F32),
            jax.ShapeDtypeStruct((rows, model_width), HALF),
            jax.ShapeDtypeStruct((rows, model_width), HALF),
        ],
        scratch_shapes=[
            pltpu.VMEM((model_width, model_width), HALF),
            pltpu.VMEM((model_width, model_width), HALF),
            pltpu.SemaphoreType.DMA((2 * count,)),
            pltpu.SemaphoreType.DMA((2,)),
        ],
        compiler_params=pltpu.CompilerParams(vmem_limit_bytes=VMEM_LIMIT),
        cost_estimate=pl.CostEstimate(
            flops=4 * rows * model_width * model_width,
            bytes_accessed=model_width * (4 * model_width + 12 * rows),
            transcendentals=0,
        ),
        name="middle",
    )(scalars, *pieces, x, params, out_weights, query_weights)


def turn_kernel(
    scalars, grad_query, mid_ref, grad_ref, params, query_hbm, out_hbm,
    grad_mid, half_ref, own, other, sums,
    query_weights, out_weights, back, weight_sem,
):
    first = pltpu.make_async_copy(query_hbm, query_weights, weight_sem.at[0])
    second = pltpu.make_async_copy(out_hbm, out_weights, weight_sem.at[1])
    first.start()
    second.start()
    count, _, width = own.shape
    chip, core = scalars[1] // 2, lax.bitwise_and(scalars[1], 1)
    unit, inverse = normalized(mid_ref[...])
    first.wait()
    left = grad_query[...]
    model_width = left.shape[1]
    for j in range(model_width // TILE):
        cols = slice(j * TILE, (j + 1) * TILE)
        back[:, cols] = mxu(left, query_weights[cols, :], NT)
    grad_in, gain, shift = norm_backward(unit, inverse, params[0:1], back[...])
    total = grad_ref[...] + grad_in
    grad_mid[...] = total
    half = total.astype(HALF)
    half_ref[...] = half
    sums[0:1] = gain[None]
    sums[1:2] = shift[None]
    sums[2:3] = jnp.sum(half.astype(F32), axis=0, keepdims=True)
    sums[3:4] = jnp.sum(left.astype(F32), axis=0, keepdims=True)
    sums[4:8] = jnp.zeros((4, model_width), F32)
    second.wait()
    for p in range(count):
        tile = mxu(half, out_weights[p * 2 * width : (p + 1) * 2 * width, :], NT).astype(HALF)
        slot = lax.bitwise_xor(chip, p)
        own[slot], other[slot] = by_parity(core, tile, width)


def turn(scalars, grad_query, mid, grad, params, query_weights, out_weights, n):
    rows, model_width = mid.shape
    count, width = n // 2, model_width // n
    any_spec = pl.BlockSpec(memory_space=pl.ANY)
    vmem = pl.BlockSpec(memory_space=pltpu.VMEM)
    return pl.pallas_call(
        turn_kernel,
        in_specs=[pl.BlockSpec(memory_space=pltpu.SMEM)] + [vmem] * 4 + [any_spec] * 2,
        out_specs=[vmem] * 5,
        out_shape=[
            jax.ShapeDtypeStruct((rows, model_width), F32),
            jax.ShapeDtypeStruct((rows, model_width), HALF),
            jax.ShapeDtypeStruct((count, rows, width), HALF),
            jax.ShapeDtypeStruct((count, rows, width), HALF),
            jax.ShapeDtypeStruct((8, model_width), F32),
        ],
        scratch_shapes=[
            pltpu.VMEM((model_width, model_width), HALF),
            pltpu.VMEM((model_width, model_width), HALF),
            pltpu.VMEM((rows, model_width), F32),
            pltpu.SemaphoreType.DMA((2,)),
        ],
        compiler_params=pltpu.CompilerParams(vmem_limit_bytes=VMEM_LIMIT),
        cost_estimate=pl.CostEstimate(
            flops=4 * rows * model_width * model_width,
            bytes_accessed=model_width * (4 * model_width + 20 * rows),
            transcendentals=0,
        ),
        name="turn",
    )(scalars, grad_query, mid, grad, params, query_weights, out_weights)


def finish_kernel(scalars, *refs, count):
    pieces, refs = refs[:count], refs[count:]
    x_ref, grad_ref, params, weights_hbm, grad_x, sums = refs[:6]
    grads, weights, back, sem, weight_sem = refs[6:]
    copies = load_columns(scalars, pieces, grads, sem, 3)
    fetch = pltpu.make_async_copy(weights_hbm, weights, weight_sem.at[0])
    fetch.start()
    unit, inverse = normalized(x_ref[...].astype(F32))
    for copy in copies:
        copy.wait()
    fetch.wait()
    left = grads[...]
    model_width = back.shape[1]
    for j in range(model_width // TILE):
        cols = slice(j * TILE, (j + 1) * TILE)
        back[:, cols] = mxu(left, weights[cols, :], NT)
    grad_in, gain, shift = norm_backward(unit, inverse, params[0:1], back[...])
    grad_x[...] = grad_ref[...] + grad_in
    sums[0:1] = gain[None]
    sums[1:2] = shift[None]
    sums[2:8] = jnp.zeros((6, model_width), F32)


def finish(scalars, pieces, x, grad, params, weights):
    rows, model_width = x.shape
    count = len(pieces)
    any_spec = pl.BlockSpec(memory_space=pl.ANY)
    vmem = pl.BlockSpec(memory_space=pltpu.VMEM)
    return pl.pallas_call(
        partial(finish_kernel, count=count),
        in_specs=[pl.BlockSpec(memory_space=pltpu.SMEM)] + [any_spec] * count + [vmem] * 3 + [any_spec],
        out_specs=[vmem] * 2,
        out_shape=[
            jax.ShapeDtypeStruct((rows, model_width), F32),
            jax.ShapeDtypeStruct((8, model_width), F32),
        ],
        scratch_shapes=[
            pltpu.VMEM((rows, 3 * model_width), HALF),
            pltpu.VMEM((model_width, 3 * model_width), HALF),
            pltpu.VMEM((rows, model_width), F32),
            pltpu.SemaphoreType.DMA((6 * count,)),
            pltpu.SemaphoreType.DMA((1,)),
        ],
        compiler_params=pltpu.CompilerParams(vmem_limit_bytes=VMEM_LIMIT),
        cost_estimate=pl.CostEstimate(
            flops=6 * rows * model_width * model_width,
            bytes_accessed=model_width * (6 * model_width + 16 * rows),
            transcendentals=0,
        ),
        name="finish",
    )(scalars, *pieces, x, grad, params, weights)


def col_sums(tensor):
    return jnp.sum(tensor.astype(F32), axis=0)


def shards(
    tokens,
    memory,
    end_only,
    lengths,
    norm_gain,
    norm_bias,
    self_qkv,
    self_out,
    cross_q,
    cross_kv,
    cross_out,
    fc_in,
    fc_out,
    fc_in_bias,
    proj_bias,
    cotangent,
    *,
    n,
    pages,
):
    seqs, rows, model_width = tokens.shape
    mem_count, shard_width = memory.shape[1], memory.shape[2]
    head_dim = model_width // HEADS
    n_heads = HEADS // n
    width = n_heads * head_dim
    flat = seqs * rows
    me = lax.axis_index("blk")
    offset = me * rows
    span = jnp.where(end_only == 1, 1, lengths)
    order = jnp.argsort(-span, stable=True).astype(jnp.int32)
    place = jnp.argsort(order).astype(jnp.int32)
    span = jnp.take(span, order)
    scalars = [jnp.stack([span[s], me, order[s]]).astype(jnp.int32) for s in range(seqs)]
    positions = offset + jnp.arange(rows, dtype=jnp.int32)

    def arranged(tensors, index):
        found = []
        for s in range(seqs):
            item = tensors[0]
            for t in range(1, seqs):
                item = jnp.where(index[s] == t, tensors[t], item)
            found.append(item)
        return found

    row_mask = (positions[None, :] < span[:, None]).astype(F32).reshape(flat, 1)
    q_scale = 0.125 * LOG2E

    ordered = lax.optimization_barrier
    x = arranged(tokens, order)

    padded = -(-mem_count // 16) * 16
    own_memory = jnp.stack(arranged(memory, order))
    own_memory = jnp.pad(own_memory, ((0, 0), (0, padded - mem_count), (0, 0)))
    whole_memory = lax.all_gather(own_memory, "blk", axis=2, tiled=True)
    self_norm = jnp.stack([norm_gain[0], norm_bias[0]])
    normed_self, kept = [], []
    for s in range(seqs):
        normed, own, other = project(scalars[s], tokens, self_norm, proj_bias[:2], self_qkv, n, q_scale)
        normed_self.append(normed)
        kept.append(exchange(own, other, n))
    normed_self = jnp.stack(normed_self).reshape(flat, model_width)

    whole_memory = whole_memory.reshape(seqs * padded, model_width)
    mem_proj = mxu(whole_memory, cross_kv)
    cross_keys = mem_proj[:, :model_width].astype(HALF).reshape(seqs, padded, model_width)
    cross_values = (mem_proj[:, model_width:] + proj_bias[4]).astype(HALF)
    cross_values = cross_values.reshape(seqs, padded, model_width)

    kept[0], normed_self, cross_keys, cross_values = ordered(
        (kept[0], normed_self, cross_keys, cross_values)
    )
    normed_whole = lax.all_gather(normed_self, "blk", axis=0, tiled=True)
    self_saved, attended = [], []
    for s in range(seqs):
        own, other, kept_out, log_sums = self_forward(scalars[s], kept[s], n_heads, head_dim)
        sibling = cores(other, n)
        if s + 1 < seqs:
            kept[s + 1], log_sums, sibling = ordered((kept[s + 1], log_sums, sibling))
        self_saved.append((kept_out, log_sums))
        attended.append(chips(own, sibling, n))

    mids, crosses, cross_saved, normed_cross = [], [], [], []
    middle_params = jnp.stack([norm_gain[1], norm_bias[1], proj_bias[2], proj_bias[3]])
    for s in range(seqs):
        attended[s], mid, normed, query = middle(
            scalars[s], columns_of(attended[s], me, 1, rows), x[s], middle_params, self_out, cross_q, q_scale
        )
        crossed, log_sums = cross_forward(
            scalars[s], query, cross_keys[s], cross_values[s], mem_count, head_dim
        )
        mids.append(mid)
        normed_cross.append(normed)
        crosses.append(crossed)
        cross_saved.append((query, log_sums))
    crossed = jnp.concatenate(crosses, axis=0)
    stream_mid = jnp.concatenate(mids, axis=0)
    stream_mid, normed_whole = ordered((stream_mid, normed_whole))

    stream_late = stream_mid + mxu(crossed, cross_out) + proj_bias[5]
    unit_mlp, inverse_mlp = normalized(stream_late)
    normed_mlp = (unit_mlp * norm_gain[2] + norm_bias[2]).astype(HALF)
    hidden_pre = mxu(normed_mlp, fc_in) + fc_in_bias
    gate = 0.5 * (1.0 + lax.erf(hidden_pre * (0.5**0.5)))
    hidden_act = (hidden_pre * gate).astype(HALF)
    slope = (gate + hidden_pre * (jnp.exp(-0.5 * hidden_pre * hidden_pre) * 0.3989422804014327)).astype(HALF)
    grad_late = jnp.concatenate(arranged(cotangent, order), axis=0).astype(F32) * row_mask
    grad_mlp = grad_late.astype(HALF)
    out_own, out_other = row_grads(scalars[0], grad_mlp, hidden_act, n)
    grad_pre = (slope.astype(F32) * mxu(grad_mlp, fc_out, NT)).astype(HALF)
    grad_fc_bias = col_sums(grad_pre)
    grad_x2, gain_two, shift_two = norm_backward(
        unit_mlp, inverse_mlp, norm_gain[2], mxu(grad_pre, fc_in, NT)
    )
    grad_two = grad_late + grad_x2
    grad_cross = grad_two.astype(HALF)
    in_own, in_other = weight_grads(
        scalars[0], [([normed_mlp], [grad_pre]), (crosses, [grad_cross])], None, n
    )
    bits = n.bit_length() - 2
    fold_steps = [Fold(b, n, False) for b in reversed(range(bits))]
    other_steps = [Fold(b, n, True) for b in range(bits)]
    out_other, in_other = cores(out_other, n), cores(in_other, n)
    grad_crossed = mxu(grad_cross, cross_out, NT).astype(HALF)
    grad_crossed, out_other, in_other = ordered((grad_crossed, out_other, in_other))
    fc_row = Chain((out_own, out_other), fold_steps)
    fc_col = Chain((in_own, in_other), other_steps)
    fc = [fc_row, fc_col]
    grad_crossed = launch(fc, grad_crossed)

    cq_grads, ckv_parts, ones, selfs, self_grads = [], [], [], [], []
    turn_sums = 0.0
    for s in range(seqs):
        part = slice(s * rows, (s + 1) * rows)
        query, log_sums = cross_saved[s]
        grad_cq, grad_ck, grad_cv = cross_backward(
            scalars[s],
            query,
            cross_keys[s],
            cross_values[s],
            grad_crossed[part],
            crosses[s],
            log_sums,
            mem_count,
            head_dim,
        )
        cq_grads.append(grad_cq)
        ckv_parts.append((grad_ck, grad_cv))
        grad_one, half, own, other, sums = turn(
            scalars[s], grad_cq, mids[s], grad_two[part], norm_gain[1:2], cross_q, self_out, n
        )
        if s == 1:
            half = after(fc, half)
            grad_cross = launch(fc, grad_cross)
        ones.append(grad_one)
        selfs.append(half)
        turn_sums = turn_sums + sums
        self_grads.append(exchange(own, other, n))

    bias_cross_v = sum(col_sums(grad_cv) for _, grad_cv in ckv_parts)
    own, other = weight_grads(
        scalars[0],
        [
            (normed_cross, cq_grads),
            (attended, selfs),
            ([whole_memory], ckv_parts),
        ],
        cross_kv,
        n,
    )
    own = after(fc, own)
    row_sum, col_sum = fc_row.complete()[0], fc_col.complete()[0]
    fc = Chain(jnp.concatenate([row_sum, col_sum], axis=1), page_steps(pages))
    hidden_act, own, other = ordered((hidden_act, own, other))
    hidden_act = launch([fc], hidden_act)
    sibling = cores(other, n)
    stream_out = mxu(hidden_act, fc_out)
    stream_out, sibling = after([fc], (stream_out, sibling))
    self_grads[0], stream_out = ordered((self_grads[0], stream_out))
    group = Chain((own, sibling), fold_steps)
    self_grads[0] = launch([fc, group], self_grads[0])

    normed_whole = normed_whole.reshape(n, seqs, rows, model_width)
    earlier, received = None, []
    for s in range(seqs):
        kept_out, log_sums = self_saved[s]
        own, other, *columns = self_backward(
            scalars[s],
            kept[s],
            self_grads[s],
            kept_out,
            log_sums,
            normed_whole,
            s,
            n_heads,
            head_dim,
            earlier,
        )
        earlier, qkv_sums = columns, columns[-1]
        own, other = after([fc, group], (own, other))
        if s + 1 == seqs:
            folded = group.complete()[0]
            memory_columns = folded[:, 4 * model_width : 4 * model_width + seqs * padded]
            group = Chain(folded[:, : 4 * model_width], page_steps(pages))
            other = launch([fc, group], other)
            sibling = cores(other, n)
            received[0], sibling = after([group], (received[0], sibling))
            messages = chip_messages(own, sibling, n)
            received[0], pieces = launch([group], received[0], messages)
        else:
            messages = chip_messages(own, cores(other, n), n)
            self_grads[s + 1], pieces = launch([fc, group], self_grads[s + 1], messages)
        received.append(pieces)

    outs, finish_sums = [], 0.0
    for s in range(seqs):
        grad_x, sums = finish(
            scalars[s], columns_of(received[s], me, 3, rows), x[s], ones[s], norm_gain[0:1], self_qkv
        )
        if s + 2 == seqs:
            grad_x = after([group], grad_x)
            grad_x = launch([group], grad_x)
            grad_x, received[s + 1] = after([group], (grad_x, received[s + 1]))
            qkv = [piece[u, rows:] for piece in received[s + 1] for u in range(2)]
            qkv = Chain(jnp.concatenate(qkv, axis=1), page_steps(pages))
            ones[s + 1] = launch([qkv, group], ones[s + 1])
        outs.append(grad_x)
        finish_sums = finish_sums + sums
    stream_out = stream_out + stream_late + proj_bias[6]
    result = (stream_out * row_mask).reshape(seqs, rows, model_width).astype(HALF)
    result = jnp.stack(arranged(result, place))
    grad_tokens = jnp.stack(arranged(outs, place))

    def own_columns(vector):
        return lax.dynamic_update_slice(jnp.zeros((model_width,), F32), vector, (me * width,))

    small = jnp.concatenate(
        [
            jnp.stack(
                [
                    finish_sums[0],
                    turn_sums[0],
                    gain_two,
                    finish_sums[1],
                    turn_sums[1],
                    shift_two,
                    own_columns(qkv_sums[0]),
                    own_columns(qkv_sums[1]),
                    turn_sums[2],
                    turn_sums[3],
                    bias_cross_v,
                    col_sums(grad_cross),
                    col_sums(grad_mlp),
                ]
            ),
            grad_fc_bias.reshape(n, 4, -1).transpose(1, 0, 2).reshape(4, -1),
        ],
        axis=0,
    )
    small = jnp.pad(small, ((0, -small.shape[0] % 8), (0, 0)))
    small = small_sums(small.reshape(-1, n, shard_width).transpose(1, 0, 2), n, pages)

    total_qkv = qkv.complete()
    owners = lax.bitwise_xor(jnp.arange(n, dtype=jnp.int32), me)
    total_qkv = jnp.take(total_qkv.reshape(shard_width, n, 3, width), owners, axis=1)
    total_qkv = total_qkv.transpose(0, 2, 1, 3).reshape(shard_width, 3 * model_width)
    total_fc = fc.complete().astype(F32)
    total_out = total_fc[:, : fc_out.shape[0]].reshape(shard_width, n, -1).transpose(2, 1, 0)
    total_out = total_out.reshape(-1, model_width)
    total_in = total_fc[:, fc_out.shape[0] : 2 * fc_out.shape[0]]
    wide = model_width
    group = group.complete().astype(F32)
    grad_memory = memory_columns.astype(F32).T
    grad_memory = grad_memory.reshape(seqs, padded, shard_width)[:, :mem_count]
    grad_memory = jnp.stack(arranged(grad_memory, place))
    return (
        result,
        grad_tokens,
        grad_memory,
        small[0:3],
        small[3:6],
        total_qkv.astype(F32),
        group[:, wide : 2 * wide],
        group[:, :wide],
        group[:, 2 * wide :],
        total_fc[:, 2 * fc_out.shape[0] :],
        total_in,
        total_out,
        small[13:17].reshape(-1),
        small[6:13],
    )


def solution(mesh):
    rows_spec = P("page", "blk", None)
    return jax.shard_map(
        partial(shards, n=mesh.shape["blk"], pages=mesh.shape["page"]),
        mesh=mesh,
        in_specs=(rows_spec, P("page", None, "blk"), P("page"), P("page"))
        + (P(),) * 11
        + (rows_spec,),
        out_specs=(
            rows_spec,
            rows_spec,
            P("page", None, "blk"),
            P(None, "blk"),
            P(None, "blk"),
            P("blk", None),
            P("blk", None),
            P("blk", None),
            P("blk", None),
            P("blk", None),
            P("blk", None),
            P("blk", None),
            P("blk"),
            P(None, "blk"),
        ),
        check_vma=False,
    )
```
